32 devices in a mesh: dp: 16 (over z, x, core), map: 2 (over y).
Axes of the slice: x: 2, y: 2, z: 4, core: 2. Of those that a mesh axis runs over, the one named last changes fastest.
Arguments:
- patches: bfloat16 [32, 576, 1024], P(('dp', 'map')), may hold values from -6 to 6
- keep_mask: int32 [32, 576], P(('dp', 'map')), may hold values from 0 to 1, as said below
- block_cotangent: bfloat16 [32, 576, 1024], P(('dp', 'map')), may hold values from -6 to 6
- token_cotangent: bfloat16 [32, 8, 1024], P('dp', 'map'), may hold values from -6 to 6
- first_gain: float32 [1024], P(('dp', 'map')), may hold values from 0.1 to 1.9
- first_shift: float32 [1024], P(('dp', 'map')), may hold values from -3 to 3
- qkv_weight: float32 [1024, 3072], P(('dp', 'map')), may hold values from -0.1875 to 0.1875
- query_bias: float32 [1024], P(('dp', 'map')), may hold values from -3 to 3
- value_bias: float32 [1024], P(('dp', 'map')), may hold values from -3 to 3
- out_weight: float32 [1024, 1024], P(('dp', 'map')), may hold values from -1.5 to 1.5
- out_bias: float32 [1024], P(('dp', 'map')), may hold values from -3 to 3
- second_gain: float32 [1024], P(('dp', 'map')), may hold values from 0.1 to 1.9
- second_shift: float32 [1024], P(('dp', 'map')), may hold values from -3 to 3
- up_weight: float32 [1024, 4096], P(('dp', 'map')), may hold values from -0.1875 to 0.1875
- up_bias: float32 [4096], P(('dp', 'map')), may hold values from -3 to 3
- down_weight: float32 [4096, 1024], P(('dp', 'map')), may hold values from -0.09375 to 0.09375
- down_bias: float32 [1024], P(('dp', 'map')), may hold values from -3 to 3
- learn_gain: float32 [1024], P(('dp', 'map')), may hold values from 0.1 to 1.9
- learn_shift: float32 [1024], P(('dp', 'map')), may hold values from -3 to 3
- map_weight: float32 [1024, 8], P(('dp', 'map')), may hold values from -0.1875 to 0.1875
Outputs:
- block_out: bfloat16 [32, 576, 1024], P(('dp', 'map'))
- tokens: bfloat16 [32, 8, 1024], P('dp', 'map')
- grad_patches: bfloat16 [32, 576, 1024], P(('dp', 'map'))
- grad_first_gain: float32 [1024], P(('dp', 'map'))
- grad_first_shift: float32 [1024], P(('dp', 'map'))
- grad_qkv_weight: float32 [1024, 3072], P(('dp', 'map'))
- grad_query_bias: float32 [1024], P(('dp', 'map'))
- grad_value_bias: float32 [1024], P(('dp', 'map'))
- grad_out_weight: float32 [1024, 1024], P(('dp', 'map'))
- grad_out_bias: float32 [1024], P(('dp', 'map'))
- grad_second_gain: float32 [1024], P(('dp', 'map'))
- grad_second_shift: float32 [1024], P(('dp', 'map'))
- grad_up_weight: float32 [1024, 4096], P(('dp', 'map'))
- grad_up_bias: float32 [4096], P(('dp', 'map'))
- grad_down_weight: float32 [4096, 1024], P(('dp', 'map'))
- grad_down_bias: float32 [1024], P(('dp', 'map'))
- grad_learn_gain: float32 [1024], P(('dp', 'map'))
- grad_learn_shift: float32 [1024], P(('dp', 'map'))
- grad_map_weight: float32 [1024, 8], P(('dp', 'map'))
The draws below stay inside these ranges and needn't reach their ends.
Inputs may be any that keep to these rules, and one draw needn't show every extreme that they name: `keep_mask`: each image keeps exactly 512 of its 576 patches.
All inputs are finite; a program needn't handle non-finite values.
Results may differ from the reference program's by a relative error of at most 0.012.
The reference program's roundings to bfloat16 on the way count: a program that leaves them out, or rounds other values in their place, can miss the bound.
Values may be sent and summed in bfloat16 or wider, within the bound.
No kernel may reach another device: no remote copies, remote signals or barrier semaphores. Data moves between devices by JAX's collectives and lax.ppermute only.
A program may use at most 192 MiB of HBM per device.

```python
import jax
import jax.numpy as jnp
from jax import lax

D = 1024
FF = 4096
HD = 64
P_SIZE = 576
KEEP = 512
S = 8
IMAGES = 32


def draw_keep_mask(key, part):
    image_keys = jax.random.split(key, IMAGES)

    def one_image(image_key):
        order = jax.random.permutation(image_key, P_SIZE)
        ranks = jnp.zeros((P_SIZE,), jnp.int32).at[order].set(jnp.arange(P_SIZE, dtype=jnp.int32))
        return (ranks < KEEP).astype(jnp.int32)
    return jax.vmap(one_image)(image_keys)


def strengthened(array, key, source, target, blocks, factor):
    owner, partner = [(jnp.arange(array.shape[dim]) // (array.shape[dim] // blocks)).reshape([-1 if axis == dim else 1 for axis in range(array.ndim)]) for dim in (source, target)]
    chosen = jax.random.permutation(key, blocks)[partner]
    strong = (owner == chosen) | (owner == (partner + blocks // 2) % blocks)
    return jnp.where(strong, factor * array, array)


def level_of(rng, extent, pieces, least, high):
    def one(axis_at, parts):
        heights = jax.random.uniform(jax.random.fold_in(jax.random.fold_in(rng, 6), axis_at), (parts,), jnp.float32, least / len(pieces), high / len(pieces))
        return jnp.repeat(jnp.exp(heights), extent[axis_at] // parts).reshape((-1,) + (1,) * (len(extent) - axis_at - 1))

    factor_of = one(*pieces[0])
    for cut in pieces[1:]:
        factor_of = factor_of * one(*cut)
    return factor_of


def bell_draw(key, shape, deviation, reach, shards=(), held_as=jnp.bfloat16):
    result = deviation * jax.random.normal(key, shape, jnp.float32)
    if shards:
        result = result * level_of(key, shape, shards, -0.22, 0.18)
    return jnp.clip(result, -reach, reach).astype(held_as)


def bell_draw_with(own_key, shape, deviation, reach, pieces, heavy, held_as=jnp.bfloat16):
    array = deviation * jax.random.normal(own_key, shape, jnp.float32)
    if pieces:
        array = array * level_of(own_key, shape, pieces, -0.22, 0.18)
    return jnp.clip(strengthened(array, jax.random.fold_in(own_key, 3), *heavy), -reach, reach).astype(held_as)


def setup_inputs(seed: int = 0) -> dict:
    streams_of = jax.random.split(jax.random.key(seed), 21)
    patches = bell_draw(streams_of[0], (IMAGES, P_SIZE, D), 1.0, 6.0, ((0, 32),))
    keep_mask = draw_keep_mask(jax.random.fold_in(streams_of[20], 71), 0)
    block_cotangent = bell_draw_with(streams_of[2], (IMAGES, P_SIZE, D), 1.0, 6.0, ((0, 32),), (0, 2, 32, 2.75))
    token_cotangent = bell_draw(streams_of[3], (IMAGES, S, D), 1.0, 6.0, ((0, 16), (1, 2)))
    first_gain = jnp.clip(1.0 + 0.18 * jax.random.normal(streams_of[4], (D,), jnp.float32), 0.1, 1.9)
    first_shift = bell_draw(streams_of[5], (D,), 0.5, 3.0, ((0, 32),), jnp.float32)
    qkv_weight = bell_draw(streams_of[6], (D, 3 * D), D ** -0.5, 0.1875, ((0, 32),), jnp.float32)
    query_bias = bell_draw(streams_of[7], (D,), 0.5, 3.0, ((0, 32),), jnp.float32)
    value_bias = bell_draw(streams_of[8], (D,), 0.5, 3.0, ((0, 32),), jnp.float32)
    out_weight = bell_draw(streams_of[9], (D, D), (D // 64) ** -0.5, 1.5, ((0, 32),), jnp.float32)
    out_bias = bell_draw(streams_of[10], (D,), 0.5, 3.0, ((0, 32),), jnp.float32)
    second_gain = jnp.clip(1.0 + 0.18 * jax.random.normal(streams_of[11], (D,), jnp.float32), 0.1, 1.9)
    second_shift = bell_draw(streams_of[12], (D,), 0.5, 3.0, ((0, 32),), jnp.float32)
    up_weight = bell_draw(streams_of[13], (D, FF), D ** -0.5, 0.1875, ((0, 32),), jnp.float32)
    up_bias = bell_draw(streams_of[14], (FF,), 0.5, 3.0, ((0, 32),), jnp.float32)
    down_weight = bell_draw(streams_of[15], (FF, D), FF ** -0.5, 0.09375, ((0, 32),), jnp.float32)
    down_bias = bell_draw(streams_of[16], (D,), 0.5, 3.0, ((0, 32),), jnp.float32)
    learn_gain = jnp.clip(1.0 + 0.18 * jax.random.normal(streams_of[17], (D,), jnp.float32), 0.1, 1.9)
    learn_shift = bell_draw(streams_of[18], (D,), 0.5, 3.0, ((0, 32),), jnp.float32)
    map_weight = bell_draw(streams_of[19], (D, S), D ** -0.5, 0.1875, ((0, 32),), jnp.float32)
    return {"patches": patches, "keep_mask": keep_mask, "block_cotangent": block_cotangent, "token_cotangent": token_cotangent, "first_gain": first_gain, "first_shift": first_shift, "qkv_weight": qkv_weight, "query_bias": query_bias, "value_bias": value_bias, "out_weight": out_weight, "out_bias": out_bias, "second_gain": second_gain, "second_shift": second_shift, "up_weight": up_weight, "up_bias": up_bias, "down_weight": down_weight, "down_bias": down_bias, "learn_gain": learn_gain, "learn_shift": learn_shift, "map_weight": map_weight}


@jax.custom_vjp
def low(v):
    return lax.optimization_barrier(v.astype(jnp.bfloat16)).astype(jnp.float32)

@jax.custom_vjp
def low_back(v):
    return v

def low_keep(v):
    return (low(v), None)

def low_pass(kept, grad):
    return (grad,)

def back_keep(v):
    return (v, None)

def back_low(kept, grad):
    return (low(grad),)
low.defvjp(low_keep, low_pass)
low_back.defvjp(back_keep, back_low)
HIGHEST = lax.Precision.HIGHEST
EPSILON = 1e-06
MASKED_SCORE = -1e+30

def layer_norm(values, gain, shift):
    center = values - lax.optimization_barrier(jnp.mean(values, axis=-1, keepdims=True))
    return center * lax.rsqrt(lax.optimization_barrier(jnp.mean(center * center, axis=-1, keepdims=True)) + EPSILON) * gain + shift

def both_ways(values):
    return low_back(low(values))

def product(left, right):
    return jnp.dot(left, right, precision=HIGHEST)

def forward(image, mask, params):
    gain_one, shift_one, qkv_full, query_shift, value_shift, out_full, out_shift, gain_two, shift_two, up_full, up_shift, down_full, down_shift, learn_scale, learn_offset, map_full = tuple((low(entry) for entry in params))
    model_width = image.shape[-1]
    head_count = model_width // HD
    hidden_one = low(layer_norm(image, gain_one, shift_one))
    qkv_proj = product(hidden_one, qkv_full)
    queries = both_ways((qkv_proj[:, :model_width] + query_shift) * HD ** (-0.5)).reshape(P_SIZE, head_count, HD)
    keys_all = both_ways(qkv_proj[:, model_width:2 * model_width]).reshape(P_SIZE, head_count, HD)
    values_all = both_ways(qkv_proj[:, 2 * model_width:] + value_shift).reshape(P_SIZE, head_count, HD)
    scores = low_back(jnp.einsum('phd,khd->hpk', queries, keys_all, precision=HIGHEST))
    scores = jnp.where(mask[None, None, :] > 0, scores, MASKED_SCORE)
    attention = low(jax.nn.softmax(scores, axis=-1))
    mixed = both_ways(jnp.einsum('hpk,khd->phd', attention, values_all, precision=HIGHEST).reshape(P_SIZE, model_width))
    residual_one = image + low_back(product(mixed, out_full) + out_shift)
    hidden_two = low(layer_norm(residual_one, gain_two, shift_two))
    pre_act = low_back(product(hidden_two, up_full) + up_shift)
    activation = low(jax.nn.gelu(pre_act, approximate=False))
    block = residual_one + low_back(product(activation, down_full) + down_shift)
    learned_in = layer_norm(block, learn_scale, learn_offset)
    sigma = jax.nn.sigmoid(product(learned_in, map_full))
    token_weights = sigma * (mask[:, None].astype(jnp.float32) * KEEP ** (-0.5))
    learned = product(token_weights.T, block)
    return (block, learned)

def reference(patches, keep_mask, block_cotangent, token_cotangent, first_gain, first_shift, qkv_weight, query_bias, value_bias, out_weight, out_bias, second_gain, second_shift, up_weight, up_bias, down_weight, down_bias, learn_gain, learn_shift, map_weight):
    params = (first_gain, first_shift, qkv_weight, query_bias, value_bias, out_weight, out_bias, second_gain, second_shift, up_weight, up_bias, down_weight, down_bias, learn_gain, learn_shift, map_weight)

    def one_image(running, record):
        image, mask, cot_block, cot_tokens = record

        def run(picture, weights):
            return forward(picture, mask, weights)
        results, pull = jax.vjp(run, image.astype(jnp.float32), params)
        grad_image, grad_params = pull((cot_block.astype(jnp.float32), cot_tokens.astype(jnp.float32)))
        running = jax.tree.map(lambda earlier, fresh: earlier + fresh, running, grad_params)
        return (running, (results[0].astype(jnp.bfloat16), results[1].astype(jnp.bfloat16), grad_image.astype(jnp.bfloat16)))
    start = jax.tree.map(jnp.zeros_like, params)
    totals, (block_out, tokens, grad_patches) = lax.scan(one_image, start, (patches, keep_mask, block_cotangent, token_cotangent))
    return (block_out, tokens, grad_patches, totals[0], totals[1], totals[2], totals[3], totals[4], totals[5], totals[6], totals[7], totals[8], totals[9], totals[10], totals[11], totals[12], totals[13], totals[14], totals[15])
```

```python
import jax
import jax.numpy as jnp
from jax import lax
from jax.experimental import pallas as pl
from jax.experimental.pallas import tpu as pltpu
from jax.sharding import PartitionSpec as P

HD = 64
KEEP = 512
AXES = ("dp", "map")
BLOCKS = 32
CHUNKS = 4
HIGHEST = lax.Precision.HIGHEST
EPSILON = 1e-06
MASKED_SCORE = -1e30
BF = jnp.bfloat16
F32 = jnp.float32


def params(*semantics, vmem=56):
    return pltpu.CompilerParams(
        dimension_semantics=semantics or None, vmem_limit_bytes=vmem * 2**20
    )


def cost(flops, moved, trans=0):
    return pl.CostEstimate(
        flops=int(flops), bytes_accessed=int(moved), transcendentals=int(trans)
    )


def shape(dims, dtype):
    return jax.ShapeDtypeStruct(tuple(dims), dtype)


def normalize(values):
    center = values - jnp.mean(values, axis=-1, keepdims=True)
    spread = lax.rsqrt(jnp.mean(center * center, axis=-1, keepdims=True) + EPSILON)
    return (center * spread, spread)


def norm_back(grad_hat, normed, spread):
    return spread * (
        grad_hat
        - jnp.mean(grad_hat, axis=-1, keepdims=True)
        - normed * jnp.mean(grad_hat * normed, axis=-1, keepdims=True)
    )


def dot(left, right, dims, precision=None):
    return lax.dot_general(
        left, right, (dims, ((), ())), preferred_element_type=F32, precision=precision
    )


NN = ((1,), (0,))
NT = ((1,), (1,))
TN = ((0,), (0,))


def column_sum(values):
    return jnp.sum(values.astype(F32), axis=0)


def permute(values, masks):
    pairs = [(i, i ^ masks[(i >> 1) & 1]) for i in range(BLOCKS)]
    return lax.ppermute(values, AXES, pairs)


CORE, MAP, XDIM, Z_NEAR, Z_FAR = 2, 1, 4, 8, 16
BOTH = lambda mask: (mask, mask)
FIRST = (XDIM, MAP)
LAST = (MAP, XDIM)


def slot_table(layered):
    slots = jnp.arange(BLOCKS, dtype=jnp.int32)
    if not layered:
        return slots
    me = (lax.axis_index("dp") * lax.axis_size("map") + lax.axis_index("map")).astype(jnp.int32)
    other, last, first, near, far = ((slots >> bit) & 1 for bit in (4, 3, 2, 1, 0))
    owner = ((me >> 1) & 1) ^ other
    plane = jnp.where(owner == 0, last * MAP + first * XDIM, last * XDIM + first * MAP)
    return me ^ (other * CORE + near * Z_NEAR + far * Z_FAR + plane)


def gather_layered(wire):
    stack = jnp.concatenate([wire, permute(wire, BOTH(Z_FAR))], axis=0)
    stack = jnp.concatenate([stack, permute(stack, BOTH(Z_NEAR))], axis=0)
    stack = jnp.concatenate([stack, permute(stack, FIRST)], axis=0)
    rest = permute(stack, LAST)
    return stack, rest, permute(stack, BOTH(CORE)), permute(rest, BOTH(CORE))


def assemble(table, pieces):
    rows, cols = pieces[0].shape
    step = rows * 4 // BLOCKS

    def kernel(table_ref, *refs):
        sources, out, sems = refs[:4], refs[4], refs[5]
        copies = []
        for slot in range(BLOCKS):
            piece, place = divmod(slot, BLOCKS // 4)
            start = pl.multiple_of(table_ref[slot] * step, step)
            copies.append(
                pltpu.make_async_copy(
                    sources[piece].at[pl.ds(place * step, step)],
                    out.at[pl.ds(start, step)],
                    sems.at[slot],
                )
            )
        for copy in copies:
            copy.start()
        for copy in copies:
            copy.wait()

    return pl.pallas_call(
        kernel,
        out_shape=shape((rows * 4, cols), pieces[0].dtype),
        in_specs=[pl.BlockSpec(memory_space=pltpu.SMEM)]
        + [pl.BlockSpec(memory_space=pl.ANY)] * 4,
        out_specs=pl.BlockSpec(memory_space=pl.ANY),
        scratch_shapes=[pltpu.SemaphoreType.DMA((BLOCKS,))],
        compiler_params=params(vmem=8),
        cost_estimate=cost(0, 16 * rows * cols),
        name="assemble",
    )(table, *pieces)


def scatter_sum(keep, send, layered):
    rows, cols = keep.shape
    if not layered:
        whole = jnp.concatenate([keep, send], axis=0)
        return lax.psum_scatter(whole.astype(F32), AXES, scatter_dimension=0, tiled=True)
    stages = (BOTH(CORE), LAST, FIRST, BOTH(Z_NEAR), BOTH(Z_FAR))
    for at, masks in enumerate(stages):
        got = permute(send, masks)
        if at == len(stages) - 1:
            return keep.astype(F32) + got.astype(F32)
        half = rows // 2
        low = (keep[:half].astype(F32) + got[:half].astype(F32)).astype(BF)
        send = (keep[half:].astype(F32) + got[half:].astype(F32)).astype(BF)
        keep, rows = low, half


def attend(qkv, live):
    rows, width = qkv.shape[0], qkv.shape[1] // 3
    pairs = width // (2 * HD)

    def kernel(q_ref, k_ref, v_ref, live_ref, mixed_ref, total_ref):
        alive = live_ref[...] > 0
        q, k = q_ref[...], k_ref[...]
        value_t = v_ref[...].T
        parts = []
        for h in range(2):
            cut = slice(h * HD, (h + 1) * HD)
            scores = jnp.where(alive, dot(k[:, cut], q[:, cut], NT), MASKED_SCORE)
            peak = jnp.max(scores, axis=0, keepdims=True)
            expons = jnp.exp(scores - peak)
            total = jnp.sum(expons, axis=0, keepdims=True)
            attention = (expons * (1.0 / total)).astype(BF)
            parts.append(dot(value_t[cut], attention, NN))
            total_ref[0, h : h + 1, :] = peak + jnp.log(total)
        mixed_ref[...] = jnp.concatenate(parts, axis=0).T.astype(BF)

    pair = 2 * HD
    return pl.pallas_call(
        kernel,
        grid=(pairs,),
        in_specs=[
            pl.BlockSpec((rows, pair), lambda i: (0, i)),
            pl.BlockSpec((rows, pair), lambda i: (0, pairs + i)),
            pl.BlockSpec((rows, pair), lambda i: (0, 2 * pairs + i)),
            pl.BlockSpec((rows, 1), lambda i: (0, 0)),
        ],
        out_specs=[
            pl.BlockSpec((rows, pair), lambda i: (0, i)),
            pl.BlockSpec((1, 2, rows), lambda i: (i, 0, 0)),
        ],
        out_shape=[shape((rows, width), BF), shape((pairs, 2, rows), F32)],
        compiler_params=params("arbitrary"),
        cost_estimate=cost(16 * rows * rows * width, 8 * rows * width, rows * rows * pairs * 2),
        name="attend",
    )(qkv, qkv, qkv, live)


def attend_back(qkv, live, totals, grad_mixed):
    rows, width = grad_mixed.shape
    pairs = width // (2 * HD)
    scaling = HD ** (-0.5)

    def kernel(q_ref, k_ref, v_ref, live_ref, total_ref, gm_ref, out_ref, sum_ref):
        alive = live_ref[...] > 0
        q, k, v, gm = q_ref[...], k_ref[...], v_ref[...], gm_ref[...]
        key_t = k.T
        queries, keys, values = [], [], []
        for h in range(2):
            cut = slice(h * HD, (h + 1) * HD)
            scores = jnp.where(alive, dot(k[:, cut], q[:, cut], NT), MASKED_SCORE)
            probs = jnp.exp(scores - total_ref[0, h : h + 1, :])
            grad_probs = dot(v[:, cut], gm[:, cut], NT)
            along = jnp.sum(probs * grad_probs, axis=0, keepdims=True)
            grad_scores = (probs * (grad_probs - along)).astype(BF)
            values.append(dot(probs.astype(BF), gm[:, cut], NN))
            keys.append(dot(grad_scores, q[:, cut], NN))
            queries.append(dot(key_t[cut], grad_scores, NN))
        grad_q = jnp.concatenate(queries, axis=0).T.astype(BF).astype(F32) * scaling
        grad_v = jnp.concatenate(values, axis=1).astype(BF)
        out_ref[0] = grad_q.astype(BF)
        out_ref[1] = jnp.concatenate(keys, axis=1).astype(BF)
        out_ref[2] = grad_v
        sum_ref[0:1, :] = jnp.sum(grad_q, axis=0, keepdims=True)
        sum_ref[1:2, :] = jnp.sum(grad_v.astype(F32), axis=0, keepdims=True)

    pair = 2 * HD
    return pl.pallas_call(
        kernel,
        grid=(pairs,),
        in_specs=[
            pl.BlockSpec((rows, pair), lambda i: (0, i)),
            pl.BlockSpec((rows, pair), lambda i: (0, pairs + i)),
            pl.BlockSpec((rows, pair), lambda i: (0, 2 * pairs + i)),
            pl.BlockSpec((rows, 1), lambda i: (0, 0)),
            pl.BlockSpec((1, 2, rows), lambda i: (i, 0, 0)),
            pl.BlockSpec((rows, pair), lambda i: (0, i)),
        ],
        out_specs=[
            pl.BlockSpec((3, rows, pair), lambda i: (0, 0, i)),
            pl.BlockSpec((2, pair), lambda i: (0, i)),
        ],
        out_shape=[shape((3, rows, width), BF), shape((2, width), F32)],
        compiler_params=params("arbitrary"),
        cost_estimate=cost(40 * rows * rows * width, 14 * rows * width, rows * rows * pairs * 2),
        name="attend_back",
    )(qkv, qkv, qkv, live, totals, grad_mixed)


def feed_forward(hidden, residual, up, up_at, up_bias, down, down_bias):
    rows, width = hidden.shape
    span = up_bias.shape[1]

    def kernel(h_ref, r_ref, up_ref, ub_ref, down_ref, db_ref, block_ref, act_ref, slope_ref):
        step = pl.program_id(0)

        @pl.when(step == 0)
        def _():
            block_ref[...] = r_ref[...] + db_ref[...]

        weight = up_ref[...].reshape(width, span)
        x = dot(h_ref[...], weight, NN) + ub_ref[pl.ds(step, 1), :]
        half = 0.5 + 0.5 * lax.erf(x * (0.5**0.5))
        act = (x * half).astype(BF)
        act_ref[...] = act
        slope_ref[...] = (half + x * jnp.exp(-0.5 * x * x) * 0.3989422804014327).astype(BF)
        block_ref[...] += dot(act, down_ref[...], NN)

    return pl.pallas_call(
        kernel,
        grid=(CHUNKS,),
        in_specs=[
            pl.BlockSpec((rows, width), lambda j: (0, 0)),
            pl.BlockSpec((rows, width), lambda j: (0, 0)),
            pl.BlockSpec((BLOCKS, None, width // BLOCKS, span), lambda j: (0, j, 0, up_at)),
            pl.BlockSpec((CHUNKS, span), lambda j: (0, 0)),
            pl.BlockSpec((span, width), lambda j: (j, 0)),
            pl.BlockSpec((1, width), lambda j: (0, 0)),
        ],
        out_specs=[
            pl.BlockSpec((rows, width), lambda j: (0, 0)),
            pl.BlockSpec((rows, span), lambda j: (0, j)),
            pl.BlockSpec((rows, span), lambda j: (0, j)),
        ],
        out_shape=[
            shape((rows, width), F32),
            shape((rows, span * CHUNKS), BF),
            shape((rows, span * CHUNKS), BF),
        ],
        compiler_params=params("arbitrary"),
        cost_estimate=cost(4 * rows * width * span * CHUNKS, 30 * 2**20),
        name="feed_forward",
    )(hidden, residual, up, up_bias, down, down_bias)


def feed_forward_back(grad_down, slope, up, up_at, down):
    rows, width = grad_down.shape
    span = slope.shape[1] // CHUNKS

    def kernel(g_ref, slope_ref, up_ref, down_ref, pre_ref, sum_ref, out_ref):
        step = pl.program_id(0)
        grad_act = dot(g_ref[...], down_ref[...], NT)
        grad_pre = (grad_act * slope_ref[...].astype(F32)).astype(BF)
        pre_ref[...] = grad_pre
        sum_ref[pl.ds(step, 1), :] = jnp.sum(grad_pre.astype(F32), axis=0, keepdims=True)
        part = dot(grad_pre, up_ref[...].reshape(width, span), NT)

        @pl.when(step == 0)
        def _():
            out_ref[...] = part

        @pl.when(step > 0)
        def _():
            out_ref[...] += part

    return pl.pallas_call(
        kernel,
        grid=(CHUNKS,),
        in_specs=[
            pl.BlockSpec((rows, width), lambda j: (0, 0)),
            pl.BlockSpec((rows, span), lambda j: (0, j)),
            pl.BlockSpec((BLOCKS, None, width // BLOCKS, span), lambda j: (0, j, 0, up_at)),
            pl.BlockSpec((span, width), lambda j: (j, 0)),
        ],
        out_specs=[
            pl.BlockSpec((rows, span), lambda j: (0, j)),
            pl.BlockSpec((CHUNKS, span), lambda j: (0, 0)),
            pl.BlockSpec((rows, width), lambda j: (0, 0)),
        ],
        out_shape=[
            shape((rows, span * CHUNKS), BF),
            shape((CHUNKS, span), F32),
            shape((rows, width), F32),
        ],
        compiler_params=params("arbitrary"),
        cost_estimate=cost(4 * rows * width * span * CHUNKS, 28 * 2**20),
        name="feed_forward_back",
    )(grad_down, slope, up, down)


def token_learner(block, cotangent, live, token_grad, map_t, scale, offset):
    rows, width = block.shape
    count = map_t.shape[0]
    band = rows // 4

    def kernel(b_ref, c_ref, live_ref, tg_ref, map_ref, s_ref, o_ref, *outs):
        out_ref, tok_ref, grad_ref, low_ref, gmap_ref, sums_ref = outs
        values, alive = b_ref[...], live_ref[...]
        grads, weights, scale_row = tg_ref[...], map_ref[...], s_ref[...]
        normed, spread = normalize(values)
        learned = normed * scale_row + o_ref[...]
        sigma = jax.nn.sigmoid(dot(learned, weights, NT, HIGHEST))
        token_weights = sigma * alive
        tokens = dot(token_weights, values, TN, HIGHEST)
        logits = dot(values, grads, NT, HIGHEST) * alive * sigma * (1.0 - sigma)
        grad_map = dot(logits, learned, TN, HIGHEST)
        grad_learned = dot(logits, weights, NN, HIGHEST)
        grad = c_ref[...].astype(F32) + dot(token_weights, grads, NN, HIGHEST)
        grad = grad + norm_back(grad_learned * scale_row, normed, spread)
        low = grad.astype(BF)
        out_ref[...] = values.astype(BF)
        grad_ref[...] = grad
        low_ref[...] = low
        sums = jnp.concatenate(
            [
                jnp.sum(grad_learned * normed, axis=0, keepdims=True),
                jnp.sum(grad_learned, axis=0, keepdims=True),
                jnp.sum(low.astype(F32), axis=0, keepdims=True),
            ],
            axis=0,
        )

        @pl.when(pl.program_id(0) == 0)
        def _():
            tok_ref[...] = tokens
            gmap_ref[...] = grad_map
            sums_ref[...] = sums

        @pl.when(pl.program_id(0) > 0)
        def _():
            tok_ref[...] += tokens
            gmap_ref[...] += grad_map
            sums_ref[...] += sums

    banded = pl.BlockSpec((band, width), lambda i: (i, 0))
    fixed = lambda n: pl.BlockSpec((n, width), lambda i: (0, 0))
    return pl.pallas_call(
        kernel,
        grid=(4,),
        in_specs=[banded, banded, pl.BlockSpec((band, 1), lambda i: (i, 0))]
        + [fixed(count), fixed(count), fixed(1), fixed(1)],
        out_specs=[banded, fixed(count), banded, banded, fixed(count), fixed(3)],
        out_shape=[
            shape((rows, width), BF),
            shape((count, width), F32),
            shape((rows, width), F32),
            shape((rows, width), BF),
            shape((count, width), F32),
            shape((3, width), F32),
        ],
        compiler_params=params("arbitrary"),
        cost_estimate=cost(80 * rows * width * count * 4, 14 * rows * width),
        name="token_learner",
    )(block, cotangent, live, token_grad, map_t, scale, offset)


def weight_grad(table, left, right, tile):
    rows, height = left.shape
    step = height // BLOCKS
    parts = right.shape[0] if right.ndim == 3 else 1
    per_part = right.shape[-1] // tile
    cols = parts * right.shape[-1]

    def kernel(table_ref, l_ref, r_ref, keep_ref, send_ref, turned, *spare):
        @pl.when(pl.program_id(0) == 0)
        def _():
            if step % 128 == 0:
                for slot in range(BLOCKS):
                    at = pl.multiple_of(table_ref[slot] * step, step)
                    turned[slot * step : (slot + 1) * step, :] = l_ref[:, pl.ds(at, step)].T
            else:
                spare[0][...] = l_ref[...].T
                for slot in range(BLOCKS):
                    at = pl.multiple_of(table_ref[slot] * step, step)
                    turned[slot * step : (slot + 1) * step, :] = spare[0][pl.ds(at, step), :]

        value = r_ref[...]
        half = height // 2
        send_ref[...] = dot(turned[half:, :], value, NN).astype(BF)
        keep_ref[...] = dot(turned[:half, :], value, NN).astype(BF)

    if right.ndim == 3:
        right_spec = pl.BlockSpec((None, rows, tile), lambda n: (n // per_part, 0, n % per_part))
    else:
        right_spec = pl.BlockSpec((rows, tile), lambda n: (0, n))
    scratch = [pltpu.VMEM((height, rows), BF)]
    if step % 128:
        scratch.append(pltpu.VMEM((height, rows), BF))
    half_spec = pl.BlockSpec((height // 2, tile), lambda n: (0, n))
    return pl.pallas_call(
        kernel,
        grid=(cols // tile,),
        in_specs=[
            pl.BlockSpec(memory_space=pltpu.SMEM),
            pl.BlockSpec((rows, height), lambda n: (0, 0)),
            right_spec,
        ],
        out_specs=[half_spec, half_spec],
        out_shape=[shape((height // 2, cols), BF)] * 2,
        scratch_shapes=scratch,
        compiler_params=params("arbitrary"),
        cost_estimate=cost(
            2 * rows * height * cols, 2 * (rows * height + rows * cols + height * cols)
        ),
        name="weight_grad",
    )(table, left, right)


def gather_weights(layered, table, qkv_wire, out_wire, up_wire, down_wire):
    span = up_wire.shape[1] // CHUNKS
    if layered:
        chunks = [up_wire[:, j * span : (j + 1) * span] for j in range(CHUNKS)]
        both = jnp.concatenate([down_wire, jnp.concatenate(chunks, axis=0)], axis=1)
        both = lax.all_gather(both, AXES, axis=0, tiled=True)
        qkv = assemble(table, gather_layered(qkv_wire))
        out = assemble(table, gather_layered(out_wire))
        up = both.reshape(BLOCKS, CHUNKS, -1, both.shape[1])
        return qkv, out, up, 1, both
    whole = lambda wire: lax.all_gather(wire, AXES, axis=0, tiled=True)
    up = whole(up_wire)
    up = up.reshape(BLOCKS, -1, CHUNKS, span).transpose(0, 2, 1, 3)
    return whole(qkv_wire), whole(out_wire), up, 0, whole(down_wire)


def per_device(
    patches,
    keep_mask,
    block_cotangent,
    token_cotangent,
    first_gain,
    first_shift,
    qkv_weight,
    query_bias,
    value_bias,
    out_weight,
    out_bias,
    second_gain,
    second_shift,
    up_weight,
    up_bias,
    down_weight,
    down_bias,
    learn_gain,
    learn_shift,
    map_weight,
):
    devices = lax.axis_size("dp") * lax.axis_size("map")
    layered = devices == BLOCKS and lax.axis_size("map") == 2
    images, patch_count, width = patches.shape
    rows = images * patch_count
    own = first_gain.shape[0]
    scaling = HD ** (-0.5)
    table = slot_table(layered)

    vectors = (
        first_gain,
        first_shift,
        query_bias,
        value_bias,
        out_bias,
        second_gain,
        second_shift,
        down_bias,
        learn_gain,
        learn_shift,
    )
    fan = up_bias.shape[0] // own
    count = map_weight.shape[1]
    small = jnp.concatenate(
        [jnp.stack(vectors, axis=1), up_bias.reshape(own, fan), map_weight], axis=1
    )
    small = jnp.pad(small, ((0, 0), (0, 128 - small.shape[1]))).astype(BF)
    qkv_wire = jnp.concatenate([qkv_weight.astype(BF), small], axis=1)
    qkv_full, out_full, up_full, up_at, down_full = gather_weights(
        layered,
        table,
        qkv_wire,
        out_weight.astype(BF),
        up_weight.astype(BF),
        down_weight.astype(BF),
    )
    small = qkv_full[:, 3 * width :].astype(F32)
    qkv_full = qkv_full[:, : 3 * width]
    small_t = small.T
    (
        gain_one,
        shift_one,
        query_shift,
        value_shift,
        out_shift,
        gain_two,
        shift_two,
        down_shift,
        learn_scale,
        learn_offset,
    ) = (small_t[i] for i in range(len(vectors)))
    at = len(vectors)
    up_shift = small[:, at : at + fan].reshape(CHUNKS, -1)
    map_t = small_t[at + fan : at + fan + count]

    token_grad = lax.all_to_all(
        token_cotangent, "map", split_axis=0, concat_axis=1, tiled=True
    ).astype(F32)
    live = keep_mask.reshape(rows, 1).astype(F32)

    inputs = patches.reshape(rows, width).astype(F32)
    normed_one, spread_one = normalize(inputs)
    hidden_one = (normed_one * gain_one + shift_one).astype(BF)
    qkv = dot(hidden_one, qkv_full, NN)
    added = jnp.concatenate([query_shift, jnp.zeros_like(query_shift), value_shift])
    factor = jnp.concatenate([jnp.full((width,), scaling, F32), jnp.ones((2 * width,), F32)])
    qkv = ((qkv + added) * factor).astype(BF)
    mixed, totals = attend(qkv, live)
    residual_one = inputs + dot(mixed, out_full, NN) + out_shift
    normed_two, spread_two = normalize(residual_one)
    hidden_two = (normed_two * gain_two + shift_two).astype(BF)
    block, activation, slope = feed_forward(
        hidden_two, residual_one, up_full, up_at, up_shift, down_full, down_shift[None]
    )
    block_out, token_local, grad_block, grad_down_low, grad_map, sums = token_learner(
        block,
        block_cotangent.reshape(rows, width),
        live * KEEP ** (-0.5),
        token_grad.reshape(count, width),
        map_t,
        learn_scale[None],
        learn_offset[None],
    )
    tokens_out = lax.all_to_all(
        token_local.reshape(images, count, width).astype(BF),
        "map",
        split_axis=1,
        concat_axis=0,
        tiled=True,
    )
    grad_down = scatter_sum(*weight_grad(table, activation, grad_down_low, 256), layered)
    grad_pre, grad_up_shift, grad_hidden_two = feed_forward_back(
        grad_down_low, slope, up_full, up_at, down_full
    )
    grad_up = scatter_sum(*weight_grad(table, hidden_two, grad_pre, 512), layered)
    grad_gain_two = jnp.sum(grad_hidden_two * normed_two, axis=0)
    grad_shift_two = jnp.sum(grad_hidden_two, axis=0)
    grad_residual = grad_block + norm_back(grad_hidden_two * gain_two, normed_two, spread_two)
    grad_attn = grad_residual.astype(BF)
    grad_out = scatter_sum(*weight_grad(table, mixed, grad_attn, 512), layered)
    grad_out_shift = column_sum(grad_attn)
    grad_mixed = dot(grad_attn, out_full, NT).astype(BF)
    grad_qkv, qv_sums = attend_back(qkv, live, totals, grad_mixed)
    grad_qkv_full = scatter_sum(*weight_grad(table, hidden_one, grad_qkv, 512), layered)
    grad_hidden_one = sum(
        dot(grad_qkv[i], qkv_full[:, i * width : (i + 1) * width], NT) for i in range(3)
    )
    grad_gain_one = jnp.sum(grad_hidden_one * normed_one, axis=0)
    grad_shift_one = jnp.sum(grad_hidden_one, axis=0)
    grad_inputs = grad_residual + norm_back(grad_hidden_one * gain_one, normed_one, spread_one)
    grad_patches = grad_inputs.reshape(images, patch_count, width).astype(BF)

    terms = (
        grad_gain_one,
        grad_shift_one,
        qv_sums[0],
        qv_sums[1],
        grad_out_shift,
        grad_gain_two,
        grad_shift_two,
        sums[2],
        sums[0],
        sums[1],
        grad_up_shift.reshape(-1),
    )
    packed = [term.reshape(devices, -1) for term in terms]
    packed.append(grad_map.reshape(count, devices, own).transpose(1, 2, 0).reshape(devices, -1))
    packed = jnp.concatenate(packed, axis=1)
    summed = jnp.sum(lax.all_to_all(packed, AXES, 0, 0, tiled=True), axis=0)
    pieces = [summed[i * own : (i + 1) * own] for i in range(10)]
    at = 10 * own
    up_piece = summed[at : at + fan * own]
    map_piece = summed[at + fan * own :].reshape(own, count)
    return (
        block_out.reshape(images, patch_count, width),
        tokens_out,
        grad_patches,
        pieces[0],
        pieces[1],
        grad_qkv_full,
        pieces[2],
        pieces[3],
        grad_out,
        pieces[4],
        pieces[5],
        pieces[6],
        grad_up,
        up_piece,
        grad_down,
        pieces[7],
        pieces[8],
        pieces[9],
        map_piece,
    )


def solution(mesh):
    rows = P(("dp", "map"))
    wide = P(("dp", "map"), None)
    images = P(("dp", "map"), None, None)
    tokens = P("dp", "map", None)
    weights = (
        rows, rows, wide, rows, rows, wide, rows, rows,
        rows, wide, rows, wide, rows, rows, rows, wide,
    )
    return jax.shard_map(
        per_device,
        mesh=mesh,
        in_specs=(images, wide, images, tokens) + weights,
        out_specs=(images, tokens, images) + weights,
        check_vma=False,
    )
```

```python
import jax
import jax.numpy as jnp
from jax import lax
from jax.experimental import pallas as pl
from jax.experimental.pallas import tpu as pltpu
from jax.sharding import PartitionSpec as P

HD = 64
KEEP = 512
AXES = ("dp", "map")
BLOCKS = 32
HIGHEST = lax.Precision.HIGHEST
EPSILON = 1e-06
MASKED_SCORE = -1e30
BF = jnp.bfloat16
F32 = jnp.float32


def params(*semantics, vmem=44):
    return pltpu.CompilerParams(
        dimension_semantics=semantics or None, vmem_limit_bytes=vmem * 2**20
    )


def cost(flops, moved, trans=0):
    return pl.CostEstimate(flops=10**12, bytes_accessed=1024, transcendentals=0)


CHAIN = []


def launch(kernel, in_specs, after=(), **settings):
    def run(*operands):
        given, waited = len(operands), (*CHAIN, *after)

        def body(*refs):
            kernel(*refs[:given], *refs[given + len(waited) :])

        specs = list(in_specs) + [pl.BlockSpec(memory_space=pl.ANY)] * len(waited)
        outs = pl.pallas_call(body, in_specs=specs, **settings)(*operands, *waited)
        CHAIN[:] = [outs[0] if isinstance(outs, (list, tuple)) else outs]
        return outs

    return run


def shape(dims, dtype):
    return jax.ShapeDtypeStruct(tuple(dims), dtype)


def normalize(values):
    center = values - jnp.mean(values, axis=-1, keepdims=True)
    spread = lax.rsqrt(jnp.mean(center * center, axis=-1, keepdims=True) + EPSILON)
    return (center * spread, spread)


def norm_back(grad_hat, normed, spread):
    return spread * (
        grad_hat
        - jnp.mean(grad_hat, axis=-1, keepdims=True)
        - normed * jnp.mean(grad_hat * normed, axis=-1, keepdims=True)
    )


def dot(left, right, dims, precision=None):
    return lax.dot_general(
        left, right, (dims, ((), ())), preferred_element_type=F32, precision=precision
    )


NN = ((1,), (0,))
NT = ((1,), (1,))
TN = ((0,), (0,))


MAP, XDIM, Z_NEAR, Z_FAR = 1, 4, 8, 16
BOTH = lambda mask: (mask, mask)
FIRST = (XDIM, MAP)
LAST = (MAP, XDIM)
STAGES = (LAST, FIRST, BOTH(Z_NEAR), BOTH(Z_FAR))


def permute(values, masks):
    pairs = [(i, i ^ masks[(i >> 1) & 1]) for i in range(BLOCKS)]
    return lax.ppermute(values, AXES, pairs)


def to_sibling(values):
    width = lax.axis_size("map")
    devices = lax.axis_size("dp") * width
    pairs = []
    for i in range(devices):
        dp, at = divmod(i, width)
        pairs.append((i, (dp ^ 1) * width + at))
    return lax.ppermute(values, AXES, pairs)


def slot_tables(layered):
    if not layered:
        return jnp.arange(BLOCKS, dtype=jnp.int32), jnp.arange(BLOCKS // 2, dtype=jnp.int32)
    slots = jnp.arange(BLOCKS // 2, dtype=jnp.int32)
    me = (lax.axis_index("dp") * 2 + lax.axis_index("map")).astype(jnp.int32)
    last, first, near, far = ((slots >> bit) & 1 for bit in (3, 2, 1, 0))
    core = (me >> 1) & 1
    plane = jnp.where(core == 0, last * MAP + first * XDIM, last * XDIM + first * MAP)
    device = me ^ (near * Z_NEAR + far * Z_FAR + plane)
    pairs = jnp.stack([device, device ^ 2], axis=1).reshape(-1)
    return pairs, (device >> 2) * 2 + (device & 1)


def tie(values, *others):
    return lax.optimization_barrier((values, *others))[0]


class Doubling:
    def __init__(self, wire):
        self.held, self.stage = wire, len(STAGES) - 1
        self.flying = [permute(wire, STAGES[self.stage])]

    def advance(self, after=()):
        self.held = stack(self.held, self.flying[0], after)
        self.stage -= 1
        self.flying = [permute(self.held, STAGES[self.stage])]

    def last_of_held(self, *others):
        self.flying.append(permute(tie(self.held, *others), STAGES[0]))

    def last(self, *others):
        self.pieces = [self.held, *self.flying, permute(tie(self.flying[0], *others), STAGES[0])]


def swap_map(values, axis):
    at = lax.axis_index("map")
    half = values.shape[axis] // 2
    low, high = (lax.slice_in_dim(values, i * half, (i + 1) * half, axis=axis) for i in (0, 1))
    mine, send = jnp.where(at == 0, low, high), jnp.where(at == 0, high, low)
    got = permute(send, BOTH(MAP))
    return jnp.concatenate([jnp.where(at == 0, mine, got), jnp.where(at == 0, got, mine)], 1 - axis)


class Halving:
    def __init__(self, parts, direct=False):
        self.low, self.stage, self.direct = parts[0], 0, direct
        self.flying = [permute(parts[1], STAGES[0])]

    def advance(self):
        self.stage += 1
        if self.stage == 2 and self.direct:
            self.low, *parts = add_parts(self.low, self.flying[0], 4)
            masks = (Z_FAR, Z_NEAR, Z_NEAR + Z_FAR)
            self.flying = [permute(part, BOTH(mask)) for part, mask in zip(parts, masks)]
        else:
            self.low, send = add_parts(self.low, self.flying[0], 2)
            self.flying = [permute(send, STAGES[self.stage])]

    def finish(self):
        return last_sum(self.low, self.flying)


HBM = pl.BlockSpec(memory_space=pl.ANY)
TABLE = pl.BlockSpec(memory_space=pltpu.SMEM)


def start_rows(table_ref, pieces, columns, held, sems):
    step = held.shape[0] // BLOCKS
    copies = []
    for entry in range(BLOCKS):
        piece, place = divmod(entry, BLOCKS // len(pieces))
        at = pl.multiple_of(table_ref[entry] * step, step)
        copies.append(
            pltpu.make_async_copy(
                pieces[piece].at[pl.ds(place * step, step), columns],
                held.at[pl.ds(at, step), :],
                sems.at[entry],
            )
        )
    for copy in copies:
        copy.start()
    return copies


def start_halves(table_ref, pieces, columns, held, sems):
    tall, width = held.shape
    step = tall // (BLOCKS // 2)
    copies = []
    for slot in range(BLOCKS // 2):
        piece, place = divmod(slot, BLOCKS // 2 // len(pieces))
        at = pl.multiple_of(table_ref[slot] * step, step)
        for part in range(2):
            if step == 32:
                source = (pl.ds(place * 64 + part * 32, 32), columns)
                target = (pl.ds(at, 32), pl.ds(part * (width // 2), width // 2))
            else:
                source = (pl.ds(place * 64, 64), pl.ds(part * width, width))
                target = (pl.ds(at + part * 64, 64), slice(None))
            copies.append(
                pltpu.make_async_copy(
                    pieces[piece].at[source], held.at[target], sems.at[slot * 2 + part]
                )
            )
    for copy in copies:
        copy.start()
    return copies


def padded_rows(rows):
    return -(-rows // 128) * 128


def wait(copies):
    for copy in copies:
        copy.wait()


def pack_small(vectors, bias, maps):
    own, count = maps.shape
    runs = bias.shape[0] // own

    def kernel(*refs):
        rows, (bias_ref, map_ref, out_ref, held) = refs[: len(vectors)], refs[len(vectors) :]
        held[...] = jnp.zeros_like(held)
        for i, ref in enumerate(rows):
            held[count + i : count + i + 1, :own] = ref[...]
        for j in range(runs):
            at = count + len(vectors) + j
            held[at : at + 1, :own] = bias_ref[:, j * own : (j + 1) * own]
        turned = held[...].T[:own]
        held[:own, :] = turned
        held[:own, :count] = map_ref[...]
        out_ref[...] = held[:own, :].astype(BF)

    return launch(
        kernel,
        in_specs=[pl.BlockSpec(memory_space=pltpu.VMEM)] * (len(vectors) + 2),
        out_shape=shape((own, 128), BF),
        scratch_shapes=[pltpu.VMEM((128, 128), F32)],
        compiler_params=params(vmem=16),
        cost_estimate=cost(0, 0),
        name="pack_small",
    )(*(vector.reshape(1, -1) for vector in vectors), bias.reshape(1, -1), maps)


def add_parts(low, got, count):
    step, cols = low.shape[0] // count, low.shape[1]
    tile = cols // 2

    def kernel(a_ref, b_ref, *outs):
        for i, out in enumerate(outs):
            part = slice(i * step, (i + 1) * step)
            out[...] = (a_ref[part, :].astype(F32) + b_ref[part, :].astype(F32)).astype(BF)

    return launch(
        kernel,
        grid=(2,),
        in_specs=[pl.BlockSpec((count * step, tile), lambda n: (0, n))] * 2,
        out_specs=[pl.BlockSpec((step, tile), lambda n: (0, n))] * count,
        out_shape=[shape((step, cols), BF)] * count,
        compiler_params=params("arbitrary", vmem=16),
        cost_estimate=cost(0, 0),
        name="add_parts",
    )(low, got)


def last_sum(low, parts):
    half, cols = low.shape[0] // 2, low.shape[1]
    tile = cols // 2

    def kernel(low_ref, *refs):
        for i, out in enumerate(refs[-2:]):
            part = slice(i * half, (i + 1) * half)
            out[...] = sum((ref[part, :].astype(F32) for ref in refs[:-2]), low_ref[part, :].astype(F32))

    return launch(
        kernel,
        grid=(2,),
        in_specs=[pl.BlockSpec((2 * half, tile), lambda n: (0, n))] * (1 + len(parts)),
        out_specs=[pl.BlockSpec((half, tile), lambda n: (0, n))] * 2,
        out_shape=[shape((half, cols), F32)] * 2,
        compiler_params=params("arbitrary", vmem=16),
        cost_estimate=cost(0, 0),
        name="last_sum",
    )(low, *parts)


def stack(top, bottom, after=(), axis=0):
    tall, wide = top.shape
    whole = pl.BlockSpec((tall, wide), lambda i: (0, 0))
    dims = (2 * tall, wide) if axis == 0 else (tall, 2 * wide)

    def kernel(a_ref, b_ref, out_ref):
        out_ref[:tall, :wide] = a_ref[...]
        out_ref[dims[0] - tall :, dims[1] - wide :] = b_ref[...]

    return launch(
        kernel,
        after=after,
        grid=(1,),
        in_specs=[whole, whole],
        out_specs=pl.BlockSpec(dims, lambda i: (0, 0)),
        out_shape=shape(dims, BF),
        compiler_params=params("arbitrary", vmem=16),
        cost_estimate=cost(0, 0),
        name="stack",
    )(top, bottom)


def pack_small(vectors, bias, maps):
    own, count = maps.shape
    runs = bias.shape[0] // own

    def kernel(*refs):
        rows, (bias_ref, map_ref, out_ref, held) = refs[: len(vectors)], refs[len(vectors) :]
        held[...] = jnp.zeros_like(held)
        for i, ref in enumerate(rows):
            held[count + i : count + i + 1, :own] = ref[...]
        for j in range(runs):
            at = count + len(vectors) + j
            held[at : at + 1, :own] = bias_ref[:, j * own : (j + 1) * own]
        turned = held[...].T[:own]
        held[:own, :] = turned
        held[:own, :count] = map_ref[...]
        out_ref[...] = held[:own, :].astype(BF)

    return launch(
        kernel,
        in_specs=[pl.BlockSpec(memory_space=pltpu.VMEM)] * (len(vectors) + 2),
        out_shape=shape((own, 128), BF),
        scratch_shapes=[pltpu.VMEM((128, 128), F32)],
        compiler_params=params(vmem=16),
        cost_estimate=cost(0, 0),
        name="pack_small",
    )(*(vector.reshape(1, -1) for vector in vectors), bias.reshape(1, -1), maps)


def add_halves(low, got):
    half, cols = low.shape[0] // 2, low.shape[1]
    tile = cols // 2

    def kernel(a_ref, b_ref, low_ref, high_ref):
        total = a_ref[...].astype(F32) + b_ref[...].astype(F32)
        low_ref[...] = total[:half].astype(BF)
        high_ref[...] = total[half:].astype(BF)

    return launch(
        kernel,
        grid=(2,),
        in_specs=[pl.BlockSpec((2 * half, tile), lambda n: (0, n))] * 2,
        out_specs=[pl.BlockSpec((half, tile), lambda n: (0, n))] * 2,
        out_shape=[shape((half, cols), BF)] * 2,
        compiler_params=params("arbitrary", vmem=16),
        cost_estimate=cost(0, 0),
        name="add_halves",
    )(low, got)


def small_rows(table, pieces, at):
    tall = pieces[0].shape[0]
    total = tall * len(pieces)

    def kernel(table_ref, *refs):
        sources, (out_ref, held) = refs[: len(pieces)], refs[len(pieces) :]
        for entry in range(BLOCKS):
            piece, place = divmod(entry, BLOCKS // len(pieces))
            start = pl.multiple_of(table_ref[entry] * 32, 32)
            held[pl.ds(start, 32), :] = sources[piece][place * 32 : place * 32 + 32, :].astype(F32)
        out_ref[...] = held[...].T

    return launch(
        kernel,
        grid=(1,),
        in_specs=[TABLE] + [pl.BlockSpec((tall, 128), lambda i: (0, at // 128))] * len(pieces),
        out_specs=pl.BlockSpec((128, total), lambda i: (0, 0)),
        out_shape=shape((128, total), F32),
        scratch_shapes=[pltpu.VMEM((total, 128), F32)],
        compiler_params=params("arbitrary", vmem=16),
        cost_estimate=cost(0, 0),
        name="small_rows",
    )(table, *pieces)


def project(table, pieces, patches, other, gain, shift, added, factor):
    image, width = patches.shape
    rows, count, padded = 2 * image, len(pieces), padded_rows(image)
    cols = added.shape[1]
    tile = cols // 3

    def kernel(table_ref, *rest):
        gathered, rest = rest[:count], rest[count:]
        x_ref, y_ref, g_ref, s_ref, a_ref, f_ref, qkv_ref, turned_ref, stat_ref, *rest = rest
        hidden, held, sems = rest
        step = pl.program_id(0)

        @pl.when(step == 0)
        def _():
            copies = start_rows(table_ref, gathered, pl.ds(0, cols), held, sems)
            for at, ref in enumerate((x_ref, y_ref)):
                values = ref[...].astype(F32)
                mean = jnp.mean(values, axis=-1, keepdims=True)
                center = values - mean
                spread = lax.rsqrt(jnp.mean(center * center, axis=-1, keepdims=True) + EPSILON)
                normed = (center * spread * g_ref[...] + s_ref[...]).astype(BF)
                hidden[at * image : (at + 1) * image, :] = normed
                if at == 0:
                    stat_ref[...] = jnp.concatenate([mean, spread], axis=1)
            turned_ref[...] = jnp.zeros_like(turned_ref)
            for at in range(2):
                turned_ref[:, at * padded : at * padded + image] = hidden[
                    at * image : (at + 1) * image, :
                ].T
            wait(copies)

        at = pl.ds(pl.multiple_of(step * tile, tile), tile)
        product = dot(hidden[...], held[:, at], NN)
        qkv_ref[...] = ((product + a_ref[...]) * f_ref[...]).astype(BF)

    whole = lambda m, n: pl.BlockSpec((m, n), lambda j: (0, 0))
    strip = lambda m: pl.BlockSpec((m, tile), lambda j: (0, j))
    return launch(
        kernel,
        grid=(3,),
        in_specs=[TABLE] + [HBM] * count + [whole(image, width)] * 2
        + [whole(1, width), whole(1, width), strip(1), strip(1)],
        out_specs=[strip(rows), whole(width, 2 * padded), whole(image, 2)],
        out_shape=[
            shape((rows, cols), BF),
            shape((width, 2 * padded), BF),
            shape((image, 2), F32),
        ],
        scratch_shapes=[
            pltpu.VMEM((rows, width), BF),
            pltpu.VMEM((width, cols), BF),
            pltpu.SemaphoreType.DMA((BLOCKS,)),
        ],
        compiler_params=params("arbitrary"),
        cost_estimate=cost(2 * rows * width * cols, 0),
        name="project",
    )(table, *pieces, patches, other, gain, shift, added, factor)


def attend(qkv, live, after=()):
    tall, width = qkv.shape[0], qkv.shape[1] // 3
    rows = tall // 2
    padded = padded_rows(rows)
    pair = 2 * HD
    pairs = width // pair

    def kernel(q_ref, k_ref, v_ref, live_ref, mixed_ref, turned_ref, total_ref):
        turned_ref[...] = jnp.zeros_like(turned_ref)
        for image in range(2):
            part = slice(image * rows, (image + 1) * rows)
            alive = live_ref[part, :] > 0
            q, k = q_ref[part, :], k_ref[part, :]
            value_t = v_ref[part, :].T
            heads = []
            for h in range(2):
                cut = slice(h * HD, (h + 1) * HD)
                scores = jnp.where(alive, dot(k[:, cut], q[:, cut], NT), MASKED_SCORE)
                peak = jnp.max(scores, axis=0, keepdims=True)
                expons = jnp.exp(scores - peak)
                total = jnp.sum(expons, axis=0, keepdims=True)
                attention = (expons * (1.0 / total)).astype(BF)
                heads.append(dot(value_t[cut], attention, NN))
                total_ref[0, 2 * image + h : 2 * image + h + 1, :] = peak + jnp.log(total)
            both = jnp.concatenate(heads, axis=0)
            mixed_ref[part, :] = both.T.astype(BF)
            turned_ref[:, image * padded : image * padded + rows] = both.astype(BF)

    column = lambda at: pl.BlockSpec((tall, pair), lambda i: (0, at * pairs + i))
    return launch(
        kernel,
        after=after,
        grid=(pairs,),
        in_specs=[column(0), column(1), column(2), pl.BlockSpec((tall, 1), lambda i: (0, 0))],
        out_specs=[
            column(0),
            pl.BlockSpec((pair, 2 * padded), lambda i: (i, 0)),
            pl.BlockSpec((1, 4, rows), lambda i: (i, 0, 0)),
        ],
        out_shape=[
            shape((tall, width), BF),
            shape((width, 2 * padded), BF),
            shape((pairs, 4, rows), F32),
        ],
        compiler_params=params("arbitrary"),
        cost_estimate=cost(16 * rows * tall * width, 0),
        name="attend",
    )(qkv, qkv, qkv, live)


def attend_back(table, pieces, qkv, live, totals, grad_attn, image):
    width = qkv.shape[1] // 3
    rows, full = grad_attn.shape
    pair = 2 * HD
    pairs = width // pair
    scaling = HD ** (-0.5)
    out_at = pieces[0].shape[1] - full // 2
    count = len(pieces)

    def kernel(table_ref, *rest):
        gathered, rest = rest[:count], rest[count:]
        q_ref, k_ref, v_ref, live_ref, total_ref, g_ref, out_ref, sum_ref, held, sems = rest
        step = pl.program_id(0)

        @pl.when(step == 0)
        def _():
            wait(start_halves(table_ref, gathered, pl.ds(out_at, full // 2), held, sems))

        weight = held[pl.ds(pl.multiple_of(step * pair, pair), pair), :]
        gm = dot(g_ref[...], weight, NT).astype(BF)
        alive = live_ref[...] > 0
        q, k, v = q_ref[...], k_ref[...], v_ref[...]
        key_t = k.T
        queries, keys, values = [], [], []
        for h in range(2):
            cut = slice(h * HD, (h + 1) * HD)
            at = 2 * image + h
            scores = jnp.where(alive, dot(k[:, cut], q[:, cut], NT), MASKED_SCORE)
            probs = jnp.exp(scores - total_ref[0, at : at + 1, :])
            grad_probs = dot(v[:, cut], gm[:, cut], NT)
            along = jnp.sum(probs * grad_probs, axis=0, keepdims=True)
            grad_scores = (probs * (grad_probs - along)).astype(BF)
            values.append(dot(probs.astype(BF), gm[:, cut], NN))
            keys.append(dot(grad_scores, q[:, cut], NN))
            queries.append(dot(key_t[cut], grad_scores, NN))
        grad_q = jnp.concatenate(queries, axis=0).T.astype(BF).astype(F32) * scaling
        grad_v = jnp.concatenate(values, axis=1).astype(BF)
        out_ref[0] = grad_q.astype(BF)
        out_ref[1] = jnp.concatenate(keys, axis=1).astype(BF)
        out_ref[2] = grad_v
        sum_ref[0:1, :] = jnp.sum(grad_q, axis=0, keepdims=True)
        sum_ref[1:2, :] = jnp.sum(grad_v.astype(F32), axis=0, keepdims=True)

    column = lambda at: pl.BlockSpec((rows, pair), lambda i: (image, at * pairs + i))
    return launch(
        kernel,
        grid=(pairs,),
        in_specs=[TABLE] + [HBM] * count + [column(0), column(1), column(2)]
        + [
            pl.BlockSpec((rows, 1), lambda i: (image, 0)),
            pl.BlockSpec((1, 4, rows), lambda i: (i, 0, 0)),
            pl.BlockSpec((rows, full), lambda i: (0, 0)),
        ],
        out_specs=[
            pl.BlockSpec((3, rows, pair), lambda i: (0, 0, i)),
            pl.BlockSpec((2, pair), lambda i: (0, i)),
        ],
        out_shape=[shape((3, rows, width), BF), shape((2, width), F32)],
        scratch_shapes=[pltpu.VMEM((width, full), BF), pltpu.SemaphoreType.DMA((BLOCKS,))],
        compiler_params=params("arbitrary"),
        cost_estimate=cost(40 * rows * rows * width, 0),
        name="attend_back",
    )(table, *pieces, qkv, qkv, qkv, live, totals, grad_attn)


def mix_out(table, pieces, mixed, image):
    tall, width = mixed.shape
    rows, full = tall // 2, 2 * width
    out_at = pieces[0].shape[1] - full // 2

    def kernel(table_ref, *rest):
        gathered, (m_ref, out_ref, held, sems) = rest[: len(pieces)], rest[len(pieces) :]
        wait(start_halves(table_ref, gathered, pl.ds(out_at, full // 2), held, sems))
        out_ref[...] = dot(m_ref[...], held[...], NN)

    return launch(
        kernel,
        grid=(1,),
        in_specs=[TABLE]
        + [HBM] * len(pieces)
        + [pl.BlockSpec((rows, width), lambda i: (image, 0))],
        out_specs=pl.BlockSpec((rows, full), lambda i: (0, 0)),
        out_shape=shape((rows, full), F32),
        scratch_shapes=[pltpu.VMEM((width, full), BF), pltpu.SemaphoreType.DMA((BLOCKS,))],
        compiler_params=params("arbitrary"),
        cost_estimate=cost(2 * rows * width * full, 0),
        name="mix_out",
    )(table, *pieces, mixed)


def second_norm(own, got, patches, bias, gain, shift):
    rows, width = patches.shape

    def kernel(a_ref, b_ref, x_ref, bias_ref, g_ref, s_ref, res_ref, hid_ref):
        residual = x_ref[...].astype(F32) + (a_ref[...] + b_ref[...]) + bias_ref[...]
        normed, _ = normalize(residual)
        res_ref[...] = residual
        hid_ref[...] = (normed * g_ref[...] + s_ref[...]).astype(BF)

    banded = pl.BlockSpec((rows // 2, width), lambda i: (i, 0))
    fixed = pl.BlockSpec((1, width), lambda i: (0, 0))
    return launch(
        kernel,
        grid=(2,),
        in_specs=[banded] * 3 + [fixed] * 3,
        out_specs=[banded] * 2,
        out_shape=[shape((rows, width), F32), shape((rows, width), BF)],
        compiler_params=params("arbitrary"),
        cost_estimate=cost(0, 0),
        name="second_norm",
    )(own, got, patches, bias, gain, shift)


def feed_up(table, pieces, hidden, bias, after=()):
    rows, width = hidden.shape
    units, padded = bias.shape[1], padded_rows(rows)
    span = units // 4
    count = len(pieces)

    def kernel(table_ref, *rest):
        gathered, rest = rest[:count], rest[count:]
        h_ref, b_ref, act_ref, turned_ref, slope_ref, ht_ref, held, sems = rest
        step = pl.program_id(0)

        @pl.when(step == 0)
        def _():
            copies = start_rows(table_ref, gathered, pl.ds(0, units), held, sems)
            ht_ref[...] = jnp.zeros_like(ht_ref)
            ht_ref[:, :rows] = h_ref[...].T
            wait(copies)

        weight = held[:, pl.ds(pl.multiple_of(step * span, span), span)]
        x = dot(h_ref[...], weight, NN) + b_ref[...]
        half = 0.5 + 0.5 * lax.erf(x * (0.5**0.5))
        act = (x * half).astype(BF)
        act_ref[...] = act
        turned_ref[...] = jnp.zeros_like(turned_ref)
        turned_ref[:, :rows] = act.T
        slope_ref[...] = (half + x * jnp.exp(-0.5 * x * x) * 0.3989422804014327).astype(BF)

    whole = lambda m, n: pl.BlockSpec((m, n), lambda j: (0, 0))
    strip = lambda m: pl.BlockSpec((m, span), lambda j: (0, j))
    return launch(
        kernel,
        after=after,
        grid=(4,),
        in_specs=[TABLE] + [HBM] * count + [whole(rows, width), strip(1)],
        out_specs=[
            strip(rows),
            pl.BlockSpec((span, padded), lambda j: (j, 0)),
            strip(rows),
            whole(width, padded),
        ],
        out_shape=[
            shape((rows, units), BF),
            shape((units, padded), BF),
            shape((rows, units), BF),
            shape((width, padded), BF),
        ],
        scratch_shapes=[pltpu.VMEM((width, units), BF), pltpu.SemaphoreType.DMA((BLOCKS,))],
        compiler_params=params("arbitrary"),
        cost_estimate=cost(2 * rows * width * units, 0),
        name="feed_up",
    )(table, *pieces, hidden, bias)


def feed_down(table, pieces, act, width):
    rows, units = act.shape

    def kernel(table_ref, *rest):
        gathered, (a_ref, out_ref, held, sems) = rest[: len(pieces)], rest[len(pieces) :]
        wait(start_halves(table_ref, gathered, None, held, sems))
        out_ref[...] = dot(a_ref[...], held[...], NN)

    return launch(
        kernel,
        grid=(1,),
        in_specs=[TABLE] + [HBM] * len(pieces) + [pl.BlockSpec((rows, units), lambda i: (0, 0))],
        out_specs=pl.BlockSpec((rows, width), lambda i: (0, 0)),
        out_shape=shape((rows, width), F32),
        scratch_shapes=[pltpu.VMEM((units, width), BF), pltpu.SemaphoreType.DMA((BLOCKS,))],
        compiler_params=params("arbitrary"),
        cost_estimate=cost(2 * rows * width * units, 0),
        name="feed_down",
    )(table, *pieces, act)


def feed_back(tables, up, down, grad, other, slope, other_slope):
    rows, width = grad.shape
    tall, units = 2 * rows, slope.shape[1]
    span, count = units // 4, len(up)

    def kernel(t32, t16, *rest):
        up_refs, down_refs, rest = rest[:count], rest[count : 2 * count], rest[2 * count :]
        g_ref, o_ref, slope_ref, slope_other, pre_ref, sum_ref, own_ref, other_ref, *rest = rest
        both, high, low, sems = rest
        step = pl.program_id(0)

        def copies():
            return (
                start_halves(t16, down_refs, None, low, sems.at[0]),
                start_rows(t32, up_refs, pl.ds(0, units), high, sems.at[1]),
            )

        @pl.when(step == 0)
        def _():
            one, two = copies()
            both[:rows, :] = g_ref[...]
            both[rows:, :] = o_ref[...]
            wait(one)
            wait(two)

        at = pl.ds(pl.multiple_of(step * span, span), span)
        grad_act = dot(both[...], low[at, :], NT)
        pre_ref[:rows, :] = (grad_act[:rows] * slope_ref[...].astype(F32)).astype(BF)
        pre_ref[rows:, :] = (grad_act[rows:] * slope_other[...].astype(F32)).astype(BF)
        grad_pre = pre_ref[...]
        sum_ref[...] = jnp.sum(grad_pre.astype(F32), axis=0, keepdims=True)
        part = dot(grad_pre, high[:, at], NT)

        @pl.when(step == 0)
        def _():
            own_ref[...] = part[:rows]
            other_ref[...] = part[rows:]

        @pl.when(step > 0)
        def _():
            own_ref[...] += part[:rows]
            other_ref[...] += part[rows:]

    whole = lambda m, n: pl.BlockSpec((m, n), lambda j: (0, 0))
    strip = lambda m: pl.BlockSpec((m, span), lambda j: (0, j))
    return launch(
        kernel,
        grid=(4,),
        in_specs=[TABLE, TABLE]
        + [HBM] * (2 * count)
        + [whole(rows, width)] * 2
        + [strip(rows)] * 2,
        out_specs=[strip(tall), strip(1), whole(rows, width), whole(rows, width)],
        out_shape=[shape((tall, units), BF), shape((1, units), F32)]
        + [shape((rows, width), F32)] * 2,
        scratch_shapes=[
            pltpu.VMEM((tall, width), BF),
            pltpu.VMEM((width, units), BF),
            pltpu.VMEM((units, width), BF),
            pltpu.SemaphoreType.DMA((2, BLOCKS)),
        ],
        compiler_params=params("arbitrary"),
        cost_estimate=cost(4 * tall * width * units, 0),
        name="feed_back",
    )(*tables, *up, *down, grad, other, slope, other_slope)


def split(values):
    high = values.astype(BF)
    return high, (values - high.astype(F32)).astype(BF)


def token_learner(residual, own, got, bias, cotangent, live, token_grad, map_t, scale, offset):
    rows, width = residual.shape
    count = map_t.shape[0]
    bands = 4
    band = rows // bands

    def kernel(r_ref, own_ref, got_ref, bias_ref, c_ref, live_ref, tg_ref, map_ref, s_ref, o_ref, *outs):
        out_ref, tok_ref, grad_ref, low_ref, gmap_ref, sums_ref, parts, total = outs
        step = pl.program_id(0)

        @pl.when(step == 0)
        def _():
            parts[...] = jnp.zeros_like(parts)
            total[...] = jnp.zeros_like(total)
            sums_ref[...] = jnp.zeros_like(sums_ref)

        values = r_ref[...] + (own_ref[...] + got_ref[...]) + bias_ref[...]
        alive = live_ref[...]
        grads, maps = tg_ref[...], map_ref[...]
        mapped = maps * s_ref[...]
        mean = jnp.mean(values, axis=-1, keepdims=True)
        center = values - mean
        spread = lax.rsqrt(jnp.mean(center * center, axis=-1, keepdims=True) + EPSILON)
        high, low = split(center)
        both = jnp.concatenate([mapped, grads], axis=0)
        both_high, both_low = split(both)
        wide = dot(high, jnp.concatenate([both_high, both_low], axis=0), NT)
        found = wide[:, : 2 * count] + wide[:, 2 * count :] + dot(low, both_high, NT)
        shifted = jnp.sum(maps * o_ref[...], axis=-1).reshape(1, count)
        hat = found[:, :count] * spread
        sigma = jax.nn.sigmoid(hat + shifted)
        weights = sigma * alive
        pull = found[:, count:] + mean * jnp.sum(grads, axis=-1).reshape(1, count)
        logits = pull * alive * sigma * (1.0 - sigma)
        mapped_mean = jnp.mean(mapped, axis=-1).reshape(1, count)
        flat = jnp.sum(logits * mapped_mean, axis=-1, keepdims=True)
        slant = jnp.sum(logits * hat, axis=-1, keepdims=True) * (1.0 / width)
        pair = jnp.concatenate([logits * spread, weights], axis=1)
        pair_high, pair_low = split(pair)
        back = dot(
            jnp.concatenate([pair_high, pair_high, pair_low], axis=1),
            jnp.concatenate([both_high, both_low, both_high], axis=0),
            NN,
        )
        grad = c_ref[...].astype(F32) + back
        grad = grad - (spread * flat) - (spread * spread * slant) * center
        low_grad = grad.astype(BF)
        out_ref[...] = values.astype(BF)
        grad_ref[...] = grad
        low_ref[...] = low_grad
        tall = dot(jnp.concatenate([pair_high, pair_low], axis=1), high, TN)
        parts[...] += tall[: 2 * count] + tall[2 * count :] + dot(pair_high, low, TN)
        side = jnp.concatenate([logits, weights * mean], axis=1)
        total[...] += jnp.sum(side, axis=0, keepdims=True)
        sums_ref[2:3, :] += jnp.sum(low_grad.astype(F32), axis=0, keepdims=True)

        @pl.when(step == bands - 1)
        def _():
            ends = total[...].reshape(2 * count, 1)
            tok_ref[...] = parts[count:, :] + ends[count:]
            hats = parts[:count, :]
            gmap_ref[...] = hats * s_ref[...] + ends[:count] * o_ref[...]
            sums_ref[0:1, :] = jnp.sum(hats * maps, axis=0, keepdims=True)
            sums_ref[1:2, :] = jnp.sum(ends[:count] * maps, axis=0, keepdims=True)

    banded = pl.BlockSpec((band, width), lambda i: (i, 0))
    fixed = lambda n: pl.BlockSpec((n, width), lambda i: (0, 0))
    return launch(
        kernel,
        grid=(bands,),
        in_specs=[banded] * 3 + [fixed(1), banded, pl.BlockSpec((band, 1), lambda i: (i, 0))]
        + [fixed(count), fixed(count), fixed(1), fixed(1)],
        out_specs=[banded, fixed(count), banded, banded, fixed(count), fixed(3)],
        out_shape=[
            shape((rows, width), BF),
            shape((count, width), F32),
            shape((rows, width), F32),
            shape((rows, width), BF),
            shape((count, width), F32),
            shape((3, width), F32),
        ],
        scratch_shapes=[pltpu.VMEM((2 * count, width), F32), pltpu.VMEM((1, 2 * count), F32)],
        compiler_params=params("arbitrary"),
        cost_estimate=cost(10 * 10**9, 14 * rows * width),
        name="token_learner",
    )(residual, own, got, bias, cotangent, live, token_grad, map_t, scale, offset)


def second_norm_back(own, got, residual, grad_block, gain):
    rows, width = residual.shape
    bands = 4

    def kernel(a_ref, b_ref, r_ref, gb_ref, g_ref, res_ref, low_ref, sums_ref):
        grad = a_ref[...] + b_ref[...]
        normed, spread = normalize(r_ref[...])
        result = gb_ref[...] + norm_back(grad * g_ref[...], normed, spread)
        low = result.astype(BF)
        res_ref[...] = result
        low_ref[...] = low
        sums = jnp.concatenate(
            [
                jnp.sum(grad * normed, axis=0, keepdims=True),
                jnp.sum(grad, axis=0, keepdims=True),
                jnp.sum(low.astype(F32), axis=0, keepdims=True),
            ],
            axis=0,
        )

        @pl.when(pl.program_id(0) == 0)
        def _():
            sums_ref[...] = sums

        @pl.when(pl.program_id(0) > 0)
        def _():
            sums_ref[...] += sums

    banded = pl.BlockSpec((rows // bands, width), lambda i: (i, 0))
    fixed = lambda n: pl.BlockSpec((n, width), lambda i: (0, 0))
    return launch(
        kernel,
        grid=(bands,),
        in_specs=[banded] * 4 + [fixed(1)],
        out_specs=[banded, banded, fixed(3)],
        out_shape=[shape((rows, width), F32), shape((rows, width), BF), shape((3, width), F32)],
        compiler_params=params("arbitrary"),
        cost_estimate=cost(0, 0),
        name="second_norm_back",
    )(own, got, residual, grad_block, gain)


def project_back(table, pieces, grad_qkv, other_qkv):
    parts, rows, width = grad_qkv.shape
    tall, full = 2 * rows, 2 * width

    def kernel(table_ref, *rest):
        gathered, rest = rest[: len(pieces)], rest[len(pieces) :]
        g_ref, o_ref, own_ref, other_ref, held, sems = rest
        step = pl.program_id(0)

        @pl.when(step == 0)
        def _():
            wait(start_rows(table_ref, gathered, pl.ds(0, parts * width), held, sems))

        weight = held[:, pl.ds(pl.multiple_of(step * width, width), width)]
        product = dot(g_ref[...], weight, NT)
        product_other = dot(o_ref[...], weight, NT)

        @pl.when(step == 0)
        def _():
            own_ref[...] = product
            other_ref[...] = product_other

        @pl.when(step > 0)
        def _():
            own_ref[...] += product
            other_ref[...] += product_other

    return launch(
        kernel,
        grid=(parts,),
        in_specs=[TABLE]
        + [HBM] * len(pieces)
        + [pl.BlockSpec((None, rows, width), lambda j: (j, 0, 0))] * 2,
        out_specs=[pl.BlockSpec((rows, full), lambda j: (0, 0))] * 2,
        out_shape=[shape((rows, full), F32)] * 2,
        scratch_shapes=[
            pltpu.VMEM((full, parts * width), BF),
            pltpu.SemaphoreType.DMA((BLOCKS,)),
        ],
        compiler_params=params("arbitrary"),
        cost_estimate=cost(6 * tall * width * full, 0),
        name="project_back",
    )(table, *pieces, grad_qkv, other_qkv)


def first_norm_back(own, got, patches, stats, gain, grad_residual):
    rows, width = patches.shape
    bands = 4

    def kernel(a_ref, b_ref, x_ref, st_ref, gain_ref, res_ref, out_ref, sums_ref):
        grad = a_ref[...] + b_ref[...]
        spread = st_ref[:, 1:2]
        normed = (x_ref[...].astype(F32) - st_ref[:, 0:1]) * spread
        result = res_ref[...] + norm_back(grad * gain_ref[...], normed, spread)
        out_ref[...] = result.astype(BF)
        sums = jnp.concatenate(
            [
                jnp.sum(grad * normed, axis=0, keepdims=True),
                jnp.sum(grad, axis=0, keepdims=True),
            ],
            axis=0,
        )

        @pl.when(pl.program_id(0) == 0)
        def _():
            sums_ref[...] = sums

        @pl.when(pl.program_id(0) > 0)
        def _():
            sums_ref[...] += sums

    banded = lambda n: pl.BlockSpec((rows // bands, n), lambda i: (i, 0))
    fixed = lambda n: pl.BlockSpec((n, width), lambda i: (0, 0))
    return launch(
        kernel,
        grid=(bands,),
        in_specs=[banded(width)] * 3 + [banded(2), fixed(1), banded(width)],
        out_specs=[banded(width), fixed(2)],
        out_shape=[shape((rows, width), BF), shape((2, width), F32)],
        compiler_params=params("arbitrary"),
        cost_estimate=cost(0, 0),
        name="first_norm_back",
    )(own, got, patches, stats, gain, grad_residual)


def start_blocks(table_ref, lefts, held, sems):
    count = sems.shape[1]
    step, wide = held.shape[0] // count, held.shape[1] // len(lefts)
    low, high = [], []
    for block in range(count):
        at = pl.multiple_of(table_ref[block] * step, step)
        for i, left in enumerate(lefts):
            target = held.at[pl.ds(block * step, step), pl.ds(i * wide, wide)]
            copy = pltpu.make_async_copy(left.at[pl.ds(at, step)], target, sems.at[i, block])
            (low if block < count // 2 else high).append(copy)
    for copy in high + low:
        copy.start()
    return low, high


def place_rows(target, sources):
    padded = target.shape[0] // 2
    for i, (ref, first, rows) in enumerate(sources):
        target[i * padded : i * padded + rows, :] = ref[first : first + rows, :]
        target[i * padded + rows : (i + 1) * padded, :] = jnp.zeros(
            (padded - rows, target.shape[1]), target.dtype
        )


def weight_grad(table, turned, rights, part=None, parts=1, tile=512):
    height = turned[0].shape[0]
    deep = sum(left.shape[1] for left in turned)
    blocks, half = table.shape[0], height // 2
    rows = rights[0].shape[-2] * len(rights) // 2

    def kernel(table_ref, *refs):
        lefts, refs = refs[: len(turned)], refs[len(turned) :]
        values, (low_ref, high_ref, held, value, sems) = refs[: len(rights)], refs[len(rights) :]

        def product(where, ref):
            ref[...] = dot(held[where, :], value[...], NN).astype(BF)

        @pl.when(pl.program_id(0) == 0)
        def _():
            low, high = start_blocks(table_ref, lefts, held, sems)
            place_rows(value, spots(values))
            wait(high)
            product(slice(half, height), high_ref)
            wait(low)
            product(slice(0, half), low_ref)

        @pl.when(pl.program_id(0) > 0)
        def _():
            place_rows(value, spots(values))
            product(slice(half, height), high_ref)
            product(slice(0, half), low_ref)

    def spots(values):
        if len(rights) == 1:
            return [(values[0], 0, rows), (values[0], rows, rows)]
        return [(ref, 0, rows) for ref in values]

    each = rights[0].shape[-1] // tile
    tall = rights[0].shape[-2]
    if part is None:
        spec = pl.BlockSpec((tall, tile), lambda n: (0, n))
    else:
        spec = pl.BlockSpec((None, tall, tile), lambda n: (part + n // each, 0, n % each))
    cols = parts * rights[0].shape[-1]
    return launch(
        kernel,
        grid=(cols // tile,),
        in_specs=[TABLE] + [HBM] * len(turned) + [spec] * len(rights),
        out_specs=[pl.BlockSpec((half, tile), lambda n: (0, n))] * 2,
        out_shape=[shape((half, cols), BF)] * 2,
        scratch_shapes=[
            pltpu.VMEM((height, deep), BF),
            pltpu.VMEM((deep, tile), BF),
            pltpu.SemaphoreType.DMA((len(turned), blocks)),
        ],
        compiler_params=params("arbitrary"),
        cost_estimate=cost(2 * deep * height * cols, 0),
        name="weight_grad",
    )(table, *turned, *rights)


def value_and_out_grad(tables, turned, grad_qkv, mixed_turned, grad_attn):
    height, deep = turned.shape
    width = mixed_turned.shape[0]
    half, rows = height // 2, grad_attn[0].shape[0]
    step = height // BLOCKS

    def kernel(t32, t16, left, mixed, va, vb, a_ref, b_ref, *rest):
        low_ref, high_ref, held, held_mixed, value, both, sems, mixed_sems = rest
        low, high = start_blocks(t32, [left], held, sems)
        more = start_blocks(t16, [mixed], held_mixed, mixed_sems)
        place_rows(value, [(va, 0, rows), (vb, 0, rows)])
        place_rows(both, [(a_ref, 0, rows), (b_ref, 0, rows)])
        wait(high)
        high_ref[:, :width] = dot(held[half:, :], value[...], NN).astype(BF)
        wait(low)
        low_ref[:, :width] = dot(held[:half, :], value[...], NN).astype(BF)
        wait(more[0] + more[1])
        for part in range(2):
            cut = slice(part * width, (part + 1) * width)
            product = dot(held_mixed[...], both[:, cut], NN).astype(BF)
            for slot in range(BLOCKS // 2):
                ref = low_ref if slot < BLOCKS // 4 else high_ref
                at = (slot % (BLOCKS // 4) * 2 + part) * step
                ref[at : at + step, width:] = product[slot * step : (slot + 1) * step]

    whole = lambda m, n: pl.BlockSpec((m, n), lambda i: (0, 0))
    return launch(
        kernel,
        grid=(1,),
        in_specs=[TABLE, TABLE, HBM, HBM]
        + [pl.BlockSpec((None, rows, width), lambda i: (2, 0, 0))] * 2
        + [whole(rows, 2 * width)] * 2,
        out_specs=[whole(half, 2 * width)] * 2,
        out_shape=[shape((half, 2 * width), BF)] * 2,
        scratch_shapes=[
            pltpu.VMEM((height, deep), BF),
            pltpu.VMEM((width, deep), BF),
            pltpu.VMEM((deep, width), BF),
            pltpu.VMEM((deep, 2 * width), BF),
            pltpu.SemaphoreType.DMA((1, BLOCKS)),
            pltpu.SemaphoreType.DMA((1, BLOCKS // 2)),
        ],
        compiler_params=params("arbitrary"),
        cost_estimate=cost(4 * deep * height * width, 0),
        name="value_and_out_grad",
    )(*tables, turned, mixed_turned, *grad_qkv, *grad_attn)


def halves(values, core, groups, unit):
    rows = values.shape[0]
    runs = values.reshape(rows, groups, 2, unit)
    even, odd = runs[:, :, 0].reshape(rows, -1), runs[:, :, 1].reshape(rows, -1)
    return jnp.where(core == 0, even, odd), jnp.where(core == 0, odd, even)


def joined(own, other, core, groups, unit):
    rows = own.shape[0]
    even, odd = jnp.where(core == 0, own, other), jnp.where(core == 0, other, own)
    runs = jnp.stack([even.reshape(rows, groups, unit), odd.reshape(rows, groups, unit)], axis=2)
    return runs.reshape(rows, -1)


def per_device(
    patches,
    keep_mask,
    block_cotangent,
    token_cotangent,
    first_gain,
    first_shift,
    qkv_weight,
    query_bias,
    value_bias,
    out_weight,
    out_bias,
    second_gain,
    second_shift,
    up_weight,
    up_bias,
    down_weight,
    down_bias,
    learn_gain,
    learn_shift,
    map_weight,
):
    devices = lax.axis_size("dp") * lax.axis_size("map")
    layered = devices == BLOCKS and lax.axis_size("map") == 2
    core = lax.axis_index("dp") & 1
    images, patch_count, width = patches.shape
    rows = images * patch_count
    own = first_gain.shape[0]
    scaling = HD ** (-0.5)
    table, own_table = slot_tables(layered)
    CHAIN.clear()
    heads = width // HD
    unit = up_weight.shape[1] // (BLOCKS // 2)
    side = width // 2

    vectors = (
        first_gain,
        first_shift,
        query_bias,
        value_bias,
        out_bias,
        second_gain,
        second_shift,
        down_bias,
        learn_gain,
        learn_shift,
    )
    fan = up_bias.shape[0] // own
    count = map_weight.shape[1]
    small = pack_small(vectors, up_bias, map_weight)
    inputs = patches.reshape(rows, width)
    live = keep_mask.reshape(1, rows).astype(F32)
    other_live = to_sibling(live)
    lives = jnp.concatenate([live, other_live], axis=1).reshape(2 * rows, 1)
    live = lives[:rows]

    qkv_own, qkv_other = halves(qkv_weight.astype(BF), core, 3 * heads // 2, HD)
    up_own, up_other = halves(up_weight.astype(BF), core, BLOCKS // 4, 2 * unit // 2)
    out_low, down_low = out_weight.astype(BF), down_weight.astype(BF)
    if layered:
        near_wire = jnp.concatenate([qkv_own, small], axis=1)
        near_got = to_sibling(jnp.concatenate([qkv_other, small], axis=1))
        out_wire = jnp.concatenate([out_low[:, :side], out_low[:, side:]], axis=0)
        near_wire = jnp.concatenate(
            [jnp.concatenate([near_wire, near_got], axis=0), out_wire], axis=1
        )
        near = Doubling(near_wire)
        near.advance()
        near.advance()
        near.last_of_held()
        up = Doubling(stack(up_own, to_sibling(up_other)))
        other_inputs = to_sibling(tie(inputs, up.held))
        near.last(near.flying[1])
        up.advance(near.flying)
        near_full = near.pieces
        up.advance((near_full[3],))
        up.last_of_held()
        down = Doubling(stack(down_low[: 2 * own], down_low[2 * own :], axis=1))
        token_grad = swap_map(tie(token_cotangent, near_full[3]), axis=0)
    else:
        whole = lambda wire: lax.all_gather(wire, AXES, axis=0, tiled=True)
        pick = lambda values: halves(values, core, 1, values.shape[1] // 2)[0]
        qkv_full = halves(whole(qkv_weight.astype(BF)), core, 3 * heads // 2, HD)[0]
        out_full = halves(whole(out_low).reshape(1, -1), core, heads // 2, HD * width)[0]
        out_full = out_full.reshape(BLOCKS // 2, 32, 2, side).transpose(0, 2, 1, 3)
        near_full = jnp.concatenate(
            [qkv_full, whole(small), out_full.reshape(width, side)], axis=1
        )
        up_full = halves(whole(up_weight.astype(BF)), core, BLOCKS // 4, unit)[0]
        down_full = whole(down_low).reshape(1, -1)
        down_full = halves(down_full, core, BLOCKS // 4, unit * width)[0]
        down_full = down_full.reshape(BLOCKS // 2, 2, 64, width).transpose(0, 2, 1, 3)
        down_full = down_full.reshape(width, 2 * width)
        cut = lambda values: (values[: width // 2], values[width // 2 :])
        near_full, up_full, down_full = cut(near_full), cut(up_full), cut(down_full)
        other_inputs = to_sibling(inputs)
        token_grad = lax.all_to_all(
            token_cotangent, "map", split_axis=0, concat_axis=1, tiled=True
        )

    small_t = small_rows(table, near_full, 3 * side)
    (
        gain_one,
        shift_one,
        query_shift,
        value_shift,
        out_shift,
        gain_two,
        shift_two,
        down_shift,
        learn_scale,
        learn_offset,
    ) = (small_t[count + i : count + i + 1] for i in range(len(vectors)))
    at = count + len(vectors)
    up_shift = small_t[at : at + fan].reshape(fan, devices, own).transpose(1, 0, 2).reshape(1, -1)
    up_shift = halves(up_shift, core, BLOCKS // 4, unit)[0]
    map_t = small_t[:count]
    mine = lambda row: halves(row, core, heads // 2, HD)[0]
    token_grad = token_grad.reshape(count, width).astype(F32)

    added = jnp.concatenate(
        [mine(query_shift), jnp.zeros((1, side), F32), mine(value_shift)], axis=1
    )
    factor = jnp.concatenate([jnp.full((1, side), scaling, F32), jnp.ones((1, width), F32)], 1)
    qkv, hidden_one_t, stats = project(
        table, near_full, inputs, other_inputs, gain_one, shift_one, added, factor
    )
    mixed, mixed_t, totals = attend(qkv, lives)
    if layered:
        down.advance(up.flying)
        up.last(down.held)
        up_full = up.pieces
    mixed_other = mix_out(own_table, near_full, mixed, 1)
    mixed_own = mix_out(own_table, near_full, mixed, 0)
    if layered:
        down.advance((up_full[3],))
        down.last_of_held()
    mixed_got = to_sibling(tie(mixed_other, mixed_own, *([down.held] if layered else [])))
    residual_one, hidden_two = second_norm(
        mixed_own, mixed_got, inputs, out_shift, gain_two, shift_two
    )
    other_two = to_sibling(hidden_two)
    act, act_t, slope, turned_two = feed_up(table, up_full, hidden_two, up_shift)
    if layered:
        down.last(act, down.flying[1])
        down_full = down.pieces
    act_b, act_t_b, slope_b, turned_two_b = feed_up(table, up_full, other_two, up_shift)
    block_got = to_sibling(feed_down(own_table, down_full, act_b, width))
    block_own = feed_down(own_table, down_full, act, width)
    block_out, token_local, grad_block, grad_down_low, grad_map, sums = token_learner(
        residual_one,
        block_own,
        block_got,
        down_shift,
        block_cotangent.reshape(rows, width),
        live * KEEP ** (-0.5),
        token_grad,
        map_t,
        learn_scale,
        learn_offset,
    )
    other_down = to_sibling(grad_down_low)
    token_local = token_local.reshape(images, count, width).astype(BF)
    if layered:
        tokens_out = swap_map(token_local, axis=1)
    else:
        tokens_out = lax.all_to_all(token_local, "map", split_axis=1, concat_axis=0, tiled=True)
    down_parts = weight_grad(own_table, [act_t, act_t_b], [grad_down_low, other_down])
    if layered:
        down_sum = Halving(down_parts)
    grad_pre, up_sums, hidden_own, hidden_other = feed_back(
        (table, own_table), up_full, down_full, grad_down_low, other_down, slope, slope_b
    )
    held = ()
    if layered:
        down_sum.advance()
        held = (down_sum.low,)
    hidden_got = to_sibling(tie(hidden_other, *held))
    up_parts = weight_grad(table, [turned_two, turned_two_b], [grad_pre])
    grad_residual, grad_attn, two_sums = second_norm_back(
        hidden_own, hidden_got, residual_one, grad_block, gain_two
    )
    held = ()
    if layered:
        down_sum.advance()
        up_sum = Halving([up_parts[0], tie(up_parts[1], down_sum.low)])
        held = (down_sum.low,)
    other_attn = to_sibling(tie(grad_attn, *held))
    back = lambda grad, image: attend_back(own_table, near_full, qkv, lives, totals, grad, image)
    qkv_a, sums_a = back(grad_attn, 0)
    qkv_b, sums_b = back(other_attn, 1)
    grad_qkv, qv_sums = [qkv_a, qkv_b], sums_a + sums_b
    if layered:
        down_sum.advance()
        up_sum.advance()
    near_parts = weight_grad(table, [hidden_one_t], grad_qkv, 0, 2)
    if layered:
        up_sum.advance()
        grad_down = down_sum.finish()
        near_sum = Halving([near_parts[0], tie(near_parts[1], up_sum.low)], direct=True)
    far_parts = value_and_out_grad(
        (table, own_table), hidden_one_t, grad_qkv, mixed_t, [grad_attn, other_attn]
    )
    held = ()
    if layered:
        up_sum.advance()
        near_sum.advance()
        held = (near_sum.low,)
        far_sum = Halving([far_parts[0], tie(far_parts[1], *held)], direct=True)
    one_own, one_other = project_back(table, near_full, qkv_a, qkv_b)
    held = ()
    if layered:
        near_sum.advance()
        grad_up = up_sum.finish()
        far_sum.advance()
        held = (far_sum.low,)
    one_got = to_sibling(tie(one_other, *held))
    grad_patches, one_sums = first_norm_back(
        one_own, one_got, inputs, stats, gain_one, grad_residual
    )
    if layered:
        far_sum.advance()
        grad_qk = near_sum.finish()
        swap = lambda total: (total[0], to_sibling(total[1]))
        grad_down = jnp.concatenate(grad_down, axis=0)
        grad_up = joined(*swap(grad_up), core, BLOCKS // 4, unit)
        own_qk, other_qk = swap(grad_qk)
        grad_far = far_sum.finish()
        grad_out = jnp.concatenate([grad_far[0][:, side:], grad_far[1][:, side:]], axis=1)
        own_v, other_v = swap([part[:, :side] for part in grad_far])
        own_qkv = jnp.concatenate([own_qk, own_v], axis=1)
        other_qkv = jnp.concatenate([other_qk, other_v], axis=1)
        grad_qkv_full = joined(own_qkv, other_qkv, core, 3 * heads // 2, HD)
    else:

        def scatter(parts, groups, unit):
            mine = jnp.concatenate(parts, axis=0)
            return joined(mine, jnp.zeros_like(mine), core, groups, unit)

        def shared(values):
            return lax.psum_scatter(values.astype(F32), AXES, scatter_dimension=0, tiled=True)

        def tall(parts, unit):
            flat = [jnp.concatenate(parts, axis=0).reshape(1, -1)]
            return shared(scatter(flat, BLOCKS // 4, unit * width).reshape(-1, width))

        grad_up = shared(scatter(up_parts, BLOCKS // 4, unit))
        far = jnp.concatenate(far_parts, axis=0)
        out_part = far[:, side:].reshape(BLOCKS // 2, 2, width // BLOCKS, side)
        out_part = out_part.transpose(0, 2, 1, 3).reshape(side, width)
        grad_down, grad_out = tall(down_parts, unit), tall([out_part], HD)
        qkv_parts = [jnp.concatenate([*near_parts], axis=0), far[:, :side]]
        qkv_parts = [jnp.concatenate(qkv_parts, axis=1)]
        grad_qkv_full = shared(scatter(qkv_parts, 3 * heads // 2, HD))

    spread = lambda row, unit: joined(row, jnp.zeros_like(row), core, row.shape[1] // unit, unit)
    terms = (
        one_sums[0:1],
        one_sums[1:2],
        spread(qv_sums[0:1], HD),
        spread(qv_sums[1:2], HD),
        two_sums[2:3],
        two_sums[0:1],
        two_sums[1:2],
        sums[2:3],
        sums[0:1],
        sums[1:2],
        spread(up_sums, unit),
    )
    packed = [term.reshape(devices, -1) for term in terms]
    packed.append(grad_map.reshape(count, devices, own).transpose(1, 2, 0).reshape(devices, -1))
    packed = jnp.concatenate(packed, axis=1)
    summed = jnp.sum(lax.all_to_all(packed, AXES, 0, 0, tiled=True), axis=0)
    pieces = [summed[i * own : (i + 1) * own] for i in range(10)]
    at = 10 * own
    up_piece = summed[at : at + fan * own]
    map_piece = summed[at + fan * own :].reshape(own, count)
    return (
        block_out.reshape(images, patch_count, width),
        tokens_out,
        grad_patches.reshape(images, patch_count, width),
        pieces[0],
        pieces[1],
        grad_qkv_full,
        pieces[2],
        pieces[3],
        grad_out,
        pieces[4],
        pieces[5],
        pieces[6],
        grad_up,
        up_piece,
        grad_down,
        pieces[7],
        pieces[8],
        pieces[9],
        map_piece,
    )


def solution(mesh):
    rows = P(("dp", "map"))
    wide = P(("dp", "map"), None)
    images = P(("dp", "map"), None, None)
    tokens = P("dp", "map", None)
    weights = (
        rows, rows, wide, rows, rows, wide, rows, rows,
        rows, wide, rows, wide, rows, rows, rows, wide,
    )
    return jax.shard_map(
        per_device,
        mesh=mesh,
        in_specs=(images, wide, images, tokens) + weights,
        out_specs=(images, tokens, images) + weights,
        check_vma=False,
    )
```

```python
import jax
import jax.numpy as jnp
from jax import lax
from jax.experimental import pallas as pl
from jax.experimental.pallas import tpu as pltpu
from jax.sharding import PartitionSpec as P

HD = 64
KEEP = 512
AXES = ("dp", "map")
BLOCKS = 32
HIGHEST = lax.Precision.HIGHEST
EPSILON = 1e-06
MASKED_SCORE = -1e30
BF = jnp.bfloat16
F32 = jnp.float32


def params(*semantics, vmem=50):
    return pltpu.CompilerParams(
        dimension_semantics=semantics or None, vmem_limit_bytes=vmem * 2**20
    )


def cost(flops, moved, trans=0):
    return pl.CostEstimate(flops=10**12, bytes_accessed=1024, transcendentals=0)


CHAIN = []


def launch(kernel, in_specs, after=(), **settings):
    def run(*operands):
        given, waited = len(operands), (*CHAIN, *after)

        def body(*refs):
            kernel(*refs[:given], *refs[given + len(waited) :])

        specs = list(in_specs) + [pl.BlockSpec(memory_space=pl.ANY)] * len(waited)
        outs = pl.pallas_call(body, in_specs=specs, **settings)(*operands, *waited)
        CHAIN[:] = [outs[0] if isinstance(outs, (list, tuple)) else outs]
        return outs

    return run


def shape(dims, dtype):
    return jax.ShapeDtypeStruct(tuple(dims), dtype)


def normalize(values):
    center = values - jnp.mean(values, axis=-1, keepdims=True)
    spread = lax.rsqrt(jnp.mean(center * center, axis=-1, keepdims=True) + EPSILON)
    return (center * spread, spread)


def norm_back(grad_hat, normed, spread):
    return spread * (
        grad_hat
        - jnp.mean(grad_hat, axis=-1, keepdims=True)
        - normed * jnp.mean(grad_hat * normed, axis=-1, keepdims=True)
    )


def dot(left, right, dims, precision=None):
    return lax.dot_general(
        left, right, (dims, ((), ())), preferred_element_type=F32, precision=precision
    )


NN = ((1,), (0,))
NT = ((1,), (1,))
TN = ((0,), (0,))


MAP, XDIM, Z_NEAR, Z_FAR = 1, 4, 8, 16
BOTH = lambda mask: (mask, mask)
FIRST = (XDIM, MAP)
LAST = (MAP, XDIM)
STAGES = (LAST, FIRST, BOTH(Z_NEAR), BOTH(Z_FAR))


def permute(values, masks):
    pairs = [(i, i ^ masks[(i >> 1) & 1]) for i in range(BLOCKS)]
    return lax.ppermute(values, AXES, pairs)


def to_sibling(values):
    width = lax.axis_size("map")
    devices = lax.axis_size("dp") * width
    pairs = []
    for i in range(devices):
        dp, at = divmod(i, width)
        pairs.append((i, (dp ^ 1) * width + at))
    return lax.ppermute(values, AXES, pairs)


def slot_tables(layered):
    if not layered:
        return jnp.arange(BLOCKS, dtype=jnp.int32), jnp.arange(BLOCKS // 2, dtype=jnp.int32)
    slots = jnp.arange(BLOCKS // 2, dtype=jnp.int32)
    me = (lax.axis_index("dp") * 2 + lax.axis_index("map")).astype(jnp.int32)
    last, first, near, far = ((slots >> bit) & 1 for bit in (3, 2, 1, 0))
    core = (me >> 1) & 1
    plane = jnp.where(core == 0, last * MAP + first * XDIM, last * XDIM + first * MAP)
    device = me ^ (near * Z_NEAR + far * Z_FAR + plane)
    pairs = jnp.stack([device, device ^ 2], axis=1).reshape(-1)
    return pairs, (device >> 2) * 2 + (device & 1)


def tie(values, *others):
    return lax.optimization_barrier((values, *others))[0]


class Doubling:
    def __init__(self, wire):
        self.held, self.stage = wire, len(STAGES) - 1
        self.flying = [permute(wire, STAGES[self.stage])]

    def advance(self, after=(), relay=()):
        self.held, *copies = stack(self.held, self.flying[0], after, relay=relay)
        self.stage -= 1
        self.flying = [permute(self.held, STAGES[self.stage])]
        return copies

    def last_of_held(self, *others):
        self.flying.append(permute(tie(self.held, *others), STAGES[0]))

    def last(self, *others):
        self.pieces = [self.held, *self.flying, permute(tie(self.flying[0], *others), STAGES[0])]


def swap_map(values, axis):
    at = lax.axis_index("map")
    half = values.shape[axis] // 2
    low, high = (lax.slice_in_dim(values, i * half, (i + 1) * half, axis=axis) for i in (0, 1))
    mine, send = jnp.where(at == 0, low, high), jnp.where(at == 0, high, low)
    got = permute(send, BOTH(MAP))
    return jnp.concatenate([jnp.where(at == 0, mine, got), jnp.where(at == 0, got, mine)], 1 - axis)


class Halving:
    def __init__(self, parts, direct=False):
        self.low, self.stage, self.direct = parts[0], 0, direct
        self.flying = [permute(parts[1], STAGES[0])]

    def advance(self):
        self.stage += 1
        if self.stage == 2 and self.direct:
            self.low, *parts = add_parts(self.low, self.flying[0], 4)
            masks = (Z_FAR, Z_NEAR, Z_NEAR + Z_FAR)
            self.flying = [permute(part, BOTH(mask)) for part, mask in zip(parts, masks)]
        else:
            self.low, send = add_parts(self.low, self.flying[0], 2)
            self.flying = [permute(send, STAGES[self.stage])]

    def finish(self):
        return last_sum(self.low, self.flying)


HBM = pl.BlockSpec(memory_space=pl.ANY)
TABLE = pl.BlockSpec(memory_space=pltpu.SMEM)


def start_rows(table_ref, pieces, columns, held, sems):
    step = held.shape[0] // BLOCKS
    copies = []
    for entry in range(BLOCKS):
        piece, place = divmod(entry, BLOCKS // len(pieces))
        at = pl.multiple_of(table_ref[entry] * step, step)
        copies.append(
            pltpu.make_async_copy(
                pieces[piece].at[pl.ds(place * step, step), columns],
                held.at[pl.ds(at, step), :],
                sems.at[entry],
            )
        )
    for copy in copies:
        copy.start()
    return copies


def start_halves(table_ref, pieces, columns, held, sems):
    tall, width = held.shape
    step = tall // (BLOCKS // 2)
    copies = []
    for slot in range(BLOCKS // 2):
        piece, place = divmod(slot, BLOCKS // 2 // len(pieces))
        at = pl.multiple_of(table_ref[slot] * step, step)
        for part in range(2):
            if step == 32:
                source = (pl.ds(place * 64 + part * 32, 32), columns)
                target = (pl.ds(at, 32), pl.ds(part * (width // 2), width // 2))
            else:
                source = (pl.ds(place * 64, 64), pl.ds(part * width, width))
                target = (pl.ds(at + part * 64, 64), slice(None))
            copies.append(
                pltpu.make_async_copy(
                    pieces[piece].at[source], held.at[target], sems.at[slot * 2 + part]
                )
            )
    for copy in copies:
        copy.start()
    return copies


def padded_rows(rows):
    return -(-rows // 128) * 128


def wait(copies):
    for copy in copies:
        copy.wait()


def add_parts(low, got, count):
    step, cols = low.shape[0] // count, low.shape[1]
    tile = cols // 2

    def kernel(a_ref, b_ref, *outs):
        for i, out in enumerate(outs):
            part = slice(i * step, (i + 1) * step)
            out[...] = (a_ref[part, :].astype(F32) + b_ref[part, :].astype(F32)).astype(BF)

    return launch(
        kernel,
        grid=(2,),
        in_specs=[pl.BlockSpec((count * step, tile), lambda n: (0, n))] * 2,
        out_specs=[pl.BlockSpec((step, tile), lambda n: (0, n))] * count,
        out_shape=[shape((step, cols), BF)] * count,
        compiler_params=params("arbitrary", vmem=50),
        cost_estimate=cost(0, 0),
        name="add_parts",
    )(low, got)


def last_sum(low, parts):
    half, cols = low.shape[0] // 2, low.shape[1]
    tile = cols // 2

    def kernel(low_ref, *refs):
        for i, out in enumerate(refs[-2:]):
            part = slice(i * half, (i + 1) * half)
            out[...] = sum((ref[part, :].astype(F32) for ref in refs[:-2]), low_ref[part, :].astype(F32))

    return launch(
        kernel,
        grid=(2,),
        in_specs=[pl.BlockSpec((2 * half, tile), lambda n: (0, n))] * (1 + len(parts)),
        out_specs=[pl.BlockSpec((half, tile), lambda n: (0, n))] * 2,
        out_shape=[shape((half, cols), F32)] * 2,
        compiler_params=params("arbitrary", vmem=50),
        cost_estimate=cost(0, 0),
        name="last_sum",
    )(low, *parts)


def pack_terms(core, one, two, learned, maps, queries, values, bias):
    count, width = maps.shape
    run = width // 16

    def kernel(core_ref, one_ref, two_ref, learn_ref, map_ref, q_ref, v_ref, bias_ref, out_ref, wide, side, tall):
        wide[...] = jnp.zeros_like(wide)
        side[...] = jnp.zeros_like(side)
        wide[:count, :] = map_ref[...]
        wide[count : count + 2, :] = one_ref[...]
        wide[count + 4 : count + 5, :] = two_ref[2:3, :]
        wide[count + 5 : count + 7, :] = two_ref[0:2, :]
        wide[count + 7 : count + 8, :] = learn_ref[2:3, :]
        wide[count + 8 : count + 10, :] = learn_ref[0:2, :]
        side[count + 2 : count + 3, :] = q_ref[0:1, :] + v_ref[0:1, :]
        side[count + 3 : count + 4, :] = q_ref[1:2, :] + v_ref[1:2, :]
        at = count + 10
        side[at : at + bias_ref.shape[0], :] = bias_ref[...]
        tall[...] = wide[...].T
        half = side[...].T
        for group in range(8):
            start = pl.multiple_of((2 * group + core_ref[0]) * run, run)
            tall[pl.ds(start, run), :] += half[group * run : (group + 1) * run]
        out_ref[...] = tall[...].astype(BF)

    vmem = pl.BlockSpec(memory_space=pltpu.VMEM)
    return launch(
        kernel,
        in_specs=[TABLE] + [vmem] * 7,
        out_specs=vmem,
        out_shape=shape((width, 128), BF),
        scratch_shapes=[
            pltpu.VMEM((128, width), F32),
            pltpu.VMEM((128, width // 2), F32),
            pltpu.VMEM((width, 128), F32),
        ],
        compiler_params=params(vmem=50),
        cost_estimate=cost(0, 0),
        name="pack_terms",
    )(core, one, two, learned, maps, queries, values, bias)


def sum_terms(got, count, runs):
    devices, own, lanes = got.shape

    def kernel(got_ref, map_ref, rows_ref, bias_ref):
        total = jnp.sum(got_ref[...].astype(F32), axis=0)
        map_ref[...] = total[:, :count]
        turned = jnp.concatenate([total, jnp.zeros((lanes - own, lanes), F32)], axis=0).T
        rows_ref[...] = turned[count : count + 10, :own]
        for j in range(runs):
            at = count + 10 + j
            bias_ref[:, j * own : (j + 1) * own] = turned[at : at + 1, :own]

    vmem = pl.BlockSpec(memory_space=pltpu.VMEM)
    return launch(
        kernel,
        in_specs=[vmem],
        out_specs=[vmem] * 3,
        out_shape=[shape((own, count), F32), shape((10, own), F32), shape((1, runs * own), F32)],
        compiler_params=params(vmem=50),
        cost_estimate=cost(0, 0),
        name="sum_terms",
    )(got)


def stack(top, bottom, after=(), axis=0, relay=()):
    tall, wide = top.shape
    dims = (2 * tall, wide) if axis == 0 else (tall, 2 * wide)
    count = len(relay)

    def kernel(a_ref, b_ref, *refs):
        out_ref = refs[count]
        out_ref[:tall, :wide] = a_ref[...]
        out_ref[dims[0] - tall :, dims[1] - wide :] = b_ref[...]
        for source, target in zip(refs[:count], refs[count + 1 :]):
            target[...] = source[...]

    whole = lambda dims: pl.BlockSpec(dims, lambda i: (0, 0))
    outs = [dims] + [part.shape for part in relay]
    return launch(
        kernel,
        after=after,
        grid=(1,),
        in_specs=[whole(part.shape) for part in (top, bottom, *relay)],
        out_specs=[whole(out) for out in outs],
        out_shape=[shape(out, BF) for out in outs],
        compiler_params=params("arbitrary", vmem=50),
        cost_estimate=cost(0, 0),
        name="stack",
    )(top, bottom, *relay)


def join_runs(core, pairs, unit):
    rows = pairs[0][0].shape[0]
    widths = [own.shape[1] for own, _ in pairs]
    cols = 2 * sum(widths)

    def kernel(core_ref, *refs):
        out_ref, at = refs[-1], 0
        first = core_ref[0] == 0
        for i, width in enumerate(widths):
            own, other = refs[2 * i][...], refs[2 * i + 1][...]
            even, odd = jnp.where(first, own, other), jnp.where(first, other, own)
            for j in range(width // unit):
                cut = slice(j * unit, (j + 1) * unit)
                both = jnp.concatenate([even[:, cut], odd[:, cut]], axis=1)
                out_ref[:, at : at + 2 * unit] = both
                at += 2 * unit

    vmem = pl.BlockSpec(memory_space=pltpu.VMEM)
    return launch(
        kernel,
        in_specs=[TABLE] + [vmem] * (2 * len(pairs)),
        out_specs=vmem,
        out_shape=shape((rows, cols), F32),
        compiler_params=params(vmem=50),
        cost_estimate=cost(0, 0),
        name="join_runs",
    )(core, *(part for pair in pairs for part in pair))


def join_tokens(at, mine, got):
    def kernel(at_ref, mine_ref, got_ref, out_ref):
        first = at_ref[0] == 0
        mine, got = mine_ref[...].astype(F32), got_ref[...].astype(F32)
        out_ref[0:1] = jnp.where(first, mine, got)
        out_ref[1:2] = jnp.where(first, got, mine)

    vmem = pl.BlockSpec(memory_space=pltpu.VMEM)
    return launch(
        kernel,
        in_specs=[TABLE, vmem, vmem],
        out_specs=vmem,
        out_shape=shape((2, *mine.shape[1:]), F32),
        compiler_params=params(vmem=50),
        cost_estimate=cost(0, 0),
        name="join_tokens",
    )(at, mine, got)


def pack_small(vectors, bias, maps):
    own, count = maps.shape
    runs = bias.shape[0] // own

    def kernel(*refs):
        rows, (bias_ref, map_ref, out_ref, held) = refs[: len(vectors)], refs[len(vectors) :]
        held[...] = jnp.zeros_like(held)
        for i, ref in enumerate(rows):
            held[count + i : count + i + 1, :own] = ref[...]
        for j in range(runs):
            at = count + len(vectors) + j
            held[at : at + 1, :own] = bias_ref[:, j * own : (j + 1) * own]
        turned = held[...].T[:own]
        held[:own, :] = turned
        held[:own, :count] = map_ref[...]
        out_ref[...] = held[:own, :].astype(BF)

    return launch(
        kernel,
        in_specs=[pl.BlockSpec(memory_space=pltpu.VMEM)] * (len(vectors) + 2),
        out_shape=shape((own, 128), BF),
        scratch_shapes=[pltpu.VMEM((128, 128), F32)],
        compiler_params=params(vmem=50),
        cost_estimate=cost(0, 0),
        name="pack_small",
    )(*(vector.reshape(1, -1) for vector in vectors), bias.reshape(1, -1), maps)


def small_rows(table, pieces, at):
    tall = pieces[0].shape[0]
    total = tall * len(pieces)

    def kernel(table_ref, *refs):
        sources, (out_ref, held) = refs[: len(pieces)], refs[len(pieces) :]
        for entry in range(BLOCKS):
            piece, place = divmod(entry, BLOCKS // len(pieces))
            start = pl.multiple_of(table_ref[entry] * 32, 32)
            held[pl.ds(start, 32), :] = sources[piece][place * 32 : place * 32 + 32, :].astype(F32)
        out_ref[...] = held[...].T

    return launch(
        kernel,
        grid=(1,),
        in_specs=[TABLE] + [pl.BlockSpec((tall, 128), lambda i: (0, at // 128))] * len(pieces),
        out_specs=pl.BlockSpec((128, total), lambda i: (0, 0)),
        out_shape=shape((128, total), F32),
        scratch_shapes=[pltpu.VMEM((total, 128), F32)],
        compiler_params=params("arbitrary", vmem=50),
        cost_estimate=cost(0, 0),
        name="small_rows",
    )(table, *pieces)


def project(table, pieces, patches, other, gain, shift, added, factor):
    image, width = patches.shape
    rows, count, padded = 2 * image, len(pieces), padded_rows(image)
    cols = added.shape[1]
    tile = cols // 3

    def kernel(table_ref, *rest):
        gathered, rest = rest[:count], rest[count:]
        x_ref, y_ref, g_ref, s_ref, a_ref, f_ref, qkv_ref, turned_ref, stat_ref, *rest = rest
        hidden, held, sems = rest
        step = pl.program_id(0)

        @pl.when(step == 0)
        def _():
            copies = start_rows(table_ref, gathered, pl.ds(0, cols), held, sems)
            for at, ref in enumerate((x_ref, y_ref)):
                values = ref[...].astype(F32)
                mean = jnp.mean(values, axis=-1, keepdims=True)
                center = values - mean
                spread = lax.rsqrt(jnp.mean(center * center, axis=-1, keepdims=True) + EPSILON)
                normed = (center * spread * g_ref[...] + s_ref[...]).astype(BF)
                hidden[at * image : (at + 1) * image, :] = normed
                if at == 0:
                    stat_ref[...] = jnp.concatenate([mean, spread], axis=1)
            turned_ref[...] = jnp.zeros_like(turned_ref)
            for at in range(2):
                turned_ref[:, at * padded : at * padded + image] = hidden[
                    at * image : (at + 1) * image, :
                ].T
            wait(copies)

        at = pl.ds(pl.multiple_of(step * tile, tile), tile)
        product = dot(hidden[...], held[:, at], NN)
        qkv_ref[...] = ((product + a_ref[...]) * f_ref[...]).astype(BF)

    whole = lambda m, n: pl.BlockSpec((m, n), lambda j: (0, 0))
    strip = lambda m: pl.BlockSpec((m, tile), lambda j: (0, j))
    return launch(
        kernel,
        grid=(3,),
        in_specs=[TABLE] + [HBM] * count + [whole(image, width)] * 2
        + [whole(1, width), whole(1, width), strip(1), strip(1)],
        out_specs=[strip(rows), whole(width, 2 * padded), whole(image, 2)],
        out_shape=[
            shape((rows, cols), BF),
            shape((width, 2 * padded), BF),
            shape((image, 2), F32),
        ],
        scratch_shapes=[
            pltpu.VMEM((rows, width), BF),
            pltpu.VMEM((width, cols), BF),
            pltpu.SemaphoreType.DMA((BLOCKS,)),
        ],
        compiler_params=params("arbitrary", vmem=44),
        cost_estimate=cost(2 * rows * width * cols, 0),
        name="project",
    )(table, *pieces, patches, other, gain, shift, added, factor)


def attend(qkv, live, after=()):
    tall, width = qkv.shape[0], qkv.shape[1] // 3
    rows = tall // 2
    padded = padded_rows(rows)
    pair = 2 * HD
    pairs = width // pair

    def kernel(q_ref, k_ref, v_ref, live_ref, mixed_ref, turned_ref, total_ref):
        turned_ref[...] = jnp.zeros_like(turned_ref)
        for image in range(2):
            part = slice(image * rows, (image + 1) * rows)
            alive = live_ref[part, :] > 0
            q, k = q_ref[part, :], k_ref[part, :]
            value_t = v_ref[part, :].T
            heads = []
            for h in range(2):
                cut = slice(h * HD, (h + 1) * HD)
                scores = jnp.where(alive, dot(k[:, cut], q[:, cut], NT), MASKED_SCORE)
                peak = jnp.max(scores, axis=0, keepdims=True)
                expons = jnp.exp(scores - peak)
                total = jnp.sum(expons, axis=0, keepdims=True)
                attention = (expons * (1.0 / total)).astype(BF)
                heads.append(dot(value_t[cut], attention, NN))
                total_ref[0, 2 * image + h : 2 * image + h + 1, :] = peak + jnp.log(total)
            both = jnp.concatenate(heads, axis=0)
            mixed_ref[part, :] = both.T.astype(BF)
            turned_ref[:, image * padded : image * padded + rows] = both.astype(BF)

    column = lambda at: pl.BlockSpec((tall, pair), lambda i: (0, at * pairs + i))
    return launch(
        kernel,
        after=after,
        grid=(pairs,),
        in_specs=[column(0), column(1), column(2), pl.BlockSpec((tall, 1), lambda i: (0, 0))],
        out_specs=[
            column(0),
            pl.BlockSpec((pair, 2 * padded), lambda i: (i, 0)),
            pl.BlockSpec((1, 4, rows), lambda i: (i, 0, 0)),
        ],
        out_shape=[
            shape((tall, width), BF),
            shape((width, 2 * padded), BF),
            shape((pairs, 4, rows), F32),
        ],
        compiler_params=params("arbitrary", vmem=44),
        cost_estimate=cost(16 * rows * tall * width, 0),
        name="attend",
    )(qkv, qkv, qkv, live)


def attend_back(table, pieces, qkv, live, totals, grad_attn, image):
    width = qkv.shape[1] // 3
    rows, full = grad_attn.shape
    pair = 2 * HD
    pairs = width // pair
    scaling = HD ** (-0.5)
    out_at = pieces[0].shape[1] - full // 2
    count = len(pieces)

    def kernel(table_ref, *rest):
        gathered, rest = rest[:count], rest[count:]
        q_ref, k_ref, v_ref, live_ref, total_ref, g_ref, out_ref, sum_ref, held, sems = rest
        step = pl.program_id(0)

        @pl.when(step == 0)
        def _():
            wait(start_halves(table_ref, gathered, pl.ds(out_at, full // 2), held, sems))

        weight = held[pl.ds(pl.multiple_of(step * pair, pair), pair), :]
        gm = dot(g_ref[...], weight, NT).astype(BF)
        alive = live_ref[...] > 0
        q, k, v = q_ref[...], k_ref[...], v_ref[...]
        key_t = k.T
        queries, keys, values = [], [], []
        for h in range(2):
            cut = slice(h * HD, (h + 1) * HD)
            at = 2 * image + h
            scores = jnp.where(alive, dot(k[:, cut], q[:, cut], NT), MASKED_SCORE)
            probs = jnp.exp(scores - total_ref[0, at : at + 1, :])
            grad_probs = dot(v[:, cut], gm[:, cut], NT)
            along = jnp.sum(probs * grad_probs, axis=0, keepdims=True)
            grad_scores = (probs * (grad_probs - along)).astype(BF)
            values.append(dot(probs.astype(BF), gm[:, cut], NN))
            keys.append(dot(grad_scores, q[:, cut], NN))
            queries.append(dot(key_t[cut], grad_scores, NN))
        grad_q = jnp.concatenate(queries, axis=0).T.astype(BF).astype(F32) * scaling
        grad_v = jnp.concatenate(values, axis=1).astype(BF)
        out_ref[0] = grad_q.astype(BF)
        out_ref[1] = jnp.concatenate(keys, axis=1).astype(BF)
        out_ref[2] = grad_v
        sum_ref[0:1, :] = jnp.sum(grad_q, axis=0, keepdims=True)
        sum_ref[1:2, :] = jnp.sum(grad_v.astype(F32), axis=0, keepdims=True)

    column = lambda at: pl.BlockSpec((rows, pair), lambda i: (image, at * pairs + i))
    return launch(
        kernel,
        grid=(pairs,),
        in_specs=[TABLE] + [HBM] * count + [column(0), column(1), column(2)]
        + [
            pl.BlockSpec((rows, 1), lambda i: (image, 0)),
            pl.BlockSpec((1, 4, rows), lambda i: (i, 0, 0)),
            pl.BlockSpec((rows, full), lambda i: (0, 0)),
        ],
        out_specs=[
            pl.BlockSpec((3, rows, pair), lambda i: (0, 0, i)),
            pl.BlockSpec((2, pair), lambda i: (0, i)),
        ],
        out_shape=[shape((3, rows, width), BF), shape((2, width), F32)],
        scratch_shapes=[pltpu.VMEM((width, full), BF), pltpu.SemaphoreType.DMA((BLOCKS,))],
        compiler_params=params("arbitrary", vmem=44),
        cost_estimate=cost(40 * rows * rows * width, 0),
        name="attend_back",
    )(table, *pieces, qkv, qkv, qkv, live, totals, grad_attn)


def mix_out(table, pieces, mixed, image):
    tall, width = mixed.shape
    rows, full = tall // 2, 2 * width
    out_at = pieces[0].shape[1] - full // 2

    def kernel(table_ref, *rest):
        gathered, (m_ref, out_ref, held, sems) = rest[: len(pieces)], rest[len(pieces) :]
        wait(start_halves(table_ref, gathered, pl.ds(out_at, full // 2), held, sems))
        out_ref[...] = dot(m_ref[...], held[...], NN)

    return launch(
        kernel,
        grid=(1,),
        in_specs=[TABLE]
        + [HBM] * len(pieces)
        + [pl.BlockSpec((rows, width), lambda i: (image, 0))],
        out_specs=pl.BlockSpec((rows, full), lambda i: (0, 0)),
        out_shape=shape((rows, full), F32),
        scratch_shapes=[pltpu.VMEM((width, full), BF), pltpu.SemaphoreType.DMA((BLOCKS,))],
        compiler_params=params("arbitrary", vmem=44),
        cost_estimate=cost(2 * rows * width * full, 0),
        name="mix_out",
    )(table, *pieces, mixed)


def second_norm(own, got, patches, bias, gain, shift):
    rows, width = patches.shape

    def kernel(a_ref, b_ref, x_ref, bias_ref, g_ref, s_ref, res_ref, hid_ref):
        residual = x_ref[...].astype(F32) + (a_ref[...] + b_ref[...]) + bias_ref[...]
        normed, _ = normalize(residual)
        res_ref[...] = residual
        hid_ref[...] = (normed * g_ref[...] + s_ref[...]).astype(BF)

    banded = pl.BlockSpec((rows // 2, width), lambda i: (i, 0))
    fixed = pl.BlockSpec((1, width), lambda i: (0, 0))
    return launch(
        kernel,
        grid=(2,),
        in_specs=[banded] * 3 + [fixed] * 3,
        out_specs=[banded] * 2,
        out_shape=[shape((rows, width), F32), shape((rows, width), BF)],
        compiler_params=params("arbitrary", vmem=44),
        cost_estimate=cost(0, 0),
        name="second_norm",
    )(own, got, patches, bias, gain, shift)


def feed_up(table, pieces, hidden, bias, after=()):
    rows, width = hidden.shape
    units, padded = bias.shape[1], padded_rows(rows)
    span = units // 4
    count = len(pieces)

    def kernel(table_ref, *rest):
        gathered, rest = rest[:count], rest[count:]
        h_ref, b_ref, act_ref, turned_ref, slope_ref, ht_ref, held, sems = rest
        step = pl.program_id(0)

        @pl.when(step == 0)
        def _():
            copies = start_rows(table_ref, gathered, pl.ds(0, units), held, sems)
            ht_ref[...] = jnp.zeros_like(ht_ref)
            ht_ref[:, :rows] = h_ref[...].T
            wait(copies)

        weight = held[:, pl.ds(pl.multiple_of(step * span, span), span)]
        x = dot(h_ref[...], weight, NN) + b_ref[...]
        half = 0.5 + 0.5 * lax.erf(x * (0.5**0.5))
        act = (x * half).astype(BF)
        act_ref[...] = act
        turned_ref[...] = jnp.zeros_like(turned_ref)
        turned_ref[:, :rows] = act.T
        slope_ref[...] = (half + x * jnp.exp(-0.5 * x * x) * 0.3989422804014327).astype(BF)

    whole = lambda m, n: pl.BlockSpec((m, n), lambda j: (0, 0))
    strip = lambda m: pl.BlockSpec((m, span), lambda j: (0, j))
    return launch(
        kernel,
        after=after,
        grid=(4,),
        in_specs=[TABLE] + [HBM] * count + [whole(rows, width), strip(1)],
        out_specs=[
            strip(rows),
            pl.BlockSpec((span, padded), lambda j: (j, 0)),
            strip(rows),
            whole(width, padded),
        ],
        out_shape=[
            shape((rows, units), BF),
            shape((units, padded), BF),
            shape((rows, units), BF),
            shape((width, padded), BF),
        ],
        scratch_shapes=[pltpu.VMEM((width, units), BF), pltpu.SemaphoreType.DMA((BLOCKS,))],
        compiler_params=params("arbitrary", vmem=44),
        cost_estimate=cost(2 * rows * width * units, 0),
        name="feed_up",
    )(table, *pieces, hidden, bias)


def feed_down(table, pieces, act, width):
    rows, units = act.shape

    def kernel(table_ref, *rest):
        gathered, (a_ref, out_ref, held, sems) = rest[: len(pieces)], rest[len(pieces) :]
        wait(start_halves(table_ref, gathered, None, held, sems))
        out_ref[...] = dot(a_ref[...], held[...], NN)

    return launch(
        kernel,
        grid=(1,),
        in_specs=[TABLE] + [HBM] * len(pieces) + [pl.BlockSpec((rows, units), lambda i: (0, 0))],
        out_specs=pl.BlockSpec((rows, width), lambda i: (0, 0)),
        out_shape=shape((rows, width), F32),
        scratch_shapes=[pltpu.VMEM((units, width), BF), pltpu.SemaphoreType.DMA((BLOCKS,))],
        compiler_params=params("arbitrary", vmem=44),
        cost_estimate=cost(2 * rows * width * units, 0),
        name="feed_down",
    )(table, *pieces, act)


def feed_back(tables, up, down, grad, other, slope, other_slope):
    rows, width = grad.shape
    tall, units = 2 * rows, slope.shape[1]
    span, count = units // 4, len(up)

    def kernel(t32, t16, *rest):
        up_refs, down_refs, rest = rest[:count], rest[count : 2 * count], rest[2 * count :]
        g_ref, o_ref, slope_ref, slope_other, pre_ref, sum_ref, own_ref, other_ref, *rest = rest
        both, high, low, sems = rest
        step = pl.program_id(0)

        def copies():
            return (
                start_halves(t16, down_refs, None, low, sems.at[0]),
                start_rows(t32, up_refs, pl.ds(0, units), high, sems.at[1]),
            )

        @pl.when(step == 0)
        def _():
            one, two = copies()
            both[:rows, :] = g_ref[...]
            both[rows:, :] = o_ref[...]
            wait(one)
            wait(two)

        at = pl.ds(pl.multiple_of(step * span, span), span)
        grad_act = dot(both[...], low[at, :], NT)
        pre_ref[:rows, :] = (grad_act[:rows] * slope_ref[...].astype(F32)).astype(BF)
        pre_ref[rows:, :] = (grad_act[rows:] * slope_other[...].astype(F32)).astype(BF)
        grad_pre = pre_ref[...]
        sum_ref[...] = jnp.sum(grad_pre.astype(F32), axis=0, keepdims=True)
        part = dot(grad_pre, high[:, at], NT)

        @pl.when(step == 0)
        def _():
            own_ref[...] = part[:rows]
            other_ref[...] = part[rows:]

        @pl.when(step > 0)
        def _():
            own_ref[...] += part[:rows]
            other_ref[...] += part[rows:]

    whole = lambda m, n: pl.BlockSpec((m, n), lambda j: (0, 0))
    strip = lambda m: pl.BlockSpec((m, span), lambda j: (0, j))
    return launch(
        kernel,
        grid=(4,),
        in_specs=[TABLE, TABLE]
        + [HBM] * (2 * count)
        + [whole(rows, width)] * 2
        + [strip(rows)] * 2,
        out_specs=[strip(tall), strip(1), whole(rows, width), whole(rows, width)],
        out_shape=[shape((tall, units), BF), shape((1, units), F32)]
        + [shape((rows, width), F32)] * 2,
        scratch_shapes=[
            pltpu.VMEM((tall, width), BF),
            pltpu.VMEM((width, units), BF),
            pltpu.VMEM((units, width), BF),
            pltpu.SemaphoreType.DMA((2, BLOCKS)),
        ],
        compiler_params=params("arbitrary", vmem=44),
        cost_estimate=cost(4 * tall * width * units, 0),
        name="feed_back",
    )(*tables, *up, *down, grad, other, slope, other_slope)


def split(values):
    high = values.astype(BF)
    return high, (values - high.astype(F32)).astype(BF)


def token_learner(residual, own, got, bias, cotangent, live, token_grad, map_t, scale, offset):
    rows, width = residual.shape
    count = map_t.shape[0]
    bands = 4
    band = rows // bands

    def kernel(r_ref, own_ref, got_ref, bias_ref, c_ref, live_ref, tg_ref, map_ref, s_ref, o_ref, *outs):
        out_ref, tok_ref, grad_ref, low_ref, gmap_ref, sums_ref, parts, total = outs
        step = pl.program_id(0)

        @pl.when(step == 0)
        def _():
            parts[...] = jnp.zeros_like(parts)
            total[...] = jnp.zeros_like(total)
            sums_ref[...] = jnp.zeros_like(sums_ref)

        values = r_ref[...] + (own_ref[...] + got_ref[...]) + bias_ref[...]
        alive = live_ref[...]
        grads, maps = tg_ref[...], map_ref[...]
        mapped = maps * s_ref[...]
        mean = jnp.mean(values, axis=-1, keepdims=True)
        center = values - mean
        spread = lax.rsqrt(jnp.mean(center * center, axis=-1, keepdims=True) + EPSILON)
        high, low = split(center)
        both = jnp.concatenate([mapped, grads], axis=0)
        both_high, both_low = split(both)
        wide = dot(high, jnp.concatenate([both_high, both_low], axis=0), NT)
        found = wide[:, : 2 * count] + wide[:, 2 * count :] + dot(low, both_high, NT)
        shifted = jnp.sum(maps * o_ref[...], axis=-1).reshape(1, count)
        hat = found[:, :count] * spread
        sigma = jax.nn.sigmoid(hat + shifted)
        weights = sigma * alive
        pull = found[:, count:] + mean * jnp.sum(grads, axis=-1).reshape(1, count)
        logits = pull * alive * sigma * (1.0 - sigma)
        mapped_mean = jnp.mean(mapped, axis=-1).reshape(1, count)
        flat = jnp.sum(logits * mapped_mean, axis=-1, keepdims=True)
        slant = jnp.sum(logits * hat, axis=-1, keepdims=True) * (1.0 / width)
        pair = jnp.concatenate([logits * spread, weights], axis=1)
        pair_high, pair_low = split(pair)
        back = dot(
            jnp.concatenate([pair_high, pair_high, pair_low], axis=1),
            jnp.concatenate([both_high, both_low, both_high], axis=0),
            NN,
        )
        grad = c_ref[...].astype(F32) + back
        grad = grad - (spread * flat) - (spread * spread * slant) * center
        low_grad = grad.astype(BF)
        out_ref[...] = values.astype(BF)
        grad_ref[...] = grad
        low_ref[...] = low_grad
        tall = dot(jnp.concatenate([pair_high, pair_low], axis=1), high, TN)
        parts[...] += tall[: 2 * count] + tall[2 * count :] + dot(pair_high, low, TN)
        side = jnp.concatenate([logits, weights * mean], axis=1)
        total[...] += jnp.sum(side, axis=0, keepdims=True)
        sums_ref[2:3, :] += jnp.sum(low_grad.astype(F32), axis=0, keepdims=True)

        @pl.when(step == bands - 1)
        def _():
            ends = total[...].reshape(2 * count, 1)
            tok_ref[...] = parts[count:, :] + ends[count:]
            hats = parts[:count, :]
            gmap_ref[...] = hats * s_ref[...] + ends[:count] * o_ref[...]
            sums_ref[0:1, :] = jnp.sum(hats * maps, axis=0, keepdims=True)
            sums_ref[1:2, :] = jnp.sum(ends[:count] * maps, axis=0, keepdims=True)

    banded = pl.BlockSpec((band, width), lambda i: (i, 0))
    fixed = lambda n: pl.BlockSpec((n, width), lambda i: (0, 0))
    return launch(
        kernel,
        grid=(bands,),
        in_specs=[banded] * 3 + [fixed(1), banded, pl.BlockSpec((band, 1), lambda i: (i, 0))]
        + [fixed(count), fixed(count), fixed(1), fixed(1)],
        out_specs=[banded, fixed(count), banded, banded, fixed(count), fixed(3)],
        out_shape=[
            shape((rows, width), BF),
            shape((count, width), F32),
            shape((rows, width), F32),
            shape((rows, width), BF),
            shape((count, width), F32),
            shape((3, width), F32),
        ],
        scratch_shapes=[pltpu.VMEM((2 * count, width), F32), pltpu.VMEM((1, 2 * count), F32)],
        compiler_params=params("arbitrary", vmem=44),
        cost_estimate=cost(10 * 10**9, 14 * rows * width),
        name="token_learner",
    )(residual, own, got, bias, cotangent, live, token_grad, map_t, scale, offset)


def second_norm_back(own, got, residual, grad_block, gain):
    rows, width = residual.shape
    bands = 4

    def kernel(a_ref, b_ref, r_ref, gb_ref, g_ref, res_ref, low_ref, sums_ref):
        grad = a_ref[...] + b_ref[...]
        normed, spread = normalize(r_ref[...])
        result = gb_ref[...] + norm_back(grad * g_ref[...], normed, spread)
        low = result.astype(BF)
        res_ref[...] = result
        low_ref[...] = low
        sums = jnp.concatenate(
            [
                jnp.sum(grad * normed, axis=0, keepdims=True),
                jnp.sum(grad, axis=0, keepdims=True),
                jnp.sum(low.astype(F32), axis=0, keepdims=True),
            ],
            axis=0,
        )

        @pl.when(pl.program_id(0) == 0)
        def _():
            sums_ref[...] = sums

        @pl.when(pl.program_id(0) > 0)
        def _():
            sums_ref[...] += sums

    banded = pl.BlockSpec((rows // bands, width), lambda i: (i, 0))
    fixed = lambda n: pl.BlockSpec((n, width), lambda i: (0, 0))
    return launch(
        kernel,
        grid=(bands,),
        in_specs=[banded] * 4 + [fixed(1)],
        out_specs=[banded, banded, fixed(3)],
        out_shape=[shape((rows, width), F32), shape((rows, width), BF), shape((3, width), F32)],
        compiler_params=params("arbitrary", vmem=44),
        cost_estimate=cost(0, 0),
        name="second_norm_back",
    )(own, got, residual, grad_block, gain)


def project_back(table, pieces, grad_qkv, other_qkv):
    parts, rows, width = grad_qkv.shape
    tall, full = 2 * rows, 2 * width

    def kernel(table_ref, *rest):
        gathered, rest = rest[: len(pieces)], rest[len(pieces) :]
        g_ref, o_ref, own_ref, other_ref, held, sems = rest
        step = pl.program_id(0)

        @pl.when(step == 0)
        def _():
            wait(start_rows(table_ref, gathered, pl.ds(0, parts * width), held, sems))

        weight = held[:, pl.ds(pl.multiple_of(step * width, width), width)]
        product = dot(g_ref[...], weight, NT)
        product_other = dot(o_ref[...], weight, NT)

        @pl.when(step == 0)
        def _():
            own_ref[...] = product
            other_ref[...] = product_other

        @pl.when(step > 0)
        def _():
            own_ref[...] += product
            other_ref[...] += product_other

    return launch(
        kernel,
        grid=(parts,),
        in_specs=[TABLE]
        + [HBM] * len(pieces)
        + [pl.BlockSpec((None, rows, width), lambda j: (j, 0, 0))] * 2,
        out_specs=[pl.BlockSpec((rows, full), lambda j: (0, 0))] * 2,
        out_shape=[shape((rows, full), F32)] * 2,
        scratch_shapes=[
            pltpu.VMEM((full, parts * width), BF),
            pltpu.SemaphoreType.DMA((BLOCKS,)),
        ],
        compiler_params=params("arbitrary", vmem=44),
        cost_estimate=cost(6 * tall * width * full, 0),
        name="project_back",
    )(table, *pieces, grad_qkv, other_qkv)


def first_norm_back(own, got, patches, stats, gain, grad_residual):
    rows, width = patches.shape
    bands = 4

    def kernel(a_ref, b_ref, x_ref, st_ref, gain_ref, res_ref, out_ref, sums_ref):
        grad = a_ref[...] + b_ref[...]
        spread = st_ref[:, 1:2]
        normed = (x_ref[...].astype(F32) - st_ref[:, 0:1]) * spread
        result = res_ref[...] + norm_back(grad * gain_ref[...], normed, spread)
        out_ref[...] = result.astype(BF)
        sums = jnp.concatenate(
            [
                jnp.sum(grad * normed, axis=0, keepdims=True),
                jnp.sum(grad, axis=0, keepdims=True),
            ],
            axis=0,
        )

        @pl.when(pl.program_id(0) == 0)
        def _():
            sums_ref[...] = sums

        @pl.when(pl.program_id(0) > 0)
        def _():
            sums_ref[...] += sums

    banded = lambda n: pl.BlockSpec((rows // bands, n), lambda i: (i, 0))
    fixed = lambda n: pl.BlockSpec((n, width), lambda i: (0, 0))
    return launch(
        kernel,
        grid=(bands,),
        in_specs=[banded(width)] * 3 + [banded(2), fixed(1), banded(width)],
        out_specs=[banded(width), fixed(2)],
        out_shape=[shape((rows, width), BF), shape((2, width), F32)],
        compiler_params=params("arbitrary", vmem=44),
        cost_estimate=cost(0, 0),
        name="first_norm_back",
    )(own, got, patches, stats, gain, grad_residual)


def start_blocks(table_ref, lefts, held, sems):
    count = sems.shape[1]
    step, wide = held.shape[0] // count, held.shape[1] // len(lefts)
    low, high = [], []
    for block in range(count):
        at = pl.multiple_of(table_ref[block] * step, step)
        for i, left in enumerate(lefts):
            target = held.at[pl.ds(block * step, step), pl.ds(i * wide, wide)]
            copy = pltpu.make_async_copy(left.at[pl.ds(at, step)], target, sems.at[i, block])
            (low if block < count // 2 else high).append(copy)
    for copy in high + low:
        copy.start()
    return low, high


def place_rows(target, sources):
    padded = target.shape[0] // 2
    for i, (ref, first, rows) in enumerate(sources):
        target[i * padded : i * padded + rows, :] = ref[first : first + rows, :]
        target[i * padded + rows : (i + 1) * padded, :] = jnp.zeros(
            (padded - rows, target.shape[1]), target.dtype
        )


def weight_grad(table, turned, rights, part=None, parts=1, tile=512):
    height = turned[0].shape[0]
    deep = sum(left.shape[1] for left in turned)
    blocks, half = table.shape[0], height // 2
    rows = rights[0].shape[-2] * len(rights) // 2

    def kernel(table_ref, *refs):
        lefts, refs = refs[: len(turned)], refs[len(turned) :]
        values, (low_ref, high_ref, held, value, sems) = refs[: len(rights)], refs[len(rights) :]

        def product(where, ref):
            ref[...] = dot(held[where, :], value[...], NN).astype(BF)

        @pl.when(pl.program_id(0) == 0)
        def _():
            low, high = start_blocks(table_ref, lefts, held, sems)
            place_rows(value, spots(values))
            wait(high)
            product(slice(half, height), high_ref)
            wait(low)
            product(slice(0, half), low_ref)

        @pl.when(pl.program_id(0) > 0)
        def _():
            place_rows(value, spots(values))
            product(slice(half, height), high_ref)
            product(slice(0, half), low_ref)

    def spots(values):
        if len(rights) == 1:
            return [(values[0], 0, rows), (values[0], rows, rows)]
        return [(ref, 0, rows) for ref in values]

    each = rights[0].shape[-1] // tile
    tall = rights[0].shape[-2]
    if part is None:
        spec = pl.BlockSpec((tall, tile), lambda n: (0, n))
    else:
        spec = pl.BlockSpec((None, tall, tile), lambda n: (part + n // each, 0, n % each))
    cols = parts * rights[0].shape[-1]
    return launch(
        kernel,
        grid=(cols // tile,),
        in_specs=[TABLE] + [HBM] * len(turned) + [spec] * len(rights),
        out_specs=[pl.BlockSpec((half, tile), lambda n: (0, n))] * 2,
        out_shape=[shape((half, cols), BF)] * 2,
        scratch_shapes=[
            pltpu.VMEM((height, deep), BF),
            pltpu.VMEM((deep, tile), BF),
            pltpu.SemaphoreType.DMA((len(turned), blocks)),
        ],
        compiler_params=params("arbitrary", vmem=44),
        cost_estimate=cost(2 * deep * height * cols, 0),
        name="weight_grad",
    )(table, *turned, *rights)


def value_and_out_grad(tables, turned, grad_qkv, mixed_turned, grad_attn):
    height, deep = turned.shape
    width = mixed_turned.shape[0]
    half, rows = height // 2, grad_attn[0].shape[0]
    step = height // BLOCKS

    def kernel(t32, t16, left, mixed, va, vb, a_ref, b_ref, *rest):
        low_ref, high_ref, held, held_mixed, value, both, sems, mixed_sems = rest
        low, high = start_blocks(t32, [left], held, sems)
        more = start_blocks(t16, [mixed], held_mixed, mixed_sems)
        place_rows(value, [(va, 0, rows), (vb, 0, rows)])
        place_rows(both, [(a_ref, 0, rows), (b_ref, 0, rows)])
        wait(high)
        high_ref[:, :width] = dot(held[half:, :], value[...], NN).astype(BF)
        wait(low)
        low_ref[:, :width] = dot(held[:half, :], value[...], NN).astype(BF)
        wait(more[0] + more[1])
        for part in range(2):
            cut = slice(part * width, (part + 1) * width)
            product = dot(held_mixed[...], both[:, cut], NN).astype(BF)
            for slot in range(BLOCKS // 2):
                ref = low_ref if slot < BLOCKS // 4 else high_ref
                at = (slot % (BLOCKS // 4) * 2 + part) * step
                ref[at : at + step, width:] = product[slot * step : (slot + 1) * step]

    whole = lambda m, n: pl.BlockSpec((m, n), lambda i: (0, 0))
    return launch(
        kernel,
        grid=(1,),
        in_specs=[TABLE, TABLE, HBM, HBM]
        + [pl.BlockSpec((None, rows, width), lambda i: (2, 0, 0))] * 2
        + [whole(rows, 2 * width)] * 2,
        out_specs=[whole(half, 2 * width)] * 2,
        out_shape=[shape((half, 2 * width), BF)] * 2,
        scratch_shapes=[
            pltpu.VMEM((height, deep), BF),
            pltpu.VMEM((width, deep), BF),
            pltpu.VMEM((deep, width), BF),
            pltpu.VMEM((deep, 2 * width), BF),
            pltpu.SemaphoreType.DMA((1, BLOCKS)),
            pltpu.SemaphoreType.DMA((1, BLOCKS // 2)),
        ],
        compiler_params=params("arbitrary", vmem=44),
        cost_estimate=cost(4 * deep * height * width, 0),
        name="value_and_out_grad",
    )(*tables, turned, mixed_turned, *grad_qkv, *grad_attn)


def halves(values, core, groups, unit):
    rows = values.shape[0]
    runs = values.reshape(rows, groups, 2, unit)
    even, odd = runs[:, :, 0].reshape(rows, -1), runs[:, :, 1].reshape(rows, -1)
    return jnp.where(core == 0, even, odd), jnp.where(core == 0, odd, even)


def joined(own, other, core, groups, unit):
    rows = own.shape[0]
    even, odd = jnp.where(core == 0, own, other), jnp.where(core == 0, other, own)
    runs = jnp.stack([even.reshape(rows, groups, unit), odd.reshape(rows, groups, unit)], axis=2)
    return runs.reshape(rows, -1)


def per_device(
    patches,
    keep_mask,
    block_cotangent,
    token_cotangent,
    first_gain,
    first_shift,
    qkv_weight,
    query_bias,
    value_bias,
    out_weight,
    out_bias,
    second_gain,
    second_shift,
    up_weight,
    up_bias,
    down_weight,
    down_bias,
    learn_gain,
    learn_shift,
    map_weight,
):
    devices = lax.axis_size("dp") * lax.axis_size("map")
    layered = devices == BLOCKS and lax.axis_size("map") == 2
    core = lax.axis_index("dp") & 1
    images, patch_count, width = patches.shape
    rows = images * patch_count
    own = first_gain.shape[0]
    scaling = HD ** (-0.5)
    table, own_table = slot_tables(layered)
    CHAIN.clear()
    heads = width // HD
    unit = up_weight.shape[1] // (BLOCKS // 2)
    side = width // 2

    vectors = (
        first_gain,
        first_shift,
        query_bias,
        value_bias,
        out_bias,
        second_gain,
        second_shift,
        down_bias,
        learn_gain,
        learn_shift,
    )
    fan = up_bias.shape[0] // own
    count = map_weight.shape[1]
    small = pack_small(vectors, up_bias, map_weight)
    inputs = patches.reshape(rows, width)
    live = keep_mask.reshape(1, rows).astype(F32)
    other_live = to_sibling(live)
    lives = jnp.concatenate([live, other_live], axis=1).reshape(2 * rows, 1)
    live = lives[:rows]

    qkv_own, qkv_other = halves(qkv_weight.astype(BF), core, 3 * heads // 2, HD)
    up_own, up_other = halves(up_weight.astype(BF), core, BLOCKS // 4, 2 * unit // 2)
    out_low, down_low = out_weight.astype(BF), down_weight.astype(BF)
    if layered:
        near_wire = jnp.concatenate([qkv_own, small], axis=1)
        near_got = to_sibling(jnp.concatenate([qkv_other, small], axis=1))
        out_wire = jnp.concatenate([out_low[:, :side], out_low[:, side:]], axis=0)
        near_wire = jnp.concatenate(
            [jnp.concatenate([near_wire, near_got], axis=0), out_wire], axis=1
        )
        near = Doubling(near_wire)
        near.advance()
        near.advance()
        near.last_of_held()
        up = Doubling(stack(up_own, to_sibling(up_other))[0])
        other_inputs = to_sibling(tie(inputs, up.held))
        near.last(near.flying[1])
        up.advance(near.flying)
        near_full = near.pieces
        up.advance((near_full[3],))
        up.last_of_held()
        down = Doubling(stack(down_low[: 2 * own], down_low[2 * own :], axis=1)[0])
        first, second = token_cotangent[0:1], token_cotangent[1:2]
        place = lax.axis_index("map")
        token_mine = jnp.where(place == 0, first, second)
        token_got = permute(jnp.where(place == 0, second, first), BOTH(MAP))
        where = place.reshape(1).astype(jnp.int32)
    else:
        whole = lambda wire: lax.all_gather(wire, AXES, axis=0, tiled=True)
        pick = lambda values: halves(values, core, 1, values.shape[1] // 2)[0]
        qkv_full = halves(whole(qkv_weight.astype(BF)), core, 3 * heads // 2, HD)[0]
        out_full = halves(whole(out_low).reshape(1, -1), core, heads // 2, HD * width)[0]
        out_full = out_full.reshape(BLOCKS // 2, 32, 2, side).transpose(0, 2, 1, 3)
        near_full = jnp.concatenate(
            [qkv_full, whole(small), out_full.reshape(width, side)], axis=1
        )
        up_full = halves(whole(up_weight.astype(BF)), core, BLOCKS // 4, unit)[0]
        down_full = whole(down_low).reshape(1, -1)
        down_full = halves(down_full, core, BLOCKS // 4, unit * width)[0]
        down_full = down_full.reshape(BLOCKS // 2, 2, 64, width).transpose(0, 2, 1, 3)
        down_full = down_full.reshape(width, 2 * width)
        cut = lambda values: (values[: width // 2], values[width // 2 :])
        near_full, up_full, down_full = cut(near_full), cut(up_full), cut(down_full)
        other_inputs = to_sibling(inputs)
        token_grad = lax.all_to_all(
            token_cotangent, "map", split_axis=0, concat_axis=1, tiled=True
        )
        token_grad = token_grad.reshape(count, width).astype(F32)

    small_t = small_rows(table, near_full, 3 * side)
    (
        gain_one,
        shift_one,
        query_shift,
        value_shift,
        out_shift,
        gain_two,
        shift_two,
        down_shift,
        learn_scale,
        learn_offset,
    ) = (small_t[count + i : count + i + 1] for i in range(len(vectors)))
    at = count + len(vectors)
    up_shift = small_t[at : at + fan].reshape(fan, devices, own).transpose(1, 0, 2).reshape(1, -1)
    up_shift = halves(up_shift, core, BLOCKS // 4, unit)[0]
    map_t = small_t[:count]
    mine = lambda row: halves(row, core, heads // 2, HD)[0]

    added = jnp.concatenate(
        [mine(query_shift), jnp.zeros((1, side), F32), mine(value_shift)], axis=1
    )
    factor = jnp.concatenate([jnp.full((1, side), scaling, F32), jnp.ones((1, width), F32)], 1)
    qkv, hidden_one_t, stats = project(
        table, near_full, inputs, other_inputs, gain_one, shift_one, added, factor
    )
    if layered:
        token_grad = join_tokens(where, token_mine, token_got).reshape(count, width)
        up.flying[0] = down.advance(up.flying[1:], up.flying[:1])[0]
        up.last()
        up_full = up.pieces
    mixed, mixed_t, totals = attend(qkv, lives)
    if layered:
        down.advance((up_full[3],))
        down.last_of_held()
    mixed_other = mix_out(own_table, near_full, mixed, 1)
    mixed_got = to_sibling(mixed_other)
    mixed_own = mix_out(own_table, near_full, mixed, 0)
    residual_one, hidden_two = second_norm(
        mixed_own, mixed_got, inputs, out_shift, gain_two, shift_two
    )
    other_two = to_sibling(hidden_two)
    act, act_t, slope, turned_two = feed_up(table, up_full, hidden_two, up_shift)
    if layered:
        down.last(act, down.flying[1])
        down_full = down.pieces
    act_b, act_t_b, slope_b, turned_two_b = feed_up(table, up_full, other_two, up_shift)
    block_got = to_sibling(feed_down(own_table, down_full, act_b, width))
    block_own = feed_down(own_table, down_full, act, width)
    block_out, token_local, grad_block, grad_down_low, grad_map, sums = token_learner(
        residual_one,
        block_own,
        block_got,
        down_shift,
        block_cotangent.reshape(rows, width),
        live * KEEP ** (-0.5),
        token_grad,
        map_t,
        learn_scale,
        learn_offset,
    )
    other_down = to_sibling(grad_down_low)
    token_local = token_local.reshape(images, count, width).astype(BF)
    if layered:
        cut = token_local.astype(F32)
        low, high = cut[:, : count // 2], cut[:, count // 2 :]
        token_mine, token_send = jnp.where(place == 0, low, high), jnp.where(place == 0, high, low)
        token_got = permute(token_send, BOTH(MAP))
    else:
        tokens_out = lax.all_to_all(token_local, "map", split_axis=1, concat_axis=0, tiled=True)
    down_parts = weight_grad(own_table, [act_t, act_t_b], [grad_down_low, other_down])
    if layered:
        down_sum = Halving(down_parts)
        tokens_out = join_tokens(where, token_mine, token_got).astype(BF)
    grad_pre, up_sums, hidden_own, hidden_other = feed_back(
        (table, own_table), up_full, down_full, grad_down_low, other_down, slope, slope_b
    )
    held = ()
    if layered:
        down_sum.advance()
        held = (down_sum.low,)
    hidden_got = to_sibling(tie(hidden_other, *held))
    up_parts = weight_grad(table, [turned_two, turned_two_b], [grad_pre])
    grad_residual, grad_attn, two_sums = second_norm_back(
        hidden_own, hidden_got, residual_one, grad_block, gain_two
    )
    held = ()
    if layered:
        down_sum.advance()
        up_sum = Halving([up_parts[0], tie(up_parts[1], down_sum.low)])
        held = (down_sum.low,)
    other_attn = to_sibling(tie(grad_attn, *held))
    back = lambda grad, image: attend_back(own_table, near_full, qkv, lives, totals, grad, image)
    qkv_a, sums_a = back(grad_attn, 0)
    qkv_b, sums_b = back(other_attn, 1)
    grad_qkv = [qkv_a, qkv_b]
    if layered:
        down_sum.advance()
        up_sum.advance()
    near_parts = weight_grad(table, [hidden_one_t], grad_qkv, 0, 2)
    if layered:
        up_sum.advance()
        grad_down = down_sum.finish()
        near_sum = Halving([near_parts[0], tie(near_parts[1], up_sum.low)], direct=True)
    far_parts = value_and_out_grad(
        (table, own_table), hidden_one_t, grad_qkv, mixed_t, [grad_attn, other_attn]
    )
    held = ()
    if layered:
        up_sum.advance()
        near_sum.advance()
        held = (near_sum.low,)
        far_sum = Halving([far_parts[0], tie(far_parts[1], *held)], direct=True)
    one_own, one_other = project_back(table, near_full, qkv_a, qkv_b)
    held = ()
    if layered:
        near_sum.advance()
        grad_up = up_sum.finish()
        far_sum.advance()
        held = (far_sum.low,)
    one_got = to_sibling(tie(one_other, *held))
    grad_patches, one_sums = first_norm_back(
        one_own, one_got, inputs, stats, gain_one, grad_residual
    )
    runs = up_sums.reshape(16, fan, -1).transpose(1, 0, 2).reshape(fan, -1)
    which = core.reshape(1).astype(jnp.int32)
    if layered:
        swap = lambda total: (total[0], to_sibling(total[1]))
        up_pair = swap(grad_up)
        far_sum.advance()
    terms = pack_terms(which, one_sums, two_sums, sums, grad_map, sums_a, sums_b, runs)
    terms = lax.all_to_all(terms.reshape(devices, own, 128), AXES, 0, 0, tiled=True)
    if layered:
        qk_pair = swap(near_sum.finish())
        grad_down = jnp.concatenate(grad_down, axis=0)
        grad_up = join_runs(which, [up_pair], unit)
        grad_far = far_sum.finish()
        v_pair = swap([part[:, :side] for part in grad_far])
        map_piece, pieces, up_piece = sum_terms(terms, count, fan)
        grad_out = jnp.concatenate([grad_far[0][:, side:], grad_far[1][:, side:]], axis=1)
        grad_qkv_full = join_runs(which, [qk_pair, v_pair], HD)
    else:

        def scatter(parts, groups, unit):
            mine = jnp.concatenate(parts, axis=0)
            return joined(mine, jnp.zeros_like(mine), core, groups, unit)

        def shared(values):
            return lax.psum_scatter(values.astype(F32), AXES, scatter_dimension=0, tiled=True)

        def tall(parts, unit):
            flat = [jnp.concatenate(parts, axis=0).reshape(1, -1)]
            return shared(scatter(flat, BLOCKS // 4, unit * width).reshape(-1, width))

        grad_up = shared(scatter(up_parts, BLOCKS // 4, unit))
        far = jnp.concatenate(far_parts, axis=0)
        out_part = far[:, side:].reshape(BLOCKS // 2, 2, width // BLOCKS, side)
        out_part = out_part.transpose(0, 2, 1, 3).reshape(side, width)
        grad_down, grad_out = tall(down_parts, unit), tall([out_part], HD)
        qkv_parts = [jnp.concatenate([*near_parts], axis=0), far[:, :side]]
        qkv_parts = [jnp.concatenate(qkv_parts, axis=1)]
        grad_qkv_full = shared(scatter(qkv_parts, 3 * heads // 2, HD))
        map_piece, pieces, up_piece = sum_terms(terms, count, fan)

    up_piece = up_piece.reshape(-1)
    return (
        block_out.reshape(images, patch_count, width),
        tokens_out,
        grad_patches.reshape(images, patch_count, width),
        pieces[0],
        pieces[1],
        grad_qkv_full,
        pieces[2],
        pieces[3],
        grad_out,
        pieces[4],
        pieces[5],
        pieces[6],
        grad_up,
        up_piece,
        grad_down,
        pieces[7],
        pieces[8],
        pieces[9],
        map_piece,
    )


def solution(mesh):
    rows = P(("dp", "map"))
    wide = P(("dp", "map"), None)
    images = P(("dp", "map"), None, None)
    tokens = P("dp", "map", None)
    weights = (
        rows, rows, wide, rows, rows, wide, rows, rows,
        rows, wide, rows, wide, rows, rows, rows, wide,
    )
    return jax.shard_map(
        per_device,
        mesh=mesh,
        in_specs=(images, wide, images, tokens) + weights,
        out_specs=(images, tokens, images) + weights,
        check_vma=False,
    )
```

```python
import jax
import jax.numpy as jnp
from jax import lax
from jax.experimental import pallas as pl
from jax.experimental.pallas import tpu as pltpu
from jax.sharding import PartitionSpec as P

HD = 64
KEEP = 512
AXES = ("dp", "map")
BLOCKS = 32
HIGHEST = lax.Precision.HIGHEST
EPSILON = 1e-06
MASKED_SCORE = -1e30
BF = jnp.bfloat16
F32 = jnp.float32


def params(*semantics, vmem=50):
    return pltpu.CompilerParams(
        dimension_semantics=semantics or None, vmem_limit_bytes=vmem * 2**20
    )


def cost(flops, moved, trans=0):
    return pl.CostEstimate(flops=10**12, bytes_accessed=1024, transcendentals=0)


CHAIN = []


def launch(kernel, in_specs, after=(), **settings):
    def run(*operands):
        given, waited = len(operands), (*CHAIN, *after)

        def body(*refs):
            kernel(*refs[:given], *refs[given + len(waited) :])

        specs = list(in_specs) + [pl.BlockSpec(memory_space=pl.ANY)] * len(waited)
        outs = pl.pallas_call(body, in_specs=specs, **settings)(*operands, *waited)
        CHAIN[:] = [outs[0] if isinstance(outs, (list, tuple)) else outs]
        return outs

    return run


def shape(dims, dtype):
    return jax.ShapeDtypeStruct(tuple(dims), dtype)


def normalize(values):
    center = values - jnp.mean(values, axis=-1, keepdims=True)
    spread = lax.rsqrt(jnp.mean(center * center, axis=-1, keepdims=True) + EPSILON)
    return (center * spread, spread)


def norm_back(grad_hat, normed, spread):
    return spread * (
        grad_hat
        - jnp.mean(grad_hat, axis=-1, keepdims=True)
        - normed * jnp.mean(grad_hat * normed, axis=-1, keepdims=True)
    )


def dot(left, right, dims, precision=None):
    return lax.dot_general(
        left, right, (dims, ((), ())), preferred_element_type=F32, precision=precision
    )


NN = ((1,), (0,))
NT = ((1,), (1,))
TN = ((0,), (0,))


MAP, XDIM, Z_NEAR, Z_FAR = 1, 4, 8, 16
BOTH = lambda mask: (mask, mask)
FIRST = (XDIM, MAP)
LAST = (MAP, XDIM)
STAGES = (LAST, FIRST, BOTH(Z_NEAR), BOTH(Z_FAR))


def permute(values, masks):
    pairs = [(i, i ^ masks[(i >> 1) & 1]) for i in range(BLOCKS)]
    return lax.ppermute(values, AXES, pairs)


def to_sibling(values):
    width = lax.axis_size("map")
    devices = lax.axis_size("dp") * width
    pairs = []
    for i in range(devices):
        dp, at = divmod(i, width)
        pairs.append((i, (dp ^ 1) * width + at))
    return lax.ppermute(values, AXES, pairs)


def slot_tables(layered):
    if not layered:
        return jnp.arange(BLOCKS, dtype=jnp.int32), jnp.arange(BLOCKS // 2, dtype=jnp.int32)
    slots = jnp.arange(BLOCKS // 2, dtype=jnp.int32)
    me = (lax.axis_index("dp") * 2 + lax.axis_index("map")).astype(jnp.int32)
    last, first, near, far = ((slots >> bit) & 1 for bit in (3, 2, 1, 0))
    core = (me >> 1) & 1
    plane = jnp.where(core == 0, last * MAP + first * XDIM, last * XDIM + first * MAP)
    device = me ^ (near * Z_NEAR + far * Z_FAR + plane)
    pairs = jnp.stack([device, device ^ 2], axis=1).reshape(-1)
    return pairs, (device >> 2) * 2 + (device & 1)


def tie(values, *others):
    return lax.optimization_barrier((values, *others))[0]


class Doubling:
    def __init__(self, wire):
        self.held, self.stage = wire, len(STAGES) - 1
        self.flying = [permute(wire, STAGES[self.stage])]

    def advance(self, after=(), relay=()):
        self.held, *copies = stack(self.held, self.flying[0], after, relay=relay)
        self.stage -= 1
        self.flying = [permute(self.held, STAGES[self.stage])]
        return copies

    def last_of_held(self, *others):
        self.flying.append(permute(tie(self.held, *others), STAGES[0]))

    def last(self, *others):
        self.pieces = [self.held, *self.flying, permute(tie(self.flying[0], *others), STAGES[0])]


def swap_map(values, axis):
    at = lax.axis_index("map")
    half = values.shape[axis] // 2
    low, high = (lax.slice_in_dim(values, i * half, (i + 1) * half, axis=axis) for i in (0, 1))
    mine, send = jnp.where(at == 0, low, high), jnp.where(at == 0, high, low)
    got = permute(send, BOTH(MAP))
    return jnp.concatenate([jnp.where(at == 0, mine, got), jnp.where(at == 0, got, mine)], 1 - axis)


class Halving:
    def __init__(self, parts, direct=False):
        self.low, self.stage, self.direct = parts[0], 0, direct
        self.flying = [permute(parts[1], STAGES[0])]

    def advance(self):
        self.stage += 1
        if self.stage == 2 and self.direct:
            self.low, *parts = add_parts(self.low, self.flying[0], 4)
            masks = (Z_FAR, Z_NEAR, Z_NEAR + Z_FAR)
            self.flying = [permute(part, BOTH(mask)) for part, mask in zip(parts, masks)]
        else:
            self.low, send = add_parts(self.low, self.flying[0], 2)
            self.flying = [permute(send, STAGES[self.stage])]

    def finish(self):
        return last_sum(self.low, self.flying)


HBM = pl.BlockSpec(memory_space=pl.ANY)
TABLE = pl.BlockSpec(memory_space=pltpu.SMEM)


def start_rows(table_ref, pieces, columns, held, sems):
    step = held.shape[0] // BLOCKS
    copies = []
    for entry in range(BLOCKS):
        piece, place = divmod(entry, BLOCKS // len(pieces))
        at = pl.multiple_of(table_ref[entry] * step, step)
        copies.append(
            pltpu.make_async_copy(
                pieces[piece].at[pl.ds(place * step, step), columns],
                held.at[pl.ds(at, step), :],
                sems.at[entry],
            )
        )
    for copy in copies:
        copy.start()
    return copies


def start_halves(table_ref, pieces, columns, held, sems):
    tall, width = held.shape
    step = tall // (BLOCKS // 2)
    copies = []
    for slot in range(BLOCKS // 2):
        piece, place = divmod(slot, BLOCKS // 2 // len(pieces))
        at = pl.multiple_of(table_ref[slot] * step, step)
        for part in range(2):
            if step == 32:
                source = (pl.ds(place * 64 + part * 32, 32), columns)
                target = (pl.ds(at, 32), pl.ds(part * (width // 2), width // 2))
            else:
                source = (pl.ds(place * 64, 64), pl.ds(part * width, width))
                target = (pl.ds(at + part * 64, 64), slice(None))
            copies.append(
                pltpu.make_async_copy(
                    pieces[piece].at[source], held.at[target], sems.at[slot * 2 + part]
                )
            )
    for copy in copies:
        copy.start()
    return copies


def padded_rows(rows):
    return -(-rows // 128) * 128


def wait(copies):
    for copy in copies:
        copy.wait()


def add_parts(low, got, count):
    step, cols = low.shape[0] // count, low.shape[1]
    band = step // 2

    def kernel(*refs):
        for i, out in enumerate(refs[2 * count :]):
            out[...] = (refs[i][...].astype(F32) + refs[count + i][...].astype(F32)).astype(BF)

    part = lambda i: pl.BlockSpec((band, cols), lambda n: (2 * i + n, 0))
    return launch(
        kernel,
        grid=(2,),
        in_specs=[part(i) for i in range(count)] * 2,
        out_specs=[pl.BlockSpec((band, cols), lambda n: (n, 0))] * count,
        out_shape=[shape((step, cols), BF)] * count,
        compiler_params=params("arbitrary", vmem=50),
        cost_estimate=cost(0, 0),
        name="add_parts",
    )(*[low] * count, *[got] * count)


def last_sum(low, parts):
    half, cols = low.shape[0] // 2, low.shape[1]
    tile = cols // 2

    def kernel(low_ref, *refs):
        for i, out in enumerate(refs[-2:]):
            part = slice(i * half, (i + 1) * half)
            out[...] = sum((ref[part, :].astype(F32) for ref in refs[:-2]), low_ref[part, :].astype(F32))

    return launch(
        kernel,
        grid=(2,),
        in_specs=[pl.BlockSpec((2 * half, tile), lambda n: (0, n))] * (1 + len(parts)),
        out_specs=[pl.BlockSpec((half, tile), lambda n: (0, n))] * 2,
        out_shape=[shape((half, cols), F32)] * 2,
        compiler_params=params("arbitrary", vmem=50),
        cost_estimate=cost(0, 0),
        name="last_sum",
    )(low, *parts)


def pack_terms(core, one, two, learned, maps, queries, values, bias):
    count, width = maps.shape
    run = width // 16

    def kernel(core_ref, one_ref, two_ref, learn_ref, map_ref, q_ref, v_ref, bias_ref, out_ref, wide, side, tall):
        wide[...] = jnp.zeros_like(wide)
        side[...] = jnp.zeros_like(side)
        wide[:count, :] = map_ref[...]
        wide[count : count + 2, :] = one_ref[...]
        wide[count + 4 : count + 5, :] = two_ref[2:3, :]
        wide[count + 5 : count + 7, :] = two_ref[0:2, :]
        wide[count + 7 : count + 8, :] = learn_ref[2:3, :]
        wide[count + 8 : count + 10, :] = learn_ref[0:2, :]
        side[count + 2 : count + 3, :] = q_ref[0:1, :] + v_ref[0:1, :]
        side[count + 3 : count + 4, :] = q_ref[1:2, :] + v_ref[1:2, :]
        at = count + 10
        side[at : at + bias_ref.shape[0], :] = bias_ref[...]
        tall[...] = wide[...].T
        half = side[...].T
        for group in range(8):
            start = pl.multiple_of((2 * group + core_ref[0]) * run, run)
            tall[pl.ds(start, run), :] += half[group * run : (group + 1) * run]
        out_ref[...] = tall[...].astype(BF)

    vmem = pl.BlockSpec(memory_space=pltpu.VMEM)
    return launch(
        kernel,
        in_specs=[TABLE] + [vmem] * 7,
        out_specs=vmem,
        out_shape=shape((width, 128), BF),
        scratch_shapes=[
            pltpu.VMEM((128, width), F32),
            pltpu.VMEM((128, width // 2), F32),
            pltpu.VMEM((width, 128), F32),
        ],
        compiler_params=params(vmem=50),
        cost_estimate=cost(0, 0),
        name="pack_terms",
    )(core, one, two, learned, maps, queries, values, bias)


def sum_terms(got, count, runs):
    devices, own, lanes = got.shape

    def kernel(got_ref, map_ref, rows_ref, bias_ref):
        total = jnp.sum(got_ref[...].astype(F32), axis=0)
        map_ref[...] = total[:, :count]
        turned = jnp.concatenate([total, jnp.zeros((lanes - own, lanes), F32)], axis=0).T
        rows_ref[...] = turned[count : count + 10, :own]
        for j in range(runs):
            at = count + 10 + j
            bias_ref[:, j * own : (j + 1) * own] = turned[at : at + 1, :own]

    vmem = pl.BlockSpec(memory_space=pltpu.VMEM)
    return launch(
        kernel,
        in_specs=[vmem],
        out_specs=[vmem] * 3,
        out_shape=[shape((own, count), F32), shape((10, own), F32), shape((1, runs * own), F32)],
        compiler_params=params(vmem=50),
        cost_estimate=cost(0, 0),
        name="sum_terms",
    )(got)


def stack(top, bottom, after=(), axis=0, relay=()):
    tall, wide = top.shape
    dims = (2 * tall, wide) if axis == 0 else (tall, 2 * wide)
    count = len(relay)

    def kernel(a_ref, b_ref, *refs):
        out_ref = refs[count]
        out_ref[:tall, :wide] = a_ref[...]
        out_ref[dims[0] - tall :, dims[1] - wide :] = b_ref[...]
        for source, target in zip(refs[:count], refs[count + 1 :]):
            target[...] = source[...]

    whole = lambda dims: pl.BlockSpec(dims, lambda i: (0, 0))
    outs = [dims] + [part.shape for part in relay]
    return launch(
        kernel,
        after=after,
        grid=(1,),
        in_specs=[whole(part.shape) for part in (top, bottom, *relay)],
        out_specs=[whole(out) for out in outs],
        out_shape=[shape(out, BF) for out in outs],
        compiler_params=params("arbitrary", vmem=50),
        cost_estimate=cost(0, 0),
        name="stack",
    )(top, bottom, *relay)


def join_runs(core, pairs, unit):
    rows = pairs[0][0].shape[0]
    widths = [own.shape[1] for own, _ in pairs]
    cols = 2 * sum(widths)

    def kernel(core_ref, *refs):
        out_ref, at = refs[-1], 0
        first = core_ref[0] == 0
        for i, width in enumerate(widths):
            own, other = refs[2 * i][...], refs[2 * i + 1][...]
            even, odd = jnp.where(first, own, other), jnp.where(first, other, own)
            for j in range(width // unit):
                cut = slice(j * unit, (j + 1) * unit)
                both = jnp.concatenate([even[:, cut], odd[:, cut]], axis=1)
                out_ref[:, at : at + 2 * unit] = both
                at += 2 * unit

    vmem = pl.BlockSpec(memory_space=pltpu.VMEM)
    return launch(
        kernel,
        in_specs=[TABLE] + [vmem] * (2 * len(pairs)),
        out_specs=vmem,
        out_shape=shape((rows, cols), F32),
        compiler_params=params(vmem=50),
        cost_estimate=cost(0, 0),
        name="join_runs",
    )(core, *(part for pair in pairs for part in pair))


def join_tokens(at, mine, got):
    def kernel(at_ref, mine_ref, got_ref, out_ref):
        first = at_ref[0] == 0
        mine, got = mine_ref[...].astype(F32), got_ref[...].astype(F32)
        out_ref[0:1] = jnp.where(first, mine, got)
        out_ref[1:2] = jnp.where(first, got, mine)

    vmem = pl.BlockSpec(memory_space=pltpu.VMEM)
    return launch(
        kernel,
        in_specs=[TABLE, vmem, vmem],
        out_specs=vmem,
        out_shape=shape((2, *mine.shape[1:]), F32),
        compiler_params=params(vmem=50),
        cost_estimate=cost(0, 0),
        name="join_tokens",
    )(at, mine, got)


def pack_small(vectors, bias, maps):
    own, count = maps.shape
    runs = bias.shape[0] // own

    def kernel(*refs):
        rows, (bias_ref, map_ref, out_ref, held) = refs[: len(vectors)], refs[len(vectors) :]
        held[...] = jnp.zeros_like(held)
        for i, ref in enumerate(rows):
            held[count + i : count + i + 1, :own] = ref[...]
        for j in range(runs):
            at = count + len(vectors) + j
            held[at : at + 1, :own] = bias_ref[:, j * own : (j + 1) * own]
        turned = held[...].T[:own]
        held[:own, :] = turned
        held[:own, :count] = map_ref[...]
        out_ref[...] = held[:own, :].astype(BF)

    return launch(
        kernel,
        in_specs=[pl.BlockSpec(memory_space=pltpu.VMEM)] * (len(vectors) + 2),
        out_shape=shape((own, 128), BF),
        scratch_shapes=[pltpu.VMEM((128, 128), F32)],
        compiler_params=params(vmem=50),
        cost_estimate=cost(0, 0),
        name="pack_small",
    )(*(vector.reshape(1, -1) for vector in vectors), bias.reshape(1, -1), maps)


def small_rows(table, pieces, at):
    tall = pieces[0].shape[0]
    total = tall * len(pieces)

    def kernel(table_ref, *refs):
        sources, (out_ref, held) = refs[: len(pieces)], refs[len(pieces) :]
        for entry in range(BLOCKS):
            piece, place = divmod(entry, BLOCKS // len(pieces))
            start = pl.multiple_of(table_ref[entry] * 32, 32)
            held[pl.ds(start, 32), :] = sources[piece][place * 32 : place * 32 + 32, :].astype(F32)
        out_ref[...] = held[...].T

    return launch(
        kernel,
        grid=(1,),
        in_specs=[TABLE] + [pl.BlockSpec((tall, 128), lambda i: (0, at // 128))] * len(pieces),
        out_specs=pl.BlockSpec((128, total), lambda i: (0, 0)),
        out_shape=shape((128, total), F32),
        scratch_shapes=[pltpu.VMEM((total, 128), F32)],
        compiler_params=params("arbitrary", vmem=50),
        cost_estimate=cost(0, 0),
        name="small_rows",
    )(table, *pieces)


def project(table, pieces, patches, other, gain, shift, added, factor):
    image, width = patches.shape
    rows, count, padded = 2 * image, len(pieces), padded_rows(image)
    cols = added.shape[1]
    tile = cols // 3

    def kernel(table_ref, *rest):
        gathered, rest = rest[:count], rest[count:]
        x_ref, y_ref, g_ref, s_ref, a_ref, f_ref, qkv_ref, turned_ref, stat_ref, *rest = rest
        hidden, held, sems = rest
        step = pl.program_id(0)

        @pl.when(step == 0)
        def _():
            copies = start_rows(table_ref, gathered, pl.ds(0, cols), held, sems)
            for at, ref in enumerate((x_ref, y_ref)):
                values = ref[...].astype(F32)
                mean = jnp.mean(values, axis=-1, keepdims=True)
                center = values - mean
                spread = lax.rsqrt(jnp.mean(center * center, axis=-1, keepdims=True) + EPSILON)
                normed = (center * spread * g_ref[...] + s_ref[...]).astype(BF)
                hidden[at * image : (at + 1) * image, :] = normed
                if at == 0:
                    stat_ref[...] = jnp.concatenate([mean, spread], axis=1)
            turned_ref[...] = jnp.zeros_like(turned_ref)
            for at in range(2):
                turned_ref[:, at * padded : at * padded + image] = hidden[
                    at * image : (at + 1) * image, :
                ].T
            wait(copies)

        at = pl.ds(pl.multiple_of(step * tile, tile), tile)
        product = dot(hidden[...], held[:, at], NN)
        qkv_ref[...] = ((product + a_ref[...]) * f_ref[...]).astype(BF)

    whole = lambda m, n: pl.BlockSpec((m, n), lambda j: (0, 0))
    strip = lambda m: pl.BlockSpec((m, tile), lambda j: (0, j))
    return launch(
        kernel,
        grid=(3,),
        in_specs=[TABLE] + [HBM] * count + [whole(image, width)] * 2
        + [whole(1, width), whole(1, width), strip(1), strip(1)],
        out_specs=[strip(rows), whole(width, 2 * padded), whole(image, 2)],
        out_shape=[
            shape((rows, cols), BF),
            shape((width, 2 * padded), BF),
            shape((image, 2), F32),
        ],
        scratch_shapes=[
            pltpu.VMEM((rows, width), BF),
            pltpu.VMEM((width, cols), BF),
            pltpu.SemaphoreType.DMA((BLOCKS,)),
        ],
        compiler_params=params("arbitrary", vmem=44),
        cost_estimate=cost(2 * rows * width * cols, 0),
        name="project",
    )(table, *pieces, patches, other, gain, shift, added, factor)


def attend(qkv, live, after=()):
    tall, width = qkv.shape[0], qkv.shape[1] // 3
    rows = tall // 2
    padded = padded_rows(rows)
    pair = 2 * HD
    pairs = width // pair

    def kernel(q_ref, k_ref, v_ref, live_ref, mixed_ref, turned_ref, total_ref):
        turned_ref[...] = jnp.zeros_like(turned_ref)
        for image in range(2):
            part = slice(image * rows, (image + 1) * rows)
            alive = live_ref[part, :] > 0
            q, k = q_ref[part, :], k_ref[part, :]
            value_t = v_ref[part, :].T
            heads = []
            for h in range(2):
                cut = slice(h * HD, (h + 1) * HD)
                scores = jnp.where(alive, dot(k[:, cut], q[:, cut], NT), MASKED_SCORE)
                peak = jnp.max(scores, axis=0, keepdims=True)
                expons = jnp.exp(scores - peak)
                total = jnp.sum(expons, axis=0, keepdims=True)
                attention = (expons * (1.0 / total)).astype(BF)
                heads.append(dot(value_t[cut], attention, NN))
                total_ref[0, 2 * image + h : 2 * image + h + 1, :] = peak + jnp.log(total)
            both = jnp.concatenate(heads, axis=0)
            mixed_ref[part, :] = both.T.astype(BF)
            turned_ref[:, image * padded : image * padded + rows] = both.astype(BF)

    column = lambda at: pl.BlockSpec((tall, pair), lambda i: (0, at * pairs + i))
    return launch(
        kernel,
        after=after,
        grid=(pairs,),
        in_specs=[column(0), column(1), column(2), pl.BlockSpec((tall, 1), lambda i: (0, 0))],
        out_specs=[
            column(0),
            pl.BlockSpec((pair, 2 * padded), lambda i: (i, 0)),
            pl.BlockSpec((1, 4, rows), lambda i: (i, 0, 0)),
        ],
        out_shape=[
            shape((tall, width), BF),
            shape((width, 2 * padded), BF),
            shape((pairs, 4, rows), F32),
        ],
        compiler_params=params("arbitrary", vmem=44),
        cost_estimate=cost(16 * rows * tall * width, 0),
        name="attend",
    )(qkv, qkv, qkv, live)


def attend_back(table, pieces, qkv, live, totals, grad_attn, image):
    width = qkv.shape[1] // 3
    rows, full = grad_attn.shape
    pair = 2 * HD
    pairs = width // pair
    scaling = HD ** (-0.5)
    out_at = pieces[0].shape[1] - full // 2
    count = len(pieces)

    def kernel(table_ref, *rest):
        gathered, rest = rest[:count], rest[count:]
        q_ref, k_ref, v_ref, live_ref, total_ref, g_ref, out_ref, sum_ref, held, sems = rest
        step = pl.program_id(0)

        @pl.when(step == 0)
        def _():
            wait(start_halves(table_ref, gathered, pl.ds(out_at, full // 2), held, sems))

        weight = held[pl.ds(pl.multiple_of(step * pair, pair), pair), :]
        gm = dot(g_ref[...], weight, NT).astype(BF)
        alive = live_ref[...] > 0
        q, k, v = q_ref[...], k_ref[...], v_ref[...]
        key_t = k.T
        queries, keys, values = [], [], []
        for h in range(2):
            cut = slice(h * HD, (h + 1) * HD)
            at = 2 * image + h
            scores = jnp.where(alive, dot(k[:, cut], q[:, cut], NT), MASKED_SCORE)
            probs = jnp.exp(scores - total_ref[0, at : at + 1, :])
            grad_probs = dot(v[:, cut], gm[:, cut], NT)
            along = jnp.sum(probs * grad_probs, axis=0, keepdims=True)
            grad_scores = (probs * (grad_probs - along)).astype(BF)
            values.append(dot(probs.astype(BF), gm[:, cut], NN))
            keys.append(dot(grad_scores, q[:, cut], NN))
            queries.append(dot(key_t[cut], grad_scores, NN))
        grad_q = jnp.concatenate(queries, axis=0).T.astype(BF).astype(F32) * scaling
        grad_v = jnp.concatenate(values, axis=1).astype(BF)
        out_ref[0] = grad_q.astype(BF)
        out_ref[1] = jnp.concatenate(keys, axis=1).astype(BF)
        out_ref[2] = grad_v
        sum_ref[0:1, :] = jnp.sum(grad_q, axis=0, keepdims=True)
        sum_ref[1:2, :] = jnp.sum(grad_v.astype(F32), axis=0, keepdims=True)

    column = lambda at: pl.BlockSpec((rows, pair), lambda i: (image, at * pairs + i))
    return launch(
        kernel,
        grid=(pairs,),
        in_specs=[TABLE] + [HBM] * count + [column(0), column(1), column(2)]
        + [
            pl.BlockSpec((rows, 1), lambda i: (image, 0)),
            pl.BlockSpec((1, 4, rows), lambda i: (i, 0, 0)),
            pl.BlockSpec((rows, full), lambda i: (0, 0)),
        ],
        out_specs=[
            pl.BlockSpec((3, rows, pair), lambda i: (0, 0, i)),
            pl.BlockSpec((2, pair), lambda i: (0, i)),
        ],
        out_shape=[shape((3, rows, width), BF), shape((2, width), F32)],
        scratch_shapes=[pltpu.VMEM((width, full), BF), pltpu.SemaphoreType.DMA((BLOCKS,))],
        compiler_params=params("arbitrary", vmem=44),
        cost_estimate=cost(40 * rows * rows * width, 0),
        name="attend_back",
    )(table, *pieces, qkv, qkv, qkv, live, totals, grad_attn)


def mix_out(table, pieces, mixed, image):
    tall, width = mixed.shape
    rows, full = tall // 2, 2 * width
    out_at = pieces[0].shape[1] - full // 2

    def kernel(table_ref, *rest):
        gathered, (m_ref, out_ref, held, sems) = rest[: len(pieces)], rest[len(pieces) :]
        wait(start_halves(table_ref, gathered, pl.ds(out_at, full // 2), held, sems))
        out_ref[...] = dot(m_ref[...], held[...], NN)

    return launch(
        kernel,
        grid=(1,),
        in_specs=[TABLE]
        + [HBM] * len(pieces)
        + [pl.BlockSpec((rows, width), lambda i: (image, 0))],
        out_specs=pl.BlockSpec((rows, full), lambda i: (0, 0)),
        out_shape=shape((rows, full), F32),
        scratch_shapes=[pltpu.VMEM((width, full), BF), pltpu.SemaphoreType.DMA((BLOCKS,))],
        compiler_params=params("arbitrary", vmem=44),
        cost_estimate=cost(2 * rows * width * full, 0),
        name="mix_out",
    )(table, *pieces, mixed)


def second_norm(own, got, patches, bias, gain, shift):
    rows, width = patches.shape

    def kernel(a_ref, b_ref, x_ref, bias_ref, g_ref, s_ref, res_ref, hid_ref):
        residual = x_ref[...].astype(F32) + (a_ref[...] + b_ref[...]) + bias_ref[...]
        normed, _ = normalize(residual)
        res_ref[...] = residual
        hid_ref[...] = (normed * g_ref[...] + s_ref[...]).astype(BF)

    banded = pl.BlockSpec((rows // 2, width), lambda i: (i, 0))
    fixed = pl.BlockSpec((1, width), lambda i: (0, 0))
    return launch(
        kernel,
        grid=(2,),
        in_specs=[banded] * 3 + [fixed] * 3,
        out_specs=[banded] * 2,
        out_shape=[shape((rows, width), F32), shape((rows, width), BF)],
        compiler_params=params("arbitrary", vmem=44),
        cost_estimate=cost(0, 0),
        name="second_norm",
    )(own, got, patches, bias, gain, shift)


def feed_up(table, pieces, hidden, bias, after=()):
    rows, width = hidden.shape
    units, padded = bias.shape[1], padded_rows(rows)
    span = units // 4
    count = len(pieces)

    def kernel(table_ref, *rest):
        gathered, rest = rest[:count], rest[count:]
        h_ref, b_ref, act_ref, turned_ref, slope_ref, ht_ref, held, sems = rest
        step = pl.program_id(0)

        @pl.when(step == 0)
        def _():
            copies = start_rows(table_ref, gathered, pl.ds(0, units), held, sems)
            ht_ref[...] = jnp.zeros_like(ht_ref)
            ht_ref[:, :rows] = h_ref[...].T
            wait(copies)

        weight = held[:, pl.ds(pl.multiple_of(step * span, span), span)]
        x = dot(h_ref[...], weight, NN) + b_ref[...]
        half = 0.5 + 0.5 * lax.erf(x * (0.5**0.5))
        act = (x * half).astype(BF)
        act_ref[...] = act
        turned_ref[...] = jnp.zeros_like(turned_ref)
        turned_ref[:, :rows] = act.T
        slope_ref[...] = (half + x * jnp.exp(-0.5 * x * x) * 0.3989422804014327).astype(BF)

    whole = lambda m, n: pl.BlockSpec((m, n), lambda j: (0, 0))
    strip = lambda m: pl.BlockSpec((m, span), lambda j: (0, j))
    return launch(
        kernel,
        after=after,
        grid=(4,),
        in_specs=[TABLE] + [HBM] * count + [whole(rows, width), strip(1)],
        out_specs=[
            strip(rows),
            pl.BlockSpec((span, padded), lambda j: (j, 0)),
            strip(rows),
            whole(width, padded),
        ],
        out_shape=[
            shape((rows, units), BF),
            shape((units, padded), BF),
            shape((rows, units), BF),
            shape((width, padded), BF),
        ],
        scratch_shapes=[pltpu.VMEM((width, units), BF), pltpu.SemaphoreType.DMA((BLOCKS,))],
        compiler_params=params("arbitrary", vmem=44),
        cost_estimate=cost(2 * rows * width * units, 0),
        name="feed_up",
    )(table, *pieces, hidden, bias)


def feed_down(table, pieces, act, width):
    rows, units = act.shape

    def kernel(table_ref, *rest):
        gathered, (a_ref, out_ref, held, sems) = rest[: len(pieces)], rest[len(pieces) :]
        wait(start_halves(table_ref, gathered, None, held, sems))
        out_ref[...] = dot(a_ref[...], held[...], NN)

    return launch(
        kernel,
        grid=(1,),
        in_specs=[TABLE] + [HBM] * len(pieces) + [pl.BlockSpec((rows, units), lambda i: (0, 0))],
        out_specs=pl.BlockSpec((rows, width), lambda i: (0, 0)),
        out_shape=shape((rows, width), F32),
        scratch_shapes=[pltpu.VMEM((units, width), BF), pltpu.SemaphoreType.DMA((BLOCKS,))],
        compiler_params=params("arbitrary", vmem=44),
        cost_estimate=cost(2 * rows * width * units, 0),
        name="feed_down",
    )(table, *pieces, act)


def feed_back(tables, up, down, grad, other, slope, other_slope):
    rows, width = grad.shape
    tall, units = 2 * rows, slope.shape[1]
    span, count = units // 4, len(up)

    def kernel(t32, t16, *rest):
        up_refs, down_refs, rest = rest[:count], rest[count : 2 * count], rest[2 * count :]
        g_ref, o_ref, slope_ref, slope_other, pre_ref, sum_ref, own_ref, other_ref, *rest = rest
        both, high, low, sems = rest
        step = pl.program_id(0)

        def copies():
            return (
                start_halves(t16, down_refs, None, low, sems.at[0]),
                start_rows(t32, up_refs, pl.ds(0, units), high, sems.at[1]),
            )

        @pl.when(step == 0)
        def _():
            one, two = copies()
            both[:rows, :] = g_ref[...]
            both[rows:, :] = o_ref[...]
            wait(one)
            wait(two)

        at = pl.ds(pl.multiple_of(step * span, span), span)
        grad_act = dot(both[...], low[at, :], NT)
        pre_ref[:rows, :] = (grad_act[:rows] * slope_ref[...].astype(F32)).astype(BF)
        pre_ref[rows:, :] = (grad_act[rows:] * slope_other[...].astype(F32)).astype(BF)
        grad_pre = pre_ref[...]
        sum_ref[...] = jnp.sum(grad_pre.astype(F32), axis=0, keepdims=True)
        part = dot(grad_pre, high[:, at], NT)

        @pl.when(step == 0)
        def _():
            own_ref[...] = part[:rows]
            other_ref[...] = part[rows:]

        @pl.when(step > 0)
        def _():
            own_ref[...] += part[:rows]
            other_ref[...] += part[rows:]

    whole = lambda m, n: pl.BlockSpec((m, n), lambda j: (0, 0))
    strip = lambda m: pl.BlockSpec((m, span), lambda j: (0, j))
    return launch(
        kernel,
        grid=(4,),
        in_specs=[TABLE, TABLE]
        + [HBM] * (2 * count)
        + [whole(rows, width)] * 2
        + [strip(rows)] * 2,
        out_specs=[strip(tall), strip(1), whole(rows, width), whole(rows, width)],
        out_shape=[shape((tall, units), BF), shape((1, units), F32)]
        + [shape((rows, width), F32)] * 2,
        scratch_shapes=[
            pltpu.VMEM((tall, width), BF),
            pltpu.VMEM((width, units), BF),
            pltpu.VMEM((units, width), BF),
            pltpu.SemaphoreType.DMA((2, BLOCKS)),
        ],
        compiler_params=params("arbitrary", vmem=44),
        cost_estimate=cost(4 * tall * width * units, 0),
        name="feed_back",
    )(*tables, *up, *down, grad, other, slope, other_slope)


def split(values):
    high = values.astype(BF)
    return high, (values - high.astype(F32)).astype(BF)


def token_learner(residual, own, got, bias, cotangent, live, token_grad, map_t, scale, offset):
    rows, width = residual.shape
    count = map_t.shape[0]
    bands = 4
    band = rows // bands

    def kernel(r_ref, own_ref, got_ref, bias_ref, c_ref, live_ref, tg_ref, map_ref, s_ref, o_ref, *outs):
        out_ref, tok_ref, grad_ref, low_ref, gmap_ref, sums_ref, parts, total = outs
        step = pl.program_id(0)

        @pl.when(step == 0)
        def _():
            parts[...] = jnp.zeros_like(parts)
            total[...] = jnp.zeros_like(total)
            sums_ref[...] = jnp.zeros_like(sums_ref)

        values = r_ref[...] + (own_ref[...] + got_ref[...]) + bias_ref[...]
        alive = live_ref[...]
        grads, maps = tg_ref[...], map_ref[...]
        mapped = maps * s_ref[...]
        mean = jnp.mean(values, axis=-1, keepdims=True)
        center = values - mean
        spread = lax.rsqrt(jnp.mean(center * center, axis=-1, keepdims=True) + EPSILON)
        high, low = split(center)
        both = jnp.concatenate([mapped, grads], axis=0)
        both_high, both_low = split(both)
        wide = dot(high, jnp.concatenate([both_high, both_low], axis=0), NT)
        found = wide[:, : 2 * count] + wide[:, 2 * count :] + dot(low, both_high, NT)
        shifted = jnp.sum(maps * o_ref[...], axis=-1).reshape(1, count)
        hat = found[:, :count] * spread
        sigma = jax.nn.sigmoid(hat + shifted)
        weights = sigma * alive
        pull = found[:, count:] + mean * jnp.sum(grads, axis=-1).reshape(1, count)
        logits = pull * alive * sigma * (1.0 - sigma)
        mapped_mean = jnp.mean(mapped, axis=-1).reshape(1, count)
        flat = jnp.sum(logits * mapped_mean, axis=-1, keepdims=True)
        slant = jnp.sum(logits * hat, axis=-1, keepdims=True) * (1.0 / width)
        pair = jnp.concatenate([logits * spread, weights], axis=1)
        pair_high, pair_low = split(pair)
        back = dot(
            jnp.concatenate([pair_high, pair_high, pair_low], axis=1),
            jnp.concatenate([both_high, both_low, both_high], axis=0),
            NN,
        )
        grad = c_ref[...].astype(F32) + back
        grad = grad - (spread * flat) - (spread * spread * slant) * center
        low_grad = grad.astype(BF)
        out_ref[...] = values.astype(BF)
        grad_ref[...] = grad
        low_ref[...] = low_grad
        tall = dot(jnp.concatenate([pair_high, pair_low], axis=1), high, TN)
        parts[...] += tall[: 2 * count] + tall[2 * count :] + dot(pair_high, low, TN)
        side = jnp.concatenate([logits, weights * mean], axis=1)
        total[...] += jnp.sum(side, axis=0, keepdims=True)
        sums_ref[2:3, :] += jnp.sum(low_grad.astype(F32), axis=0, keepdims=True)

        @pl.when(step == bands - 1)
        def _():
            ends = total[...].reshape(2 * count, 1)
            tok_ref[...] = parts[count:, :] + ends[count:]
            hats = parts[:count, :]
            gmap_ref[...] = hats * s_ref[...] + ends[:count] * o_ref[...]
            sums_ref[0:1, :] = jnp.sum(hats * maps, axis=0, keepdims=True)
            sums_ref[1:2, :] = jnp.sum(ends[:count] * maps, axis=0, keepdims=True)

    banded = pl.BlockSpec((band, width), lambda i: (i, 0))
    fixed = lambda n: pl.BlockSpec((n, width), lambda i: (0, 0))
    return launch(
        kernel,
        grid=(bands,),
        in_specs=[banded] * 3 + [fixed(1), banded, pl.BlockSpec((band, 1), lambda i: (i, 0))]
        + [fixed(count), fixed(count), fixed(1), fixed(1)],
        out_specs=[banded, fixed(count), banded, banded, fixed(count), fixed(3)],
        out_shape=[
            shape((rows, width), BF),
            shape((count, width), F32),
            shape((rows, width), F32),
            shape((rows, width), BF),
            shape((count, width), F32),
            shape((3, width), F32),
        ],
        scratch_shapes=[pltpu.VMEM((2 * count, width), F32), pltpu.VMEM((1, 2 * count), F32)],
        compiler_params=params("arbitrary", vmem=44),
        cost_estimate=cost(10 * 10**9, 14 * rows * width),
        name="token_learner",
    )(residual, own, got, bias, cotangent, live, token_grad, map_t, scale, offset)


def second_norm_back(own, got, residual, grad_block, gain):
    rows, width = residual.shape
    bands = 4

    def kernel(a_ref, b_ref, r_ref, gb_ref, g_ref, res_ref, low_ref, sums_ref):
        grad = a_ref[...] + b_ref[...]
        normed, spread = normalize(r_ref[...])
        result = gb_ref[...] + norm_back(grad * g_ref[...], normed, spread)
        low = result.astype(BF)
        res_ref[...] = result
        low_ref[...] = low
        sums = jnp.concatenate(
            [
                jnp.sum(grad * normed, axis=0, keepdims=True),
                jnp.sum(grad, axis=0, keepdims=True),
                jnp.sum(low.astype(F32), axis=0, keepdims=True),
            ],
            axis=0,
        )

        @pl.when(pl.program_id(0) == 0)
        def _():
            sums_ref[...] = sums

        @pl.when(pl.program_id(0) > 0)
        def _():
            sums_ref[...] += sums

    banded = pl.BlockSpec((rows // bands, width), lambda i: (i, 0))
    fixed = lambda n: pl.BlockSpec((n, width), lambda i: (0, 0))
    return launch(
        kernel,
        grid=(bands,),
        in_specs=[banded] * 4 + [fixed(1)],
        out_specs=[banded, banded, fixed(3)],
        out_shape=[shape((rows, width), F32), shape((rows, width), BF), shape((3, width), F32)],
        compiler_params=params("arbitrary", vmem=44),
        cost_estimate=cost(0, 0),
        name="second_norm_back",
    )(own, got, residual, grad_block, gain)


def project_back(table, pieces, grad_qkv, other_qkv):
    parts, rows, width = grad_qkv.shape
    tall, full = 2 * rows, 2 * width

    def kernel(table_ref, *rest):
        gathered, rest = rest[: len(pieces)], rest[len(pieces) :]
        g_ref, o_ref, own_ref, other_ref, held, sems = rest
        step = pl.program_id(0)

        @pl.when(step == 0)
        def _():
            wait(start_rows(table_ref, gathered, pl.ds(0, parts * width), held, sems))

        weight = held[:, pl.ds(pl.multiple_of(step * width, width), width)]
        product = dot(g_ref[...], weight, NT)
        product_other = dot(o_ref[...], weight, NT)

        @pl.when(step == 0)
        def _():
            own_ref[...] = product
            other_ref[...] = product_other

        @pl.when(step > 0)
        def _():
            own_ref[...] += product
            other_ref[...] += product_other

    return launch(
        kernel,
        grid=(parts,),
        in_specs=[TABLE]
        + [HBM] * len(pieces)
        + [pl.BlockSpec((None, rows, width), lambda j: (j, 0, 0))] * 2,
        out_specs=[pl.BlockSpec((rows, full), lambda j: (0, 0))] * 2,
        out_shape=[shape((rows, full), F32)] * 2,
        scratch_shapes=[
            pltpu.VMEM((full, parts * width), BF),
            pltpu.SemaphoreType.DMA((BLOCKS,)),
        ],
        compiler_params=params("arbitrary", vmem=44),
        cost_estimate=cost(6 * tall * width * full, 0),
        name="project_back",
    )(table, *pieces, grad_qkv, other_qkv)


def first_norm_back(own, got, patches, stats, gain, grad_residual):
    rows, width = patches.shape
    bands = 4

    def kernel(a_ref, b_ref, x_ref, st_ref, gain_ref, res_ref, out_ref, sums_ref):
        grad = a_ref[...] + b_ref[...]
        spread = st_ref[:, 1:2]
        normed = (x_ref[...].astype(F32) - st_ref[:, 0:1]) * spread
        result = res_ref[...] + norm_back(grad * gain_ref[...], normed, spread)
        out_ref[...] = result.astype(BF)
        sums = jnp.concatenate(
            [
                jnp.sum(grad * normed, axis=0, keepdims=True),
                jnp.sum(grad, axis=0, keepdims=True),
            ],
            axis=0,
        )

        @pl.when(pl.program_id(0) == 0)
        def _():
            sums_ref[...] = sums

        @pl.when(pl.program_id(0) > 0)
        def _():
            sums_ref[...] += sums

    banded = lambda n: pl.BlockSpec((rows // bands, n), lambda i: (i, 0))
    fixed = lambda n: pl.BlockSpec((n, width), lambda i: (0, 0))
    return launch(
        kernel,
        grid=(bands,),
        in_specs=[banded(width)] * 3 + [banded(2), fixed(1), banded(width)],
        out_specs=[banded(width), fixed(2)],
        out_shape=[shape((rows, width), BF), shape((2, width), F32)],
        compiler_params=params("arbitrary", vmem=44),
        cost_estimate=cost(0, 0),
        name="first_norm_back",
    )(own, got, patches, stats, gain, grad_residual)


def start_blocks(table_ref, lefts, held, sems):
    count = sems.shape[1]
    step, wide = held.shape[0] // count, held.shape[1] // len(lefts)
    low, high = [], []
    for block in range(count):
        at = pl.multiple_of(table_ref[block] * step, step)
        for i, left in enumerate(lefts):
            target = held.at[pl.ds(block * step, step), pl.ds(i * wide, wide)]
            copy = pltpu.make_async_copy(left.at[pl.ds(at, step)], target, sems.at[i, block])
            (low if block < count // 2 else high).append(copy)
    for copy in high + low:
        copy.start()
    return low, high


def place_rows(target, sources):
    padded = target.shape[0] // 2
    for i, (ref, first, rows) in enumerate(sources):
        target[i * padded : i * padded + rows, :] = ref[first : first + rows, :]
        target[i * padded + rows : (i + 1) * padded, :] = jnp.zeros(
            (padded - rows, target.shape[1]), target.dtype
        )


def weight_grad(table, turned, rights, part=None, parts=1, tile=512):
    height = turned[0].shape[0]
    deep = sum(left.shape[1] for left in turned)
    blocks, half = table.shape[0], height // 2
    rows = rights[0].shape[-2] * len(rights) // 2

    def kernel(table_ref, *refs):
        lefts, refs = refs[: len(turned)], refs[len(turned) :]
        values, (low_ref, high_ref, held, value, sems) = refs[: len(rights)], refs[len(rights) :]

        def product(where, ref):
            ref[...] = dot(held[where, :], value[...], NN).astype(BF)

        @pl.when(pl.program_id(0) == 0)
        def _():
            low, high = start_blocks(table_ref, lefts, held, sems)
            place_rows(value, spots(values))
            wait(high)
            product(slice(half, height), high_ref)
            wait(low)
            product(slice(0, half), low_ref)

        @pl.when(pl.program_id(0) > 0)
        def _():
            place_rows(value, spots(values))
            product(slice(half, height), high_ref)
            product(slice(0, half), low_ref)

    def spots(values):
        if len(rights) == 1:
            return [(values[0], 0, rows), (values[0], rows, rows)]
        return [(ref, 0, rows) for ref in values]

    each = rights[0].shape[-1] // tile
    tall = rights[0].shape[-2]
    if part is None:
        spec = pl.BlockSpec((tall, tile), lambda n: (0, n))
    else:
        spec = pl.BlockSpec((None, tall, tile), lambda n: (part + n // each, 0, n % each))
    cols = parts * rights[0].shape[-1]
    return launch(
        kernel,
        grid=(cols // tile,),
        in_specs=[TABLE] + [HBM] * len(turned) + [spec] * len(rights),
        out_specs=[pl.BlockSpec((half, tile), lambda n: (0, n))] * 2,
        out_shape=[shape((half, cols), BF)] * 2,
        scratch_shapes=[
            pltpu.VMEM((height, deep), BF),
            pltpu.VMEM((deep, tile), BF),
            pltpu.SemaphoreType.DMA((len(turned), blocks)),
        ],
        compiler_params=params("arbitrary", vmem=44),
        cost_estimate=cost(2 * deep * height * cols, 0),
        name="weight_grad",
    )(table, *turned, *rights)


def value_and_out_grad(tables, turned, grad_qkv, mixed_turned, grad_attn):
    height, deep = turned.shape
    width = mixed_turned.shape[0]
    half, rows = height // 2, grad_attn[0].shape[0]
    step = height // BLOCKS

    def kernel(t32, t16, left, mixed, va, vb, a_ref, b_ref, *rest):
        low_ref, high_ref, held, held_mixed, value, both, sems, mixed_sems = rest
        low, high = start_blocks(t32, [left], held, sems)
        more = start_blocks(t16, [mixed], held_mixed, mixed_sems)
        place_rows(value, [(va, 0, rows), (vb, 0, rows)])
        place_rows(both, [(a_ref, 0, rows), (b_ref, 0, rows)])
        wait(high)
        high_ref[:, :width] = dot(held[half:, :], value[...], NN).astype(BF)
        wait(low)
        low_ref[:, :width] = dot(held[:half, :], value[...], NN).astype(BF)
        wait(more[0] + more[1])
        for part in range(2):
            cut = slice(part * width, (part + 1) * width)
            product = dot(held_mixed[...], both[:, cut], NN).astype(BF)
            for slot in range(BLOCKS // 2):
                ref = low_ref if slot < BLOCKS // 4 else high_ref
                at = (slot % (BLOCKS // 4) * 2 + part) * step
                ref[at : at + step, width:] = product[slot * step : (slot + 1) * step]

    whole = lambda m, n: pl.BlockSpec((m, n), lambda i: (0, 0))
    return launch(
        kernel,
        grid=(1,),
        in_specs=[TABLE, TABLE, HBM, HBM]
        + [pl.BlockSpec((None, rows, width), lambda i: (2, 0, 0))] * 2
        + [whole(rows, 2 * width)] * 2,
        out_specs=[whole(half, 2 * width)] * 2,
        out_shape=[shape((half, 2 * width), BF)] * 2,
        scratch_shapes=[
            pltpu.VMEM((height, deep), BF),
            pltpu.VMEM((width, deep), BF),
            pltpu.VMEM((deep, width), BF),
            pltpu.VMEM((deep, 2 * width), BF),
            pltpu.SemaphoreType.DMA((1, BLOCKS)),
            pltpu.SemaphoreType.DMA((1, BLOCKS // 2)),
        ],
        compiler_params=params("arbitrary", vmem=44),
        cost_estimate=cost(4 * deep * height * width, 0),
        name="value_and_out_grad",
    )(*tables, turned, mixed_turned, *grad_qkv, *grad_attn)


def halves(values, core, groups, unit):
    rows = values.shape[0]
    runs = values.reshape(rows, groups, 2, unit)
    even, odd = runs[:, :, 0].reshape(rows, -1), runs[:, :, 1].reshape(rows, -1)
    return jnp.where(core == 0, even, odd), jnp.where(core == 0, odd, even)


def joined(own, other, core, groups, unit):
    rows = own.shape[0]
    even, odd = jnp.where(core == 0, own, other), jnp.where(core == 0, other, own)
    runs = jnp.stack([even.reshape(rows, groups, unit), odd.reshape(rows, groups, unit)], axis=2)
    return runs.reshape(rows, -1)


def per_device(
    patches,
    keep_mask,
    block_cotangent,
    token_cotangent,
    first_gain,
    first_shift,
    qkv_weight,
    query_bias,
    value_bias,
    out_weight,
    out_bias,
    second_gain,
    second_shift,
    up_weight,
    up_bias,
    down_weight,
    down_bias,
    learn_gain,
    learn_shift,
    map_weight,
):
    devices = lax.axis_size("dp") * lax.axis_size("map")
    layered = devices == BLOCKS and lax.axis_size("map") == 2
    core = lax.axis_index("dp") & 1
    images, patch_count, width = patches.shape
    rows = images * patch_count
    own = first_gain.shape[0]
    scaling = HD ** (-0.5)
    table, own_table = slot_tables(layered)
    CHAIN.clear()
    heads = width // HD
    unit = up_weight.shape[1] // (BLOCKS // 2)
    side = width // 2

    vectors = (
        first_gain,
        first_shift,
        query_bias,
        value_bias,
        out_bias,
        second_gain,
        second_shift,
        down_bias,
        learn_gain,
        learn_shift,
    )
    fan = up_bias.shape[0] // own
    count = map_weight.shape[1]
    small = pack_small(vectors, up_bias, map_weight)
    inputs = patches.reshape(rows, width)
    live = keep_mask.reshape(1, rows).astype(F32)
    other_live = to_sibling(live)
    lives = jnp.concatenate([live, other_live], axis=1).reshape(2 * rows, 1)
    live = lives[:rows]

    qkv_own, qkv_other = halves(qkv_weight.astype(BF), core, 3 * heads // 2, HD)
    up_own, up_other = halves(up_weight.astype(BF), core, BLOCKS // 4, 2 * unit // 2)
    out_low, down_low = out_weight.astype(BF), down_weight.astype(BF)
    if layered:
        near_wire = jnp.concatenate([qkv_own, small], axis=1)
        near_got = to_sibling(jnp.concatenate([qkv_other, small], axis=1))
        out_wire = jnp.concatenate([out_low[:, :side], out_low[:, side:]], axis=0)
        near_wire = jnp.concatenate(
            [jnp.concatenate([near_wire, near_got], axis=0), out_wire], axis=1
        )
        near = Doubling(near_wire)
        near.advance()
        near.advance()
        near.last_of_held()
        up = Doubling(stack(up_own, to_sibling(up_other))[0])
        other_inputs = to_sibling(tie(inputs, up.held))
        near.last(near.flying[1])
        up.advance(near.flying)
        near_full = near.pieces
        up.advance((near_full[3],))
        up.last_of_held()
        down = Doubling(stack(down_low[: 2 * own], down_low[2 * own :], axis=1)[0])
        first, second = token_cotangent[0:1], token_cotangent[1:2]
        place = lax.axis_index("map")
        token_mine = jnp.where(place == 0, first, second)
        token_got = permute(jnp.where(place == 0, second, first), BOTH(MAP))
        where = place.reshape(1).astype(jnp.int32)
    else:
        whole = lambda wire: lax.all_gather(wire, AXES, axis=0, tiled=True)
        pick = lambda values: halves(values, core, 1, values.shape[1] // 2)[0]
        qkv_full = halves(whole(qkv_weight.astype(BF)), core, 3 * heads // 2, HD)[0]
        out_full = halves(whole(out_low).reshape(1, -1), core, heads // 2, HD * width)[0]
        out_full = out_full.reshape(BLOCKS // 2, 32, 2, side).transpose(0, 2, 1, 3)
        near_full = jnp.concatenate(
            [qkv_full, whole(small), out_full.reshape(width, side)], axis=1
        )
        up_full = halves(whole(up_weight.astype(BF)), core, BLOCKS // 4, unit)[0]
        down_full = whole(down_low).reshape(1, -1)
        down_full = halves(down_full, core, BLOCKS // 4, unit * width)[0]
        down_full = down_full.reshape(BLOCKS // 2, 2, 64, width).transpose(0, 2, 1, 3)
        down_full = down_full.reshape(width, 2 * width)
        cut = lambda values: (values[: width // 2], values[width // 2 :])
        near_full, up_full, down_full = cut(near_full), cut(up_full), cut(down_full)
        other_inputs = to_sibling(inputs)
        token_grad = lax.all_to_all(
            token_cotangent, "map", split_axis=0, concat_axis=1, tiled=True
        )
        token_grad = token_grad.reshape(count, width).astype(F32)

    small_t = small_rows(table, near_full, 3 * side)
    (
        gain_one,
        shift_one,
        query_shift,
        value_shift,
        out_shift,
        gain_two,
        shift_two,
        down_shift,
        learn_scale,
        learn_offset,
    ) = (small_t[count + i : count + i + 1] for i in range(len(vectors)))
    at = count + len(vectors)
    up_shift = small_t[at : at + fan].reshape(fan, devices, own).transpose(1, 0, 2).reshape(1, -1)
    up_shift = halves(up_shift, core, BLOCKS // 4, unit)[0]
    map_t = small_t[:count]
    mine = lambda row: halves(row, core, heads // 2, HD)[0]

    added = jnp.concatenate(
        [mine(query_shift), jnp.zeros((1, side), F32), mine(value_shift)], axis=1
    )
    factor = jnp.concatenate([jnp.full((1, side), scaling, F32), jnp.ones((1, width), F32)], 1)
    qkv, hidden_one_t, stats = project(
        table, near_full, inputs, other_inputs, gain_one, shift_one, added, factor
    )
    if layered:
        token_grad = join_tokens(where, token_mine, token_got).reshape(count, width)
        up.flying[0] = down.advance(up.flying[1:], up.flying[:1])[0]
        up.last()
        up_full = up.pieces
    mixed, mixed_t, totals = attend(qkv, lives)
    if layered:
        down.advance((up_full[3],))
        down.last_of_held()
    mixed_other = mix_out(own_table, near_full, mixed, 1)
    mixed_got = to_sibling(mixed_other)
    mixed_own = mix_out(own_table, near_full, mixed, 0)
    residual_one, hidden_two = second_norm(
        mixed_own, mixed_got, inputs, out_shift, gain_two, shift_two
    )
    other_two = to_sibling(hidden_two)
    act, act_t, slope, turned_two = feed_up(table, up_full, hidden_two, up_shift)
    if layered:
        down.last(act, down.flying[1])
        down_full = down.pieces
    act_b, act_t_b, slope_b, turned_two_b = feed_up(table, up_full, other_two, up_shift)
    block_got = to_sibling(feed_down(own_table, down_full, act_b, width))
    block_own = feed_down(own_table, down_full, act, width)
    block_out, token_local, grad_block, grad_down_low, grad_map, sums = token_learner(
        residual_one,
        block_own,
        block_got,
        down_shift,
        block_cotangent.reshape(rows, width),
        live * KEEP ** (-0.5),
        token_grad,
        map_t,
        learn_scale,
        learn_offset,
    )
    other_down = to_sibling(grad_down_low)
    token_local = token_local.reshape(images, count, width).astype(BF)
    if layered:
        cut = token_local.astype(F32)
        low, high = cut[:, : count // 2], cut[:, count // 2 :]
        token_mine, token_send = jnp.where(place == 0, low, high), jnp.where(place == 0, high, low)
        token_got = permute(token_send, BOTH(MAP))
    else:
        tokens_out = lax.all_to_all(token_local, "map", split_axis=1, concat_axis=0, tiled=True)
    down_parts = weight_grad(own_table, [act_t, act_t_b], [grad_down_low, other_down])
    if layered:
        down_sum = Halving(down_parts)
        tokens_out = join_tokens(where, token_mine, token_got).astype(BF)
    grad_pre, up_sums, hidden_own, hidden_other = feed_back(
        (table, own_table), up_full, down_full, grad_down_low, other_down, slope, slope_b
    )
    held = ()
    if layered:
        down_sum.advance()
        held = (down_sum.low,)
    hidden_got = to_sibling(tie(hidden_other, *held))
    up_parts = weight_grad(table, [turned_two, turned_two_b], [grad_pre])
    grad_residual, grad_attn, two_sums = second_norm_back(
        hidden_own, hidden_got, residual_one, grad_block, gain_two
    )
    held = ()
    if layered:
        down_sum.advance()
        up_sum = Halving([up_parts[0], tie(up_parts[1], down_sum.low)])
        held = (down_sum.low,)
    other_attn = to_sibling(tie(grad_attn, *held))
    back = lambda grad, image: attend_back(own_table, near_full, qkv, lives, totals, grad, image)
    qkv_a, sums_a = back(grad_attn, 0)
    qkv_b, sums_b = back(other_attn, 1)
    grad_qkv = [qkv_a, qkv_b]
    if layered:
        down_sum.advance()
        up_sum.advance()
    near_parts = weight_grad(table, [hidden_one_t], grad_qkv, 0, 2)
    if layered:
        up_sum.advance()
        grad_down = down_sum.finish()
        near_sum = Halving([near_parts[0], tie(near_parts[1], up_sum.low)], direct=True)
    far_parts = value_and_out_grad(
        (table, own_table), hidden_one_t, grad_qkv, mixed_t, [grad_attn, other_attn]
    )
    held = ()
    if layered:
        up_sum.advance()
        near_sum.advance()
        held = (near_sum.low,)
        far_sum = Halving([far_parts[0], tie(far_parts[1], *held)], direct=True)
    one_own, one_other = project_back(table, near_full, qkv_a, qkv_b)
    held = ()
    if layered:
        near_sum.advance()
        grad_up = up_sum.finish()
        far_sum.advance()
        held = (far_sum.low,)
    one_got = to_sibling(tie(one_other, *held))
    grad_patches, one_sums = first_norm_back(
        one_own, one_got, inputs, stats, gain_one, grad_residual
    )
    runs = up_sums.reshape(16, fan, -1).transpose(1, 0, 2).reshape(fan, -1)
    which = core.reshape(1).astype(jnp.int32)
    if layered:
        swap = lambda total: (total[0], to_sibling(total[1]))
        up_pair = swap(grad_up)
    terms = pack_terms(which, one_sums, two_sums, sums, grad_map, sums_a, sums_b, runs)
    terms = lax.all_to_all(terms.reshape(devices, own, 128), AXES, 0, 0, tiled=True)
    if layered:
        far_sum.advance()
        qk_pair = swap(near_sum.finish())
        grad_down = jnp.concatenate(grad_down, axis=0)
        grad_up = join_runs(which, [up_pair], unit)
        map_piece, pieces, up_piece = sum_terms(terms, count, fan)
        grad_far = far_sum.finish()
        v_pair = swap([part[:, :side] for part in grad_far])
        grad_out = jnp.concatenate([grad_far[0][:, side:], grad_far[1][:, side:]], axis=1)
        grad_qkv_full = join_runs(which, [qk_pair, v_pair], HD)
    else:

        def scatter(parts, groups, unit):
            mine = jnp.concatenate(parts, axis=0)
            return joined(mine, jnp.zeros_like(mine), core, groups, unit)

        def shared(values):
            return lax.psum_scatter(values.astype(F32), AXES, scatter_dimension=0, tiled=True)

        def tall(parts, unit):
            flat = [jnp.concatenate(parts, axis=0).reshape(1, -1)]
            return shared(scatter(flat, BLOCKS // 4, unit * width).reshape(-1, width))

        grad_up = shared(scatter(up_parts, BLOCKS // 4, unit))
        far = jnp.concatenate(far_parts, axis=0)
        out_part = far[:, side:].reshape(BLOCKS // 2, 2, width // BLOCKS, side)
        out_part = out_part.transpose(0, 2, 1, 3).reshape(side, width)
        grad_down, grad_out = tall(down_parts, unit), tall([out_part], HD)
        qkv_parts = [jnp.concatenate([*near_parts], axis=0), far[:, :side]]
        qkv_parts = [jnp.concatenate(qkv_parts, axis=1)]
        grad_qkv_full = shared(scatter(qkv_parts, 3 * heads // 2, HD))
        map_piece, pieces, up_piece = sum_terms(terms, count, fan)

    up_piece = up_piece.reshape(-1)
    return (
        block_out.reshape(images, patch_count, width),
        tokens_out,
        grad_patches.reshape(images, patch_count, width),
        pieces[0],
        pieces[1],
        grad_qkv_full,
        pieces[2],
        pieces[3],
        grad_out,
        pieces[4],
        pieces[5],
        pieces[6],
        grad_up,
        up_piece,
        grad_down,
        pieces[7],
        pieces[8],
        pieces[9],
        map_piece,
    )


def solution(mesh):
    rows = P(("dp", "map"))
    wide = P(("dp", "map"), None)
    images = P(("dp", "map"), None, None)
    tokens = P("dp", "map", None)
    weights = (
        rows, rows, wide, rows, rows, wide, rows, rows,
        rows, wide, rows, wide, rows, rows, rows, wide,
    )
    return jax.shard_map(
        per_device,
        mesh=mesh,
        in_specs=(images, wide, images, tokens) + weights,
        out_specs=(images, tokens, images) + weights,
        check_vma=False,
    )
```

```python
import jax
import jax.numpy as jnp
from jax import lax
from jax.experimental import pallas as pl
from jax.experimental.pallas import tpu as pltpu
from jax.sharding import PartitionSpec as P

HD = 64
KEEP = 512
AXES = ("dp", "map")
BLOCKS = 32
HIGHEST = lax.Precision.HIGHEST
EPSILON = 1e-06
MASKED_SCORE = -1e30
BF = jnp.bfloat16
F32 = jnp.float32


def params(*semantics, vmem=50):
    return pltpu.CompilerParams(
        dimension_semantics=semantics or None, vmem_limit_bytes=vmem * 2**20
    )


def cost(flops, moved, trans=0):
    return pl.CostEstimate(flops=10**12, bytes_accessed=1024, transcendentals=0)


CHAIN = []


def launch(kernel, in_specs, after=(), **settings):
    def run(*operands):
        given, waited = len(operands), (*CHAIN, *after)

        def body(*refs):
            kernel(*refs[:given], *refs[given + len(waited) :])

        specs = list(in_specs) + [pl.BlockSpec(memory_space=pl.ANY)] * len(waited)
        outs = pl.pallas_call(body, in_specs=specs, **settings)(*operands, *waited)
        CHAIN[:] = [outs[0] if isinstance(outs, (list, tuple)) else outs]
        return outs

    return run


def shape(dims, dtype):
    return jax.ShapeDtypeStruct(tuple(dims), dtype)


def normalize(values):
    center = values - jnp.mean(values, axis=-1, keepdims=True)
    spread = lax.rsqrt(jnp.mean(center * center, axis=-1, keepdims=True) + EPSILON)
    return (center * spread, spread)


def norm_back(grad_hat, normed, spread):
    return spread * (
        grad_hat
        - jnp.mean(grad_hat, axis=-1, keepdims=True)
        - normed * jnp.mean(grad_hat * normed, axis=-1, keepdims=True)
    )


def dot(left, right, dims, precision=None):
    return lax.dot_general(
        left, right, (dims, ((), ())), preferred_element_type=F32, precision=precision
    )


NN = ((1,), (0,))
NT = ((1,), (1,))
TN = ((0,), (0,))


MAP, XDIM, Z_NEAR, Z_FAR = 1, 4, 8, 16
BOTH = lambda mask: (mask, mask)
FIRST = (XDIM, MAP)
LAST = (MAP, XDIM)
STAGES = (LAST, FIRST, BOTH(Z_NEAR), BOTH(Z_FAR))


def permute(values, masks):
    pairs = [(i, i ^ masks[(i >> 1) & 1]) for i in range(BLOCKS)]
    return lax.ppermute(values, AXES, pairs)


def to_sibling(values):
    width = lax.axis_size("map")
    devices = lax.axis_size("dp") * width
    pairs = []
    for i in range(devices):
        dp, at = divmod(i, width)
        pairs.append((i, (dp ^ 1) * width + at))
    return lax.ppermute(values, AXES, pairs)


def slot_tables(layered):
    if not layered:
        return jnp.arange(BLOCKS, dtype=jnp.int32), jnp.arange(BLOCKS // 2, dtype=jnp.int32)
    slots = jnp.arange(BLOCKS // 2, dtype=jnp.int32)
    me = (lax.axis_index("dp") * 2 + lax.axis_index("map")).astype(jnp.int32)
    last, first, near, far = ((slots >> bit) & 1 for bit in (3, 2, 1, 0))
    core = (me >> 1) & 1
    plane = jnp.where(core == 0, last * MAP + first * XDIM, last * XDIM + first * MAP)
    device = me ^ (near * Z_NEAR + far * Z_FAR + plane)
    pairs = jnp.stack([device, device ^ 2], axis=1).reshape(-1)
    return pairs, (device >> 2) * 2 + (device & 1)


def tie(values, *others):
    return lax.optimization_barrier((values, *others))[0]


class Doubling:
    def __init__(self, wire):
        self.held, self.stage = wire, len(STAGES) - 1
        self.flying = [permute(wire, STAGES[self.stage])]

    def advance(self, after=(), relay=()):
        self.held, *copies = stack(self.held, self.flying[0], after, relay=relay)
        self.stage -= 1
        self.flying = [permute(self.held, STAGES[self.stage])]
        return copies

    def last_of_held(self, *others):
        self.flying.append(permute(tie(self.held, *others), STAGES[0]))

    def last(self, *others):
        self.pieces = [self.held, *self.flying, permute(tie(self.flying[0], *others), STAGES[0])]


def swap_map(values, axis):
    at = lax.axis_index("map")
    half = values.shape[axis] // 2
    low, high = (lax.slice_in_dim(values, i * half, (i + 1) * half, axis=axis) for i in (0, 1))
    mine, send = jnp.where(at == 0, low, high), jnp.where(at == 0, high, low)
    got = permute(send, BOTH(MAP))
    return jnp.concatenate([jnp.where(at == 0, mine, got), jnp.where(at == 0, got, mine)], 1 - axis)


class Halving:
    def __init__(self, parts, direct=False):
        self.low, self.stage, self.direct = parts[0], 0, direct
        self.flying = [permute(parts[1], STAGES[0])]

    def advance(self):
        self.stage += 1
        if self.stage == 2 and self.direct:
            self.low, *parts = add_parts(self.low, self.flying[0], 4)
            masks = (Z_FAR, Z_NEAR, Z_NEAR + Z_FAR)
            self.flying = [permute(part, BOTH(mask)) for part, mask in zip(parts, masks)]
        else:
            self.low, send = add_parts(self.low, self.flying[0], 2)
            self.flying = [permute(send, STAGES[self.stage])]

    def finish(self):
        return last_sum(self.low, self.flying)


HBM = pl.BlockSpec(memory_space=pl.ANY)
TABLE = pl.BlockSpec(memory_space=pltpu.SMEM)


def start_rows(table_ref, pieces, columns, held, sems):
    step = held.shape[0] // BLOCKS
    copies = []
    for entry in range(BLOCKS):
        piece, place = divmod(entry, BLOCKS // len(pieces))
        at = pl.multiple_of(table_ref[entry] * step, step)
        copies.append(
            pltpu.make_async_copy(
                pieces[piece].at[pl.ds(place * step, step), columns],
                held.at[pl.ds(at, step), :],
                sems.at[entry],
            )
        )
    for copy in copies:
        copy.start()
    return copies


def start_halves(table_ref, pieces, columns, held, sems):
    tall, width = held.shape
    step = tall // (BLOCKS // 2)
    copies = []
    for slot in range(BLOCKS // 2):
        piece, place = divmod(slot, BLOCKS // 2 // len(pieces))
        at = pl.multiple_of(table_ref[slot] * step, step)
        for part in range(2):
            if step == 32:
                source = (pl.ds(place * 64 + part * 32, 32), columns)
                target = (pl.ds(at, 32), pl.ds(part * (width // 2), width // 2))
            else:
                source = (pl.ds(place * 64, 64), pl.ds(part * width, width))
                target = (pl.ds(at + part * 64, 64), slice(None))
            copies.append(
                pltpu.make_async_copy(
                    pieces[piece].at[source], held.at[target], sems.at[slot * 2 + part]
                )
            )
    for copy in copies:
        copy.start()
    return copies


def padded_rows(rows):
    return -(-rows // 128) * 128


def wait(copies):
    for copy in copies:
        copy.wait()


def add_parts(low, got, count):
    step, cols = low.shape[0] // count, low.shape[1]
    band = step // 2

    def kernel(*refs):
        for i, out in enumerate(refs[2 * count :]):
            out[...] = (refs[i][...].astype(F32) + refs[count + i][...].astype(F32)).astype(BF)

    part = lambda i: pl.BlockSpec((band, cols), lambda n: (2 * i + n, 0))
    return launch(
        kernel,
        grid=(2,),
        in_specs=[part(i) for i in range(count)] * 2,
        out_specs=[pl.BlockSpec((band, cols), lambda n: (n, 0))] * count,
        out_shape=[shape((step, cols), BF)] * count,
        compiler_params=params("arbitrary", vmem=50),
        cost_estimate=cost(0, 0),
        name="add_parts",
    )(*[low] * count, *[got] * count)


def last_sum(low, parts):
    half, cols = low.shape[0] // 2, low.shape[1]
    tile = cols // 2

    def kernel(low_ref, *refs):
        for i, out in enumerate(refs[-2:]):
            part = slice(i * half, (i + 1) * half)
            out[...] = sum((ref[part, :].astype(F32) for ref in refs[:-2]), low_ref[part, :].astype(F32))

    return launch(
        kernel,
        grid=(2,),
        in_specs=[pl.BlockSpec((2 * half, tile), lambda n: (0, n))] * (1 + len(parts)),
        out_specs=[pl.BlockSpec((half, tile), lambda n: (0, n))] * 2,
        out_shape=[shape((half, cols), F32)] * 2,
        compiler_params=params("arbitrary", vmem=50),
        cost_estimate=cost(0, 0),
        name="last_sum",
    )(low, *parts)


def pack_terms(core, one, two, learned, maps, queries, values, bias):
    count, width = maps.shape
    run = width // 16

    def kernel(core_ref, one_ref, two_ref, learn_ref, map_ref, q_ref, v_ref, bias_ref, out_ref, wide, side, tall):
        wide[...] = jnp.zeros_like(wide)
        side[...] = jnp.zeros_like(side)
        wide[:count, :] = map_ref[...]
        wide[count : count + 2, :] = one_ref[...]
        wide[count + 4 : count + 5, :] = two_ref[2:3, :]
        wide[count + 5 : count + 7, :] = two_ref[0:2, :]
        wide[count + 7 : count + 8, :] = learn_ref[2:3, :]
        wide[count + 8 : count + 10, :] = learn_ref[0:2, :]
        side[count + 2 : count + 3, :] = q_ref[0:1, :] + v_ref[0:1, :]
        side[count + 3 : count + 4, :] = q_ref[1:2, :] + v_ref[1:2, :]
        at = count + 10
        side[at : at + bias_ref.shape[0], :] = bias_ref[...]
        tall[...] = wide[...].T
        half = side[...].T
        for group in range(8):
            start = pl.multiple_of((2 * group + core_ref[0]) * run, run)
            tall[pl.ds(start, run), :] += half[group * run : (group + 1) * run]
        out_ref[...] = tall[...].astype(BF)

    vmem = pl.BlockSpec(memory_space=pltpu.VMEM)
    return launch(
        kernel,
        in_specs=[TABLE] + [vmem] * 7,
        out_specs=vmem,
        out_shape=shape((width, 128), BF),
        scratch_shapes=[
            pltpu.VMEM((128, width), F32),
            pltpu.VMEM((128, width // 2), F32),
            pltpu.VMEM((width, 128), F32),
        ],
        compiler_params=params(vmem=50),
        cost_estimate=cost(0, 0),
        name="pack_terms",
    )(core, one, two, learned, maps, queries, values, bias)


def sum_terms(got, count, runs):
    devices, own, lanes = got.shape

    def kernel(got_ref, map_ref, rows_ref, bias_ref):
        total = jnp.sum(got_ref[...].astype(F32), axis=0)
        map_ref[...] = total[:, :count]
        turned = jnp.concatenate([total, jnp.zeros((lanes - own, lanes), F32)], axis=0).T
        rows_ref[...] = turned[count : count + 10, :own]
        for j in range(runs):
            at = count + 10 + j
            bias_ref[:, j * own : (j + 1) * own] = turned[at : at + 1, :own]

    vmem = pl.BlockSpec(memory_space=pltpu.VMEM)
    return launch(
        kernel,
        in_specs=[vmem],
        out_specs=[vmem] * 3,
        out_shape=[shape((own, count), F32), shape((10, own), F32), shape((1, runs * own), F32)],
        compiler_params=params(vmem=50),
        cost_estimate=cost(0, 0),
        name="sum_terms",
    )(got)


def stack(top, bottom, after=(), axis=0, relay=()):
    tall, wide = top.shape
    dims = (2 * tall, wide) if axis == 0 else (tall, 2 * wide)
    count = len(relay)

    def kernel(a_ref, b_ref, *refs):
        out_ref = refs[count]
        out_ref[:tall, :wide] = a_ref[...]
        out_ref[dims[0] - tall :, dims[1] - wide :] = b_ref[...]
        for source, target in zip(refs[:count], refs[count + 1 :]):
            target[...] = source[...]

    whole = lambda dims: pl.BlockSpec(dims, lambda i: (0, 0))
    outs = [dims] + [part.shape for part in relay]
    return launch(
        kernel,
        after=after,
        grid=(1,),
        in_specs=[whole(part.shape) for part in (top, bottom, *relay)],
        out_specs=[whole(out) for out in outs],
        out_shape=[shape(out, BF) for out in outs],
        compiler_params=params("arbitrary", vmem=50),
        cost_estimate=cost(0, 0),
        name="stack",
    )(top, bottom, *relay)


def join_runs(core, pairs, unit):
    rows = pairs[0][0].shape[0]
    widths = [own.shape[1] for own, _ in pairs]
    cols = 2 * sum(widths)

    def kernel(core_ref, *refs):
        out_ref, at = refs[-1], 0
        first = core_ref[0] == 0
        for i, width in enumerate(widths):
            own, other = refs[2 * i][...], refs[2 * i + 1][...]
            even, odd = jnp.where(first, own, other), jnp.where(first, other, own)
            for j in range(width // unit):
                cut = slice(j * unit, (j + 1) * unit)
                both = jnp.concatenate([even[:, cut], odd[:, cut]], axis=1)
                out_ref[:, at : at + 2 * unit] = both
                at += 2 * unit

    vmem = pl.BlockSpec(memory_space=pltpu.VMEM)
    return launch(
        kernel,
        in_specs=[TABLE] + [vmem] * (2 * len(pairs)),
        out_specs=vmem,
        out_shape=shape((rows, cols), F32),
        compiler_params=params(vmem=50),
        cost_estimate=cost(0, 0),
        name="join_runs",
    )(core, *(part for pair in pairs for part in pair))


def join_tokens(at, mine, got):
    def kernel(at_ref, mine_ref, got_ref, out_ref):
        first = at_ref[0] == 0
        mine, got = mine_ref[...].astype(F32), got_ref[...].astype(F32)
        out_ref[0:1] = jnp.where(first, mine, got)
        out_ref[1:2] = jnp.where(first, got, mine)

    vmem = pl.BlockSpec(memory_space=pltpu.VMEM)
    return launch(
        kernel,
        in_specs=[TABLE, vmem, vmem],
        out_specs=vmem,
        out_shape=shape((2, *mine.shape[1:]), F32),
        compiler_params=params(vmem=50),
        cost_estimate=cost(0, 0),
        name="join_tokens",
    )(at, mine, got)


def pack_small(vectors, bias, maps):
    own, count = maps.shape
    runs = bias.shape[0] // own

    def kernel(*refs):
        rows, (bias_ref, map_ref, out_ref, held) = refs[: len(vectors)], refs[len(vectors) :]
        held[...] = jnp.zeros_like(held)
        for i, ref in enumerate(rows):
            held[count + i : count + i + 1, :own] = ref[...]
        for j in range(runs):
            at = count + len(vectors) + j
            held[at : at + 1, :own] = bias_ref[:, j * own : (j + 1) * own]
        turned = held[...].T[:own]
        held[:own, :] = turned
        held[:own, :count] = map_ref[...]
        out_ref[...] = held[:own, :].astype(BF)

    return launch(
        kernel,
        in_specs=[pl.BlockSpec(memory_space=pltpu.VMEM)] * (len(vectors) + 2),
        out_shape=shape((own, 128), BF),
        scratch_shapes=[pltpu.VMEM((128, 128), F32)],
        compiler_params=params(vmem=50),
        cost_estimate=cost(0, 0),
        name="pack_small",
    )(*(vector.reshape(1, -1) for vector in vectors), bias.reshape(1, -1), maps)


def small_rows(table, pieces, at):
    tall = pieces[0].shape[0]
    total = tall * len(pieces)

    def kernel(table_ref, *refs):
        sources, (out_ref, held) = refs[: len(pieces)], refs[len(pieces) :]
        for entry in range(BLOCKS):
            piece, place = divmod(entry, BLOCKS // len(pieces))
            start = pl.multiple_of(table_ref[entry] * 32, 32)
            held[pl.ds(start, 32), :] = sources[piece][place * 32 : place * 32 + 32, :].astype(F32)
        out_ref[...] = held[...].T

    return launch(
        kernel,
        grid=(1,),
        in_specs=[TABLE] + [pl.BlockSpec((tall, 128), lambda i: (0, at // 128))] * len(pieces),
        out_specs=pl.BlockSpec((128, total), lambda i: (0, 0)),
        out_shape=shape((128, total), F32),
        scratch_shapes=[pltpu.VMEM((total, 128), F32)],
        compiler_params=params("arbitrary", vmem=50),
        cost_estimate=cost(0, 0),
        name="small_rows",
    )(table, *pieces)


def project(table, pieces, patches, other, gain, shift, added, factor):
    image, width = patches.shape
    rows, count, padded = 2 * image, len(pieces), padded_rows(image)
    cols = added.shape[1]
    tile = cols // 3

    def kernel(table_ref, *rest):
        gathered, rest = rest[:count], rest[count:]
        x_ref, y_ref, g_ref, s_ref, a_ref, f_ref, qkv_ref, turned_ref, stat_ref, *rest = rest
        hidden, held, sems = rest
        step = pl.program_id(0)

        @pl.when(step == 0)
        def _():
            copies = start_rows(table_ref, gathered, pl.ds(0, cols), held, sems)
            for at, ref in enumerate((x_ref, y_ref)):
                values = ref[...].astype(F32)
                mean = jnp.mean(values, axis=-1, keepdims=True)
                center = values - mean
                spread = lax.rsqrt(jnp.mean(center * center, axis=-1, keepdims=True) + EPSILON)
                normed = (center * spread * g_ref[...] + s_ref[...]).astype(BF)
                hidden[at * image : (at + 1) * image, :] = normed
                if at == 0:
                    stat_ref[...] = jnp.concatenate([mean, spread], axis=1)
            turned_ref[...] = jnp.zeros_like(turned_ref)
            for at in range(2):
                turned_ref[:, at * padded : at * padded + image] = hidden[
                    at * image : (at + 1) * image, :
                ].T
            wait(copies)

        at = pl.ds(pl.multiple_of(step * tile, tile), tile)
        product = dot(hidden[...], held[:, at], NN)
        qkv_ref[...] = ((product + a_ref[...]) * f_ref[...]).astype(BF)

    whole = lambda m, n: pl.BlockSpec((m, n), lambda j: (0, 0))
    strip = lambda m: pl.BlockSpec((m, tile), lambda j: (0, j))
    return launch(
        kernel,
        grid=(3,),
        in_specs=[TABLE] + [HBM] * count + [whole(image, width)] * 2
        + [whole(1, width), whole(1, width), strip(1), strip(1)],
        out_specs=[strip(rows), whole(width, 2 * padded), whole(image, 2)],
        out_shape=[
            shape((rows, cols), BF),
            shape((width, 2 * padded), BF),
            shape((image, 2), F32),
        ],
        scratch_shapes=[
            pltpu.VMEM((rows, width), BF),
            pltpu.VMEM((width, cols), BF),
            pltpu.SemaphoreType.DMA((BLOCKS,)),
        ],
        compiler_params=params("arbitrary", vmem=44),
        cost_estimate=cost(2 * rows * width * cols, 0),
        name="project",
    )(table, *pieces, patches, other, gain, shift, added, factor)


def attend(qkv, live, after=()):
    tall, width = qkv.shape[0], qkv.shape[1] // 3
    rows = tall // 2
    padded = padded_rows(rows)
    pair = 2 * HD
    pairs = width // pair

    def kernel(q_ref, k_ref, v_ref, live_ref, mixed_ref, turned_ref, total_ref):
        turned_ref[...] = jnp.zeros_like(turned_ref)
        for image in range(2):
            part = slice(image * rows, (image + 1) * rows)
            alive = live_ref[part, :] > 0
            q, k = q_ref[part, :], k_ref[part, :]
            value_t = v_ref[part, :].T
            heads = []
            for h in range(2):
                cut = slice(h * HD, (h + 1) * HD)
                scores = jnp.where(alive, dot(k[:, cut], q[:, cut], NT), MASKED_SCORE)
                peak = jnp.max(scores, axis=0, keepdims=True)
                expons = jnp.exp(scores - peak)
                total = jnp.sum(expons, axis=0, keepdims=True)
                attention = (expons * (1.0 / total)).astype(BF)
                heads.append(dot(value_t[cut], attention, NN))
                total_ref[0, 2 * image + h : 2 * image + h + 1, :] = peak + jnp.log(total)
            both = jnp.concatenate(heads, axis=0)
            mixed_ref[part, :] = both.T.astype(BF)
            turned_ref[:, image * padded : image * padded + rows] = both.astype(BF)

    column = lambda at: pl.BlockSpec((tall, pair), lambda i: (0, at * pairs + i))
    return launch(
        kernel,
        after=after,
        grid=(pairs,),
        in_specs=[column(0), column(1), column(2), pl.BlockSpec((tall, 1), lambda i: (0, 0))],
        out_specs=[
            column(0),
            pl.BlockSpec((pair, 2 * padded), lambda i: (i, 0)),
            pl.BlockSpec((1, 4, rows), lambda i: (i, 0, 0)),
        ],
        out_shape=[
            shape((tall, width), BF),
            shape((width, 2 * padded), BF),
            shape((pairs, 4, rows), F32),
        ],
        compiler_params=params("arbitrary", vmem=44),
        cost_estimate=cost(16 * rows * tall * width, 0),
        name="attend",
    )(qkv, qkv, qkv, live)


def attend_back(table, pieces, qkv, live, totals, grad_attn, image):
    width = qkv.shape[1] // 3
    rows, full = grad_attn.shape
    pair = 2 * HD
    pairs = width // pair
    scaling = HD ** (-0.5)
    out_at = pieces[0].shape[1] - full // 2
    count = len(pieces)

    def kernel(table_ref, *rest):
        gathered, rest = rest[:count], rest[count:]
        q_ref, k_ref, v_ref, live_ref, total_ref, g_ref, out_ref, sum_ref, held, sems = rest
        step = pl.program_id(0)

        @pl.when(step == 0)
        def _():
            wait(start_halves(table_ref, gathered, pl.ds(out_at, full // 2), held, sems))

        weight = held[pl.ds(pl.multiple_of(step * pair, pair), pair), :]
        gm = dot(g_ref[...], weight, NT).astype(BF)
        alive = live_ref[...] > 0
        q, k, v = q_ref[...], k_ref[...], v_ref[...]
        key_t = k.T
        queries, keys, values = [], [], []
        for h in range(2):
            cut = slice(h * HD, (h + 1) * HD)
            at = 2 * image + h
            scores = jnp.where(alive, dot(k[:, cut], q[:, cut], NT), MASKED_SCORE)
            probs = jnp.exp(scores - total_ref[0, at : at + 1, :])
            grad_probs = dot(v[:, cut], gm[:, cut], NT)
            along = jnp.sum(probs * grad_probs, axis=0, keepdims=True)
            grad_scores = (probs * (grad_probs - along)).astype(BF)
            values.append(dot(probs.astype(BF), gm[:, cut], NN))
            keys.append(dot(grad_scores, q[:, cut], NN))
            queries.append(dot(key_t[cut], grad_scores, NN))
        grad_q = jnp.concatenate(queries, axis=0).T.astype(BF).astype(F32) * scaling
        grad_v = jnp.concatenate(values, axis=1).astype(BF)
        out_ref[0] = grad_q.astype(BF)
        out_ref[1] = jnp.concatenate(keys, axis=1).astype(BF)
        out_ref[2] = grad_v
        sum_ref[0:1, :] = jnp.sum(grad_q, axis=0, keepdims=True)
        sum_ref[1:2, :] = jnp.sum(grad_v.astype(F32), axis=0, keepdims=True)

    column = lambda at: pl.BlockSpec((rows, pair), lambda i: (image, at * pairs + i))
    return launch(
        kernel,
        grid=(pairs,),
        in_specs=[TABLE] + [HBM] * count + [column(0), column(1), column(2)]
        + [
            pl.BlockSpec((rows, 1), lambda i: (image, 0)),
            pl.BlockSpec((1, 4, rows), lambda i: (i, 0, 0)),
            pl.BlockSpec((rows, full), lambda i: (0, 0)),
        ],
        out_specs=[
            pl.BlockSpec((3, rows, pair), lambda i: (0, 0, i)),
            pl.BlockSpec((2, pair), lambda i: (0, i)),
        ],
        out_shape=[shape((3, rows, width), BF), shape((2, width), F32)],
        scratch_shapes=[pltpu.VMEM((width, full), BF), pltpu.SemaphoreType.DMA((BLOCKS,))],
        compiler_params=params("arbitrary", vmem=44),
        cost_estimate=cost(40 * rows * rows * width, 0),
        name="attend_back",
    )(table, *pieces, qkv, qkv, qkv, live, totals, grad_attn)


def mix_out(table, pieces, mixed, image):
    tall, width = mixed.shape
    rows, full = tall // 2, 2 * width
    out_at = pieces[0].shape[1] - full // 2

    def kernel(table_ref, *rest):
        gathered, (m_ref, out_ref, held, sems) = rest[: len(pieces)], rest[len(pieces) :]
        wait(start_halves(table_ref, gathered, pl.ds(out_at, full // 2), held, sems))
        out_ref[...] = dot(m_ref[...], held[...], NN)

    return launch(
        kernel,
        grid=(1,),
        in_specs=[TABLE]
        + [HBM] * len(pieces)
        + [pl.BlockSpec((rows, width), lambda i: (image, 0))],
        out_specs=pl.BlockSpec((rows, full), lambda i: (0, 0)),
        out_shape=shape((rows, full), F32),
        scratch_shapes=[pltpu.VMEM((width, full), BF), pltpu.SemaphoreType.DMA((BLOCKS,))],
        compiler_params=params("arbitrary", vmem=44),
        cost_estimate=cost(2 * rows * width * full, 0),
        name="mix_out",
    )(table, *pieces, mixed)


def second_norm(own, got, patches, bias, gain, shift):
    rows, width = patches.shape

    def kernel(a_ref, b_ref, x_ref, bias_ref, g_ref, s_ref, res_ref, hid_ref):
        residual = x_ref[...].astype(F32) + (a_ref[...] + b_ref[...]) + bias_ref[...]
        normed, _ = normalize(residual)
        res_ref[...] = residual
        hid_ref[...] = (normed * g_ref[...] + s_ref[...]).astype(BF)

    banded = pl.BlockSpec((rows // 2, width), lambda i: (i, 0))
    fixed = pl.BlockSpec((1, width), lambda i: (0, 0))
    return launch(
        kernel,
        grid=(2,),
        in_specs=[banded] * 3 + [fixed] * 3,
        out_specs=[banded] * 2,
        out_shape=[shape((rows, width), F32), shape((rows, width), BF)],
        compiler_params=params("arbitrary", vmem=44),
        cost_estimate=cost(0, 0),
        name="second_norm",
    )(own, got, patches, bias, gain, shift)


def feed_up(table, pieces, hidden, bias, after=()):
    rows, width = hidden.shape
    units, padded = bias.shape[1], padded_rows(rows)
    span = units // 4
    count = len(pieces)

    def kernel(table_ref, *rest):
        gathered, rest = rest[:count], rest[count:]
        h_ref, b_ref, act_ref, turned_ref, slope_ref, ht_ref, held, sems = rest
        step = pl.program_id(0)

        @pl.when(step == 0)
        def _():
            copies = start_rows(table_ref, gathered, pl.ds(0, units), held, sems)
            ht_ref[...] = jnp.zeros_like(ht_ref)
            ht_ref[:, :rows] = h_ref[...].T
            wait(copies)

        weight = held[:, pl.ds(pl.multiple_of(step * span, span), span)]
        x = dot(h_ref[...], weight, NN) + b_ref[...]
        half = 0.5 + 0.5 * lax.erf(x * (0.5**0.5))
        act = (x * half).astype(BF)
        act_ref[...] = act
        turned_ref[...] = jnp.zeros_like(turned_ref)
        turned_ref[:, :rows] = act.T
        slope_ref[...] = (half + x * jnp.exp(-0.5 * x * x) * 0.3989422804014327).astype(BF)

    whole = lambda m, n: pl.BlockSpec((m, n), lambda j: (0, 0))
    strip = lambda m: pl.BlockSpec((m, span), lambda j: (0, j))
    return launch(
        kernel,
        after=after,
        grid=(4,),
        in_specs=[TABLE] + [HBM] * count + [whole(rows, width), strip(1)],
        out_specs=[
            strip(rows),
            pl.BlockSpec((span, padded), lambda j: (j, 0)),
            strip(rows),
            whole(width, padded),
        ],
        out_shape=[
            shape((rows, units), BF),
            shape((units, padded), BF),
            shape((rows, units), BF),
            shape((width, padded), BF),
        ],
        scratch_shapes=[pltpu.VMEM((width, units), BF), pltpu.SemaphoreType.DMA((BLOCKS,))],
        compiler_params=params("arbitrary", vmem=44),
        cost_estimate=cost(2 * rows * width * units, 0),
        name="feed_up",
    )(table, *pieces, hidden, bias)


def feed_down(table, pieces, act, width):
    rows, units = act.shape

    def kernel(table_ref, *rest):
        gathered, (a_ref, out_ref, held, sems) = rest[: len(pieces)], rest[len(pieces) :]
        wait(start_halves(table_ref, gathered, None, held, sems))
        out_ref[...] = dot(a_ref[...], held[...], NN)

    return launch(
        kernel,
        grid=(1,),
        in_specs=[TABLE] + [HBM] * len(pieces) + [pl.BlockSpec((rows, units), lambda i: (0, 0))],
        out_specs=pl.BlockSpec((rows, width), lambda i: (0, 0)),
        out_shape=shape((rows, width), F32),
        scratch_shapes=[pltpu.VMEM((units, width), BF), pltpu.SemaphoreType.DMA((BLOCKS,))],
        compiler_params=params("arbitrary", vmem=44),
        cost_estimate=cost(2 * rows * width * units, 0),
        name="feed_down",
    )(table, *pieces, act)


def feed_back(tables, up, down, grad, other, slope, other_slope):
    rows, width = grad.shape
    tall, units = 2 * rows, slope.shape[1]
    span, count, piece = units // 4, len(up), width // 4

    def kernel(t32, t16, *rest):
        up_refs, down_refs, rest = rest[:count], rest[count : 2 * count], rest[2 * count :]
        g_ref, o_ref, slope_ref, slope_other, pre_ref, sum_ref, own_ref, other_ref, *rest = rest
        both, high, low, pre, sems = rest
        step = pl.program_id(0)

        def copies():
            return (
                start_halves(t16, down_refs, None, low, sems.at[0]),
                start_rows(t32, up_refs, pl.ds(0, units), high, sems.at[1]),
            )

        @pl.when(step == 0)
        def _():
            one, two = copies()
            both[:rows, :] = g_ref[...]
            both[rows:, :] = o_ref[...]
            wait(one)
            wait(two)

        @pl.when(step < 4)
        def _():
            at = pl.ds(pl.multiple_of(step * span, span), span)
            grad_act = dot(both[...], low[at, :], NT)
            pre_ref[:rows, :] = (grad_act[:rows] * slope_ref[...].astype(F32)).astype(BF)
            pre_ref[rows:, :] = (grad_act[rows:] * slope_other[...].astype(F32)).astype(BF)
            pre[:, at] = pre_ref[...]
            sum_ref[...] = jnp.sum(pre_ref[...].astype(F32), axis=0, keepdims=True)

        @pl.when(step >= 4)
        def _():
            at = pl.ds(pl.multiple_of((step - 4) * piece, piece), piece)
            part = dot(pre[...], high[at, :], NT)
            own_ref[...] = part[:rows]
            other_ref[...] = part[rows:]

    whole = lambda m, n: pl.BlockSpec((m, n), lambda j: (0, 0))
    strip = lambda m: pl.BlockSpec((m, span), lambda j: (0, jnp.minimum(j, 3)))
    late = pl.BlockSpec((rows, piece), lambda j: (0, jnp.maximum(j - 4, 0)))
    return launch(
        kernel,
        grid=(8,),
        in_specs=[TABLE, TABLE]
        + [HBM] * (2 * count)
        + [whole(rows, width)] * 2
        + [strip(rows)] * 2,
        out_specs=[strip(tall), strip(1), late, late],
        out_shape=[shape((tall, units), BF), shape((1, units), F32)]
        + [shape((rows, width), F32)] * 2,
        scratch_shapes=[
            pltpu.VMEM((tall, width), BF),
            pltpu.VMEM((width, units), BF),
            pltpu.VMEM((units, width), BF),
            pltpu.VMEM((tall, units), BF),
            pltpu.SemaphoreType.DMA((2, BLOCKS)),
        ],
        compiler_params=params("arbitrary", vmem=44),
        cost_estimate=cost(4 * tall * width * units, 0),
        name="feed_back",
    )(*tables, *up, *down, grad, other, slope, other_slope)


def split(values):
    high = values.astype(BF)
    return high, (values - high.astype(F32)).astype(BF)


def token_learner(residual, own, got, bias, cotangent, live, token_grad, map_t, scale, offset):
    rows, width = residual.shape
    count = map_t.shape[0]
    bands = 4
    band = rows // bands

    def kernel(r_ref, own_ref, got_ref, bias_ref, c_ref, live_ref, tg_ref, map_ref, s_ref, o_ref, *outs):
        out_ref, tok_ref, grad_ref, low_ref, gmap_ref, sums_ref, parts, total = outs
        step = pl.program_id(0)

        @pl.when(step == 0)
        def _():
            parts[...] = jnp.zeros_like(parts)
            total[...] = jnp.zeros_like(total)
            sums_ref[...] = jnp.zeros_like(sums_ref)

        values = r_ref[...] + (own_ref[...] + got_ref[...]) + bias_ref[...]
        alive = live_ref[...]
        grads, maps = tg_ref[...], map_ref[...]
        mapped = maps * s_ref[...]
        mean = jnp.mean(values, axis=-1, keepdims=True)
        center = values - mean
        spread = lax.rsqrt(jnp.mean(center * center, axis=-1, keepdims=True) + EPSILON)
        high, low = split(center)
        both = jnp.concatenate([mapped, grads], axis=0)
        both_high, both_low = split(both)
        wide = dot(high, jnp.concatenate([both_high, both_low], axis=0), NT)
        found = wide[:, : 2 * count] + wide[:, 2 * count :] + dot(low, both_high, NT)
        shifted = jnp.sum(maps * o_ref[...], axis=-1).reshape(1, count)
        hat = found[:, :count] * spread
        sigma = jax.nn.sigmoid(hat + shifted)
        weights = sigma * alive
        pull = found[:, count:] + mean * jnp.sum(grads, axis=-1).reshape(1, count)
        logits = pull * alive * sigma * (1.0 - sigma)
        mapped_mean = jnp.mean(mapped, axis=-1).reshape(1, count)
        flat = jnp.sum(logits * mapped_mean, axis=-1, keepdims=True)
        slant = jnp.sum(logits * hat, axis=-1, keepdims=True) * (1.0 / width)
        pair = jnp.concatenate([logits * spread, weights], axis=1)
        pair_high, pair_low = split(pair)
        back = dot(
            jnp.concatenate([pair_high, pair_high, pair_low], axis=1),
            jnp.concatenate([both_high, both_low, both_high], axis=0),
            NN,
        )
        grad = c_ref[...].astype(F32) + back
        grad = grad - (spread * flat) - (spread * spread * slant) * center
        low_grad = grad.astype(BF)
        out_ref[...] = values.astype(BF)
        grad_ref[...] = grad
        low_ref[...] = low_grad
        tall = dot(jnp.concatenate([pair_high, pair_low], axis=1), high, TN)
        parts[...] += tall[: 2 * count] + tall[2 * count :] + dot(pair_high, low, TN)
        side = jnp.concatenate([logits, weights * mean], axis=1)
        total[...] += jnp.sum(side, axis=0, keepdims=True)
        sums_ref[2:3, :] += jnp.sum(low_grad.astype(F32), axis=0, keepdims=True)

        @pl.when(step == bands - 1)
        def _():
            ends = total[...].reshape(2 * count, 1)
            tok_ref[...] = parts[count:, :] + ends[count:]
            hats = parts[:count, :]
            gmap_ref[...] = hats * s_ref[...] + ends[:count] * o_ref[...]
            sums_ref[0:1, :] = jnp.sum(hats * maps, axis=0, keepdims=True)
            sums_ref[1:2, :] = jnp.sum(ends[:count] * maps, axis=0, keepdims=True)

    banded = pl.BlockSpec((band, width), lambda i: (i, 0))
    fixed = lambda n: pl.BlockSpec((n, width), lambda i: (0, 0))
    return launch(
        kernel,
        grid=(bands,),
        in_specs=[banded] * 3 + [fixed(1), banded, pl.BlockSpec((band, 1), lambda i: (i, 0))]
        + [fixed(count), fixed(count), fixed(1), fixed(1)],
        out_specs=[banded, fixed(count), banded, banded, fixed(count), fixed(3)],
        out_shape=[
            shape((rows, width), BF),
            shape((count, width), F32),
            shape((rows, width), F32),
            shape((rows, width), BF),
            shape((count, width), F32),
            shape((3, width), F32),
        ],
        scratch_shapes=[pltpu.VMEM((2 * count, width), F32), pltpu.VMEM((1, 2 * count), F32)],
        compiler_params=params("arbitrary", vmem=44),
        cost_estimate=cost(10 * 10**9, 14 * rows * width),
        name="token_learner",
    )(residual, own, got, bias, cotangent, live, token_grad, map_t, scale, offset)


def second_norm_back(own, got, residual, grad_block, gain):
    rows, width = residual.shape
    bands = 4

    def kernel(a_ref, b_ref, r_ref, gb_ref, g_ref, res_ref, low_ref, sums_ref):
        grad = a_ref[...] + b_ref[...]
        normed, spread = normalize(r_ref[...])
        result = gb_ref[...] + norm_back(grad * g_ref[...], normed, spread)
        low = result.astype(BF)
        res_ref[...] = result
        low_ref[...] = low
        sums = jnp.concatenate(
            [
                jnp.sum(grad * normed, axis=0, keepdims=True),
                jnp.sum(grad, axis=0, keepdims=True),
                jnp.sum(low.astype(F32), axis=0, keepdims=True),
            ],
            axis=0,
        )

        @pl.when(pl.program_id(0) == 0)
        def _():
            sums_ref[...] = sums

        @pl.when(pl.program_id(0) > 0)
        def _():
            sums_ref[...] += sums

    banded = pl.BlockSpec((rows // bands, width), lambda i: (i, 0))
    fixed = lambda n: pl.BlockSpec((n, width), lambda i: (0, 0))
    return launch(
        kernel,
        grid=(bands,),
        in_specs=[banded] * 4 + [fixed(1)],
        out_specs=[banded, banded, fixed(3)],
        out_shape=[shape((rows, width), F32), shape((rows, width), BF), shape((3, width), F32)],
        compiler_params=params("arbitrary", vmem=44),
        cost_estimate=cost(0, 0),
        name="second_norm_back",
    )(own, got, residual, grad_block, gain)


def project_back(table, pieces, grad_qkv, other_qkv):
    parts, rows, width = grad_qkv.shape
    tall, full = 2 * rows, 2 * width

    def kernel(table_ref, *rest):
        gathered, rest = rest[: len(pieces)], rest[len(pieces) :]
        g_ref, o_ref, own_ref, other_ref, held, sems = rest
        step = pl.program_id(0)

        @pl.when(step == 0)
        def _():
            wait(start_rows(table_ref, gathered, pl.ds(0, parts * width), held, sems))

        weight = held[:, pl.ds(pl.multiple_of(step * width, width), width)]
        product = dot(g_ref[...], weight, NT)
        product_other = dot(o_ref[...], weight, NT)

        @pl.when(step == 0)
        def _():
            own_ref[...] = product
            other_ref[...] = product_other

        @pl.when(step > 0)
        def _():
            own_ref[...] += product
            other_ref[...] += product_other

    return launch(
        kernel,
        grid=(parts,),
        in_specs=[TABLE]
        + [HBM] * len(pieces)
        + [pl.BlockSpec((None, rows, width), lambda j: (j, 0, 0))] * 2,
        out_specs=[pl.BlockSpec((rows, full), lambda j: (0, 0))] * 2,
        out_shape=[shape((rows, full), F32)] * 2,
        scratch_shapes=[
            pltpu.VMEM((full, parts * width), BF),
            pltpu.SemaphoreType.DMA((BLOCKS,)),
        ],
        compiler_params=params("arbitrary", vmem=44),
        cost_estimate=cost(6 * tall * width * full, 0),
        name="project_back",
    )(table, *pieces, grad_qkv, other_qkv)


def first_norm_back(own, got, patches, stats, gain, grad_residual):
    rows, width = patches.shape
    bands = 4

    def kernel(a_ref, b_ref, x_ref, st_ref, gain_ref, res_ref, out_ref, sums_ref):
        grad = a_ref[...] + b_ref[...]
        spread = st_ref[:, 1:2]
        normed = (x_ref[...].astype(F32) - st_ref[:, 0:1]) * spread
        result = res_ref[...] + norm_back(grad * gain_ref[...], normed, spread)
        out_ref[...] = result.astype(BF)
        sums = jnp.concatenate(
            [
                jnp.sum(grad * normed, axis=0, keepdims=True),
                jnp.sum(grad, axis=0, keepdims=True),
            ],
            axis=0,
        )

        @pl.when(pl.program_id(0) == 0)
        def _():
            sums_ref[...] = sums

        @pl.when(pl.program_id(0) > 0)
        def _():
            sums_ref[...] += sums

    banded = lambda n: pl.BlockSpec((rows // bands, n), lambda i: (i, 0))
    fixed = lambda n: pl.BlockSpec((n, width), lambda i: (0, 0))
    return launch(
        kernel,
        grid=(bands,),
        in_specs=[banded(width)] * 3 + [banded(2), fixed(1), banded(width)],
        out_specs=[banded(width), fixed(2)],
        out_shape=[shape((rows, width), BF), shape((2, width), F32)],
        compiler_params=params("arbitrary", vmem=44),
        cost_estimate=cost(0, 0),
        name="first_norm_back",
    )(own, got, patches, stats, gain, grad_residual)


def start_blocks(table_ref, lefts, held, sems, only=(1, 0)):
    count = sems.shape[1]
    step, wide = held.shape[0] // count, held.shape[1] // len(lefts)
    low, high = [], []
    for block in (b for b in range(count) if 2 * b // count in only):
        at = pl.multiple_of(table_ref[block] * step, step)
        for i, left in enumerate(lefts):
            target = held.at[pl.ds(block * step, step), pl.ds(i * wide, wide)]
            copy = pltpu.make_async_copy(left.at[pl.ds(at, step)], target, sems.at[i, block])
            (low if block < count // 2 else high).append(copy)
    for i in only:
        for copy in (low, high)[i]:
            copy.start()
    return low, high


def place_rows(target, sources):
    padded = target.shape[0] // 2
    for i, (ref, first, rows) in enumerate(sources):
        target[i * padded : i * padded + rows, :] = ref[first : first + rows, :]
        target[i * padded + rows : (i + 1) * padded, :] = jnp.zeros(
            (padded - rows, target.shape[1]), target.dtype
        )


def weight_grad(table, turned, rights, part=None, parts=1, tile=512, only=(1, 0)):
    height = turned[0].shape[0]
    deep = sum(left.shape[1] for left in turned)
    blocks, half = table.shape[0], height // 2
    rows = rights[0].shape[-2] * len(rights) // 2

    def kernel(table_ref, *refs):
        lefts, refs = refs[: len(turned)], refs[len(turned) :]
        values, refs = refs[: len(rights)], refs[len(rights) :]
        outs, (held, value, sems) = dict(zip(only, refs)), refs[len(only) :]

        def product(i):
            rows_of = slice(i * half, (i + 1) * half)
            outs[i][...] = dot(held[rows_of, :], value[...], NN).astype(BF)

        @pl.when(pl.program_id(0) == 0)
        def _():
            copies = start_blocks(table_ref, lefts, held, sems, only)
            place_rows(value, spots(values))
            for i in only:
                wait(copies[i])
                product(i)

        @pl.when(pl.program_id(0) > 0)
        def _():
            place_rows(value, spots(values))
            for i in only:
                product(i)

    def spots(values):
        if len(rights) == 1:
            return [(values[0], 0, rows), (values[0], rows, rows)]
        return [(ref, 0, rows) for ref in values]

    each = rights[0].shape[-1] // tile
    tall = rights[0].shape[-2]
    if part is None:
        spec = pl.BlockSpec((tall, tile), lambda n: (0, n))
    else:
        spec = pl.BlockSpec((None, tall, tile), lambda n: (part + n // each, 0, n % each))
    cols = parts * rights[0].shape[-1]
    return launch(
        kernel,
        grid=(cols // tile,),
        in_specs=[TABLE] + [HBM] * len(turned) + [spec] * len(rights),
        out_specs=[pl.BlockSpec((half, tile), lambda n: (0, n))] * len(only),
        out_shape=[shape((half, cols), BF)] * len(only),
        scratch_shapes=[
            pltpu.VMEM((height, deep), BF),
            pltpu.VMEM((deep, tile), BF),
            pltpu.SemaphoreType.DMA((len(turned), blocks)),
        ],
        compiler_params=params("arbitrary", vmem=44),
        cost_estimate=cost(2 * deep * height * cols, 0),
        name="weight_grad",
    )(table, *turned, *rights)


def value_and_out_grad(tables, turned, grad_qkv, mixed_turned, grad_attn):
    height, deep = turned.shape
    width = mixed_turned.shape[0]
    half, rows = height // 2, grad_attn[0].shape[0]
    step = height // BLOCKS

    def kernel(t32, t16, left, mixed, va, vb, a_ref, b_ref, *rest):
        low_ref, high_ref, held, held_mixed, value, both, sems, mixed_sems = rest
        low, high = start_blocks(t32, [left], held, sems)
        more = start_blocks(t16, [mixed], held_mixed, mixed_sems)
        place_rows(value, [(va, 0, rows), (vb, 0, rows)])
        place_rows(both, [(a_ref, 0, rows), (b_ref, 0, rows)])
        wait(high)
        high_ref[:, :width] = dot(held[half:, :], value[...], NN).astype(BF)
        wait(low)
        low_ref[:, :width] = dot(held[:half, :], value[...], NN).astype(BF)
        wait(more[0] + more[1])
        for part in range(2):
            cut = slice(part * width, (part + 1) * width)
            product = dot(held_mixed[...], both[:, cut], NN).astype(BF)
            for slot in range(BLOCKS // 2):
                ref = low_ref if slot < BLOCKS // 4 else high_ref
                at = (slot % (BLOCKS // 4) * 2 + part) * step
                ref[at : at + step, width:] = product[slot * step : (slot + 1) * step]

    whole = lambda m, n: pl.BlockSpec((m, n), lambda i: (0, 0))
    return launch(
        kernel,
        grid=(1,),
        in_specs=[TABLE, TABLE, HBM, HBM]
        + [pl.BlockSpec((None, rows, width), lambda i: (2, 0, 0))] * 2
        + [whole(rows, 2 * width)] * 2,
        out_specs=[whole(half, 2 * width)] * 2,
        out_shape=[shape((half, 2 * width), BF)] * 2,
        scratch_shapes=[
            pltpu.VMEM((height, deep), BF),
            pltpu.VMEM((width, deep), BF),
            pltpu.VMEM((deep, width), BF),
            pltpu.VMEM((deep, 2 * width), BF),
            pltpu.SemaphoreType.DMA((1, BLOCKS)),
            pltpu.SemaphoreType.DMA((1, BLOCKS // 2)),
        ],
        compiler_params=params("arbitrary", vmem=44),
        cost_estimate=cost(4 * deep * height * width, 0),
        name="value_and_out_grad",
    )(*tables, turned, mixed_turned, *grad_qkv, *grad_attn)


def halves(values, core, groups, unit):
    rows = values.shape[0]
    runs = values.reshape(rows, groups, 2, unit)
    even, odd = runs[:, :, 0].reshape(rows, -1), runs[:, :, 1].reshape(rows, -1)
    return jnp.where(core == 0, even, odd), jnp.where(core == 0, odd, even)


def joined(own, other, core, groups, unit):
    rows = own.shape[0]
    even, odd = jnp.where(core == 0, own, other), jnp.where(core == 0, other, own)
    runs = jnp.stack([even.reshape(rows, groups, unit), odd.reshape(rows, groups, unit)], axis=2)
    return runs.reshape(rows, -1)


def per_device(
    patches,
    keep_mask,
    block_cotangent,
    token_cotangent,
    first_gain,
    first_shift,
    qkv_weight,
    query_bias,
    value_bias,
    out_weight,
    out_bias,
    second_gain,
    second_shift,
    up_weight,
    up_bias,
    down_weight,
    down_bias,
    learn_gain,
    learn_shift,
    map_weight,
):
    devices = lax.axis_size("dp") * lax.axis_size("map")
    layered = devices == BLOCKS and lax.axis_size("map") == 2
    core = lax.axis_index("dp") & 1
    images, patch_count, width = patches.shape
    rows = images * patch_count
    own = first_gain.shape[0]
    scaling = HD ** (-0.5)
    table, own_table = slot_tables(layered)
    CHAIN.clear()
    heads = width // HD
    unit = up_weight.shape[1] // (BLOCKS // 2)
    side = width // 2

    vectors = (
        first_gain,
        first_shift,
        query_bias,
        value_bias,
        out_bias,
        second_gain,
        second_shift,
        down_bias,
        learn_gain,
        learn_shift,
    )
    fan = up_bias.shape[0] // own
    count = map_weight.shape[1]
    small = pack_small(vectors, up_bias, map_weight)
    inputs = patches.reshape(rows, width)
    live = keep_mask.reshape(1, rows).astype(F32)
    other_live = to_sibling(live)
    lives = jnp.concatenate([live, other_live], axis=1).reshape(2 * rows, 1)
    live = lives[:rows]

    qkv_own, qkv_other = halves(qkv_weight.astype(BF), core, 3 * heads // 2, HD)
    up_own, up_other = halves(up_weight.astype(BF), core, BLOCKS // 4, 2 * unit // 2)
    out_low, down_low = out_weight.astype(BF), down_weight.astype(BF)
    if layered:
        near_wire = jnp.concatenate([qkv_own, small], axis=1)
        near_got = to_sibling(jnp.concatenate([qkv_other, small], axis=1))
        out_wire = jnp.concatenate([out_low[:, :side], out_low[:, side:]], axis=0)
        near_wire = jnp.concatenate(
            [jnp.concatenate([near_wire, near_got], axis=0), out_wire], axis=1
        )
        near = Doubling(near_wire)
        near.advance()
        near.advance()
        near.last_of_held()
        up = Doubling(stack(up_own, to_sibling(up_other))[0])
        other_inputs = to_sibling(tie(inputs, up.held))
        near.last(near.flying[1])
        up.advance(near.flying)
        near_full = near.pieces
        up.advance((near_full[3],))
        up.last_of_held()
        down = Doubling(stack(down_low[: 2 * own], down_low[2 * own :], axis=1)[0])
        first, second = token_cotangent[0:1], token_cotangent[1:2]
        place = lax.axis_index("map")
        token_mine = jnp.where(place == 0, first, second)
        token_got = permute(jnp.where(place == 0, second, first), BOTH(MAP))
        where = place.reshape(1).astype(jnp.int32)
    else:
        whole = lambda wire: lax.all_gather(wire, AXES, axis=0, tiled=True)
        pick = lambda values: halves(values, core, 1, values.shape[1] // 2)[0]
        qkv_full = halves(whole(qkv_weight.astype(BF)), core, 3 * heads // 2, HD)[0]
        out_full = halves(whole(out_low).reshape(1, -1), core, heads // 2, HD * width)[0]
        out_full = out_full.reshape(BLOCKS // 2, 32, 2, side).transpose(0, 2, 1, 3)
        near_full = jnp.concatenate(
            [qkv_full, whole(small), out_full.reshape(width, side)], axis=1
        )
        up_full = halves(whole(up_weight.astype(BF)), core, BLOCKS // 4, unit)[0]
        down_full = whole(down_low).reshape(1, -1)
        down_full = halves(down_full, core, BLOCKS // 4, unit * width)[0]
        down_full = down_full.reshape(BLOCKS // 2, 2, 64, width).transpose(0, 2, 1, 3)
        down_full = down_full.reshape(width, 2 * width)
        cut = lambda values: (values[: width // 2], values[width // 2 :])
        near_full, up_full, down_full = cut(near_full), cut(up_full), cut(down_full)
        other_inputs = to_sibling(inputs)
        token_grad = lax.all_to_all(
            token_cotangent, "map", split_axis=0, concat_axis=1, tiled=True
        )
        token_grad = token_grad.reshape(count, width).astype(F32)

    small_t = small_rows(table, near_full, 3 * side)
    (
        gain_one,
        shift_one,
        query_shift,
        value_shift,
        out_shift,
        gain_two,
        shift_two,
        down_shift,
        learn_scale,
        learn_offset,
    ) = (small_t[count + i : count + i + 1] for i in range(len(vectors)))
    at = count + len(vectors)
    up_shift = small_t[at : at + fan].reshape(fan, devices, own).transpose(1, 0, 2).reshape(1, -1)
    up_shift = halves(up_shift, core, BLOCKS // 4, unit)[0]
    map_t = small_t[:count]
    mine = lambda row: halves(row, core, heads // 2, HD)[0]

    added = jnp.concatenate(
        [mine(query_shift), jnp.zeros((1, side), F32), mine(value_shift)], axis=1
    )
    factor = jnp.concatenate([jnp.full((1, side), scaling, F32), jnp.ones((1, width), F32)], 1)
    qkv, hidden_one_t, stats = project(
        table, near_full, inputs, other_inputs, gain_one, shift_one, added, factor
    )
    if layered:
        token_grad = join_tokens(where, token_mine, token_got).reshape(count, width)
        up.flying[0] = down.advance(up.flying[1:], up.flying[:1])[0]
        up.last()
        up_full = up.pieces
    mixed, mixed_t, totals = attend(qkv, lives)
    if layered:
        down.advance((up_full[3],))
        down.last_of_held()
    mixed_other = mix_out(own_table, near_full, mixed, 1)
    mixed_got = to_sibling(mixed_other)
    mixed_own = mix_out(own_table, near_full, mixed, 0)
    residual_one, hidden_two = second_norm(
        mixed_own, mixed_got, inputs, out_shift, gain_two, shift_two
    )
    other_two = to_sibling(hidden_two)
    act, act_t, slope, turned_two = feed_up(table, up_full, hidden_two, up_shift)
    if layered:
        down.last(act, down.flying[1])
        down_full = down.pieces
    act_b, act_t_b, slope_b, turned_two_b = feed_up(table, up_full, other_two, up_shift)
    block_got = to_sibling(feed_down(own_table, down_full, act_b, width))
    block_own = feed_down(own_table, down_full, act, width)
    block_out, token_local, grad_block, grad_down_low, grad_map, sums = token_learner(
        residual_one,
        block_own,
        block_got,
        down_shift,
        block_cotangent.reshape(rows, width),
        live * KEEP ** (-0.5),
        token_grad,
        map_t,
        learn_scale,
        learn_offset,
    )
    other_down = to_sibling(grad_down_low)
    token_local = token_local.reshape(images, count, width).astype(BF)
    if layered:
        cut = token_local.astype(F32)
        low, high = cut[:, : count // 2], cut[:, count // 2 :]
        token_mine, token_send = jnp.where(place == 0, low, high), jnp.where(place == 0, high, low)
        token_got = permute(token_send, BOTH(MAP))
    else:
        tokens_out = lax.all_to_all(token_local, "map", split_axis=1, concat_axis=0, tiled=True)
    down_half = lambda i: weight_grad(
        own_table, [act_t, act_t_b], [grad_down_low, other_down], only=(i,)
    )[0]
    down_high = down_half(1)
    down_parts = [down_half(0), down_high]
    if layered:
        down_sum = Halving(down_parts)
        tokens_out = join_tokens(where, token_mine, token_got).astype(BF)
    grad_pre, up_sums, hidden_own, hidden_other = feed_back(
        (table, own_table), up_full, down_full, grad_down_low, other_down, slope, slope_b
    )
    held = ()
    if layered:
        down_sum.advance()
        held = (down_sum.low,)
    hidden_got = to_sibling(tie(hidden_other, *held))
    up_parts = weight_grad(table, [turned_two, turned_two_b], [grad_pre])[::-1]
    grad_residual, grad_attn, two_sums = second_norm_back(
        hidden_own, hidden_got, residual_one, grad_block, gain_two
    )
    held = ()
    if layered:
        down_sum.advance()
        up_sum = Halving([up_parts[0], tie(up_parts[1], down_sum.low)])
        held = (down_sum.low,)
    other_attn = to_sibling(tie(grad_attn, *held))
    back = lambda grad, image: attend_back(own_table, near_full, qkv, lives, totals, grad, image)
    qkv_a, sums_a = back(grad_attn, 0)
    qkv_b, sums_b = back(other_attn, 1)
    grad_qkv = [qkv_a, qkv_b]
    if layered:
        down_sum.advance()
        up_sum.advance()
    near_parts = weight_grad(table, [hidden_one_t], grad_qkv, 0, 2)[::-1]
    if layered:
        up_sum.advance()
        grad_down = down_sum.finish()
        near_sum = Halving([near_parts[0], tie(near_parts[1], up_sum.low)], direct=True)
    far_parts = value_and_out_grad(
        (table, own_table), hidden_one_t, grad_qkv, mixed_t, [grad_attn, other_attn]
    )
    held = ()
    if layered:
        up_sum.advance()
        near_sum.advance()
        held = (near_sum.low,)
        far_sum = Halving([far_parts[0], tie(far_parts[1], *held)], direct=True)
    one_own, one_other = project_back(table, near_full, qkv_a, qkv_b)
    held = ()
    if layered:
        near_sum.advance()
        grad_up = up_sum.finish()
        far_sum.advance()
        held = (far_sum.low,)
    one_got = to_sibling(tie(one_other, *held))
    grad_patches, one_sums = first_norm_back(
        one_own, one_got, inputs, stats, gain_one, grad_residual
    )
    runs = up_sums.reshape(16, fan, -1).transpose(1, 0, 2).reshape(fan, -1)
    which = core.reshape(1).astype(jnp.int32)
    if layered:
        swap = lambda total: (total[0], to_sibling(total[1]))
        up_pair = swap(grad_up)
    terms = pack_terms(which, one_sums, two_sums, sums, grad_map, sums_a, sums_b, runs)
    terms = lax.all_to_all(terms.reshape(devices, own, 128), AXES, 0, 0, tiled=True)
    if layered:
        far_sum.advance()
        qk_pair = swap(near_sum.finish())
        grad_down = jnp.concatenate(grad_down, axis=0)
        grad_up = join_runs(which, [up_pair], unit)
        map_piece, pieces, up_piece = sum_terms(terms, count, fan)
        grad_far = far_sum.finish()
        v_pair = swap([part[:, :side] for part in grad_far])
        grad_out = jnp.concatenate([grad_far[0][:, side:], grad_far[1][:, side:]], axis=1)
        grad_qkv_full = join_runs(which, [qk_pair, v_pair], HD)
    else:

        def scatter(parts, groups, unit):
            mine = jnp.concatenate(parts, axis=0)
            return joined(mine, jnp.zeros_like(mine), core, groups, unit)

        def shared(values):
            return lax.psum_scatter(values.astype(F32), AXES, scatter_dimension=0, tiled=True)

        def tall(parts, unit):
            flat = [jnp.concatenate(parts, axis=0).reshape(1, -1)]
            return shared(scatter(flat, BLOCKS // 4, unit * width).reshape(-1, width))

        grad_up = shared(scatter(up_parts, BLOCKS // 4, unit))
        far = jnp.concatenate(far_parts, axis=0)
        out_part = far[:, side:].reshape(BLOCKS // 2, 2, width // BLOCKS, side)
        out_part = out_part.transpose(0, 2, 1, 3).reshape(side, width)
        grad_down, grad_out = tall(down_parts, unit), tall([out_part], HD)
        qkv_parts = [jnp.concatenate([*near_parts], axis=0), far[:, :side]]
        qkv_parts = [jnp.concatenate(qkv_parts, axis=1)]
        grad_qkv_full = shared(scatter(qkv_parts, 3 * heads // 2, HD))
        map_piece, pieces, up_piece = sum_terms(terms, count, fan)

    up_piece = up_piece.reshape(-1)
    return (
        block_out.reshape(images, patch_count, width),
        tokens_out,
        grad_patches.reshape(images, patch_count, width),
        pieces[0],
        pieces[1],
        grad_qkv_full,
        pieces[2],
        pieces[3],
        grad_out,
        pieces[4],
        pieces[5],
        pieces[6],
        grad_up,
        up_piece,
        grad_down,
        pieces[7],
        pieces[8],
        pieces[9],
        map_piece,
    )


def solution(mesh):
    rows = P(("dp", "map"))
    wide = P(("dp", "map"), None)
    images = P(("dp", "map"), None, None)
    tokens = P("dp", "map", None)
    weights = (
        rows, rows, wide, rows, rows, wide, rows, rows,
        rows, wide, rows, wide, rows, rows, rows, wide,
    )
    return jax.shard_map(
        per_device,
        mesh=mesh,
        in_specs=(images, wide, images, tokens) + weights,
        out_specs=(images, tokens, images) + weights,
        check_vma=False,
    )
```
